32 devices in a mesh: dp: 16 (over z, y, x), mp: 2 (over core).
Axes of the slice: x: 2, y: 2, z: 4, core: 2. Of those that a mesh axis runs over, the one named last changes fastest.
Arguments:
- tokens: bfloat16 [2048, 32, 768], P('dp'), may hold values from -6 to 6
- lengths: int32 [2048], P('dp'), may hold values from 1 to 32, as said below
- send_order: int32 [2048], P('dp'), may hold values from 0 to 127, as said below
- pooled_grad: float32 [2048, 768], P('dp'), may hold values from -6 to 6
- qkv_weight: float32 [3, 768, 768], P(None, 'dp', 'mp'), may hold values from -0.21875 to 0.21875
- out_weight: float32 [768, 768], P('mp', 'dp'), may hold values from -0.875 to 0.875
- in_weight: float32 [768, 3072], P('dp', 'mp'), may hold values from -0.21875 to 0.21875
- down_weight: float32 [3072, 768], P('mp', 'dp'), may hold values from -0.109375 to 0.109375
- vectors: float32 [9216], replicated
- qkv_moment: float32 [3, 768, 768], P(None, 'dp', 'mp'), may hold values from -7 to 7
- out_moment: float32 [768, 768], P('mp', 'dp'), may hold values from -7 to 7
- in_moment: float32 [768, 3072], P('dp', 'mp'), may hold values from -7 to 7
- down_moment: float32 [3072, 768], P('mp', 'dp'), may hold values from -7 to 7
- vec_moment: float32 [9216], replicated, may hold values from -7 to 7
- qkv_square: float32 [3, 768, 768], P(None, 'dp', 'mp'), may hold values from 0.1024 to 0.4096
- out_square: float32 [768, 768], P('mp', 'dp'), may hold values from 0.1024 to 0.4096
- in_square: float32 [768, 3072], P('dp', 'mp'), may hold values from 0.1024 to 0.4096
- down_square: float32 [3072, 768], P('mp', 'dp'), may hold values from 0.1024 to 0.4096
- vec_square: float32 [9216], replicated, may hold values from 0.1024 to 0.4096
- qkv_average: float32 [3, 768, 768], P(None, 'dp', 'mp'), may hold values from -0.21875 to 0.21875
- out_average: float32 [768, 768], P('mp', 'dp'), may hold values from -0.875 to 0.875
- in_average: float32 [768, 3072], P('dp', 'mp'), may hold values from -0.21875 to 0.21875
- down_average: float32 [3072, 768], P('mp', 'dp'), may hold values from -0.109375 to 0.109375
- vec_average: float32 [9216], replicated
Outputs:
- pooled: float32 [2048, 768], P('dp')
- tokens_grad: float32 [2048, 32, 768], P('dp', None, 'mp')
- qkv_grad: float32 [3, 768, 768], P(None, 'dp', 'mp')
- out_grad: float32 [768, 768], P('mp', 'dp')
- in_grad: float32 [768, 3072], P('dp', 'mp')
- down_grad: float32 [3072, 768], P('mp', 'dp')
- vec_grad: float32 [9216], replicated
- trust_ratio: float32 [6], replicated
- weight_norm: float32 [6], replicated
- update_norm: float32 [6], replicated
- new_qkv_moment: float32 [3, 768, 768], P(None, 'dp', 'mp')
- new_out_moment: float32 [768, 768], P('mp', 'dp')
- new_in_moment: float32 [768, 3072], P('dp', 'mp')
- new_down_moment: float32 [3072, 768], P('mp', 'dp')
- new_vec_moment: float32 [9216], replicated
- new_qkv_square: float32 [3, 768, 768], P(None, 'dp', 'mp')
- new_out_square: float32 [768, 768], P('mp', 'dp')
- new_in_square: float32 [768, 3072], P('dp', 'mp')
- new_down_square: float32 [3072, 768], P('mp', 'dp')
- new_vec_square: float32 [9216], replicated
- new_qkv_weight: float32 [3, 768, 768], P(None, 'dp', 'mp')
- new_out_weight: float32 [768, 768], P('mp', 'dp')
- new_in_weight: float32 [768, 3072], P('dp', 'mp')
- new_down_weight: float32 [3072, 768], P('mp', 'dp')
- new_vectors: float32 [9216], replicated
- new_qkv_average: float32 [3, 768, 768], P(None, 'dp', 'mp')
- new_out_average: float32 [768, 768], P('mp', 'dp')
- new_in_average: float32 [768, 3072], P('dp', 'mp')
- new_down_average: float32 [3072, 768], P('mp', 'dp')
- new_vec_average: float32 [9216], replicated
The draws below stay inside these ranges and needn't reach their ends.
Inputs may be any that keep to these rules, and one draw needn't show every extreme that they name: `lengths`: every device's 128 sentences include one of length 32. `send_order`: each device's block of 128 entries is a permutation of 0 to 127 listing that device's sentences by non-falling length; send slot q goes to bucket q // 8.
All inputs are finite; a program needn't handle non-finite values.
Results may differ from the reference program's by a relative error of at most 0.0079.
Values may be sent and summed in bfloat16 or wider, within the bound.
No kernel may reach another device: no remote copies, remote signals or barrier semaphores. Data moves between devices by JAX's collectives and lax.ppermute only.
A program may use at most 320 MiB of HBM per device.

```python
import math
import jax
import jax.numpy as jnp
from jax import lax

D = 768
HEADS = 12
HEAD = 64
FF = 3072
LEN = 32
SENT_DEV = 128
STEP = 10
SENTS = 2048
SHARE = 8
VEC = 9216
N_DP = 16


def length_table(key):
    base = jax.random.fold_in(key, 11)
    first_key, second_key, third_key = jax.random.split(base, 3)
    drawn = jax.random.randint(first_key, (N_DP, SENT_DEV), 1, LEN + 1)
    longest = jax.random.randint(second_key, (N_DP,), 0, SENT_DEV)
    drawn = jnp.where(jnp.arange(SENT_DEV)[None, :] == longest[:, None], LEN, drawn)
    tiebreak = jax.vmap(lambda sub_key: jax.random.permutation(sub_key, SENT_DEV))(jax.random.split(third_key, N_DP))
    ordering = jnp.argsort(drawn * SENT_DEV + tiebreak.astype(jnp.int32), axis=1, stable=True)
    return (drawn.astype(jnp.int32), ordering.astype(jnp.int32))


def draw_lengths(key, part):
    return length_table(key)[0].reshape(-1)


def draw_send_order(key, part):
    return length_table(key)[1].reshape(-1)


def vector_values(key):
    first_key, second_key = jax.random.split(key)
    shifts = 0.3 * jax.random.normal(first_key, (8 * D + FF,), jnp.float32)
    gains = jax.random.uniform(second_key, (8 * D + FF,), jnp.float32, 0.7, 1.3)
    index = jnp.arange(8 * D + FF)
    is_gain = (index >= 4 * D) & (index < 5 * D) | (index >= 6 * D) & (index < 7 * D)
    return jnp.where(is_gain, gains, shifts)


def draw_vectors(key, part):
    return vector_values(jax.random.fold_in(key, 3))


def draw_vec_average(key, part):
    return vector_values(jax.random.fold_in(key, 5))


def block_scale(stream_key, dims, cuts, smallest, largest):
    def one(dim, parts):
        heights = jax.random.uniform(jax.random.fold_in(jax.random.fold_in(stream_key, 6), dim), (parts,), jnp.float32, smallest / len(cuts), largest / len(cuts))
        return jnp.repeat(jnp.exp(heights), dims[dim] // parts).reshape((-1,) + (1,) * (len(dims) - dim - 1))

    level = one(*cuts[0])
    for cut in cuts[1:]:
        level = level * one(*cut)
    return level


def scatter_about(own_key, dims, deviation, limit, shards=(), held_as=jnp.bfloat16):
    array = jax.random.normal(own_key, dims, jnp.float32) * deviation
    if len(shards) > 0:
        array = block_scale(own_key, dims, shards, -0.22, 0.18) * array
    return jnp.clip(array, min=-limit, max=limit).astype(held_as)


def setup_inputs(seed: int = 0) -> dict:
    seeds = jax.random.split(jax.random.key(seed), 25)
    tokens = scatter_about(seeds[0], (SENTS, LEN, D), 1.0, 6.0, ((0, 16),))
    lengths = draw_lengths(jax.random.fold_in(seeds[24], 71), 0)
    send_order = draw_send_order(jax.random.fold_in(seeds[24], 71), 0)
    pooled_grad = scatter_about(seeds[3], (SENTS, D), 1.0, 6.0, ((0, 16),), jnp.float32)
    qkv_weight = scatter_about(seeds[4], (3, D, D), D ** -0.5, 0.21875, ((1, 16), (2, 2)), jnp.float32)
    out_weight = scatter_about(seeds[5], (D, D), (D // 16) ** -0.5, 0.875, ((0, 2), (1, 16)), jnp.float32)
    in_weight = scatter_about(seeds[6], (D, FF), D ** -0.5, 0.21875, ((0, 16), (1, 2)), jnp.float32)
    down_weight = scatter_about(seeds[7], (FF, D), FF ** -0.5, 0.109375, ((0, 2), (1, 16)), jnp.float32)
    vectors = draw_vectors(jax.random.fold_in(seeds[24], 71), 0)
    qkv_moment = scatter_about(seeds[9], (3, D, D), (0.11 * (SENTS * 0.05) ** 0.5), 7.0, ((1, 16), (2, 2)), jnp.float32)
    out_moment = scatter_about(seeds[10], (D, D), (0.11 * (SENTS * 0.05) ** 0.5), 7.0, ((0, 2), (1, 16)), jnp.float32)
    in_moment = scatter_about(seeds[11], (D, FF), (0.11 * (SENTS * 0.05) ** 0.5), 7.0, ((0, 16), (1, 2)), jnp.float32)
    down_moment = scatter_about(seeds[12], (FF, D), (0.11 * (SENTS * 0.05) ** 0.5), 7.0, ((0, 2), (1, 16)), jnp.float32)
    vec_moment = scatter_about(seeds[13], (VEC,), (0.11 * (SENTS * 0.05) ** 0.5), 7.0, (), jnp.float32)
    qkv_square = jnp.clip(jnp.exp(math.log(0.4096) - 1.3862944 * jax.random.uniform(seeds[14], (3, D, D), jnp.float32) ** block_scale(seeds[14], (3, D, D), ((1, 16), (2, 2)), -0.2, 0.2)), 0.1024, 0.4096)
    out_square = jnp.clip(jnp.exp(math.log(0.4096) - 1.3862944 * jax.random.uniform(seeds[15], (D, D), jnp.float32) ** block_scale(seeds[15], (D, D), ((0, 2), (1, 16)), -0.2, 0.2)), 0.1024, 0.4096)
    in_square = jnp.clip(jnp.exp(math.log(0.4096) - 1.3862944 * jax.random.uniform(seeds[16], (D, FF), jnp.float32) ** block_scale(seeds[16], (D, FF), ((0, 16), (1, 2)), -0.2, 0.2)), 0.1024, 0.4096)
    down_square = jnp.clip(jnp.exp(math.log(0.4096) - 1.3862944 * jax.random.uniform(seeds[17], (FF, D), jnp.float32) ** block_scale(seeds[17], (FF, D), ((0, 2), (1, 16)), -0.2, 0.2)), 0.1024, 0.4096)
    vec_square = jnp.clip(jnp.exp(jax.random.uniform(seeds[18], (VEC,), jnp.float32, math.log(0.1024), math.log(0.4096))), 0.1024, 0.4096)
    qkv_average = scatter_about(seeds[19], (3, D, D), D ** -0.5, 0.21875, ((1, 16), (2, 2)), jnp.float32)
    out_average = scatter_about(seeds[20], (D, D), (D // 16) ** -0.5, 0.875, ((0, 2), (1, 16)), jnp.float32)
    in_average = scatter_about(seeds[21], (D, FF), D ** -0.5, 0.21875, ((0, 16), (1, 2)), jnp.float32)
    down_average = scatter_about(seeds[22], (FF, D), FF ** -0.5, 0.109375, ((0, 2), (1, 16)), jnp.float32)
    vec_average = draw_vec_average(jax.random.fold_in(seeds[24], 71), 0)
    return {"tokens": tokens, "lengths": lengths, "send_order": send_order, "pooled_grad": pooled_grad, "qkv_weight": qkv_weight, "out_weight": out_weight, "in_weight": in_weight, "down_weight": down_weight, "vectors": vectors, "qkv_moment": qkv_moment, "out_moment": out_moment, "in_moment": in_moment, "down_moment": down_moment, "vec_moment": vec_moment, "qkv_square": qkv_square, "out_square": out_square, "in_square": in_square, "down_square": down_square, "vec_square": vec_square, "qkv_average": qkv_average, "out_average": out_average, "in_average": in_average, "down_average": down_average, "vec_average": vec_average}


@jax.custom_vjp
def low(v):
    return lax.optimization_barrier(v.astype(jnp.bfloat16)).astype(jnp.float32)

@jax.custom_vjp
def low_back(v):
    return v

def low_keep(v):
    return (low(v), None)

def low_pass(kept, grad):
    return (grad,)

def back_keep(v):
    return (v, None)

def back_low(kept, grad):
    return (low(grad),)
low.defvjp(low_keep, low_pass)
low_back.defvjp(back_keep, back_low)
highest = lax.Precision.HIGHEST
beta_one = 0.9
beta_two = 0.999
adam_eps = 1e-06
weight_decay = 0.01
learn_rate = 0.3
vector_rate = 0.05
ema_keep = 0.9
norm_eps = 1e-12
masked_score = -1000000000.0

def layer_norm(values, norm_gain, norm_shift):
    centre = values - lax.optimization_barrier(jnp.mean(values, axis=-1, keepdims=True))
    spread = lax.optimization_barrier(jnp.mean(centre * centre, axis=-1, keepdims=True))
    return centre * lax.rsqrt(spread + norm_eps) * norm_gain + norm_shift

def gelu_tanh(values):
    return 0.5 * values * (1.0 + jnp.tanh(0.7978845608028654 * (values + 0.044715 * values * values * values)))

def adam_moments(grad_value, moment, square):
    moment_new = beta_one * moment + (1.0 - beta_one) * grad_value
    square_new = beta_two * square + (1.0 - beta_two) * grad_value * grad_value
    scaled = moment_new / (1.0 - beta_one ** STEP) / (jnp.sqrt(square_new / (1.0 - beta_two ** STEP)) + adam_eps)
    return (moment_new, square_new, scaled)

def encode(params, sent_rows, sent_lengths):
    qkv_weight, out_weight, in_weight, down_weight, vectors = params
    qkv_weight = low(qkv_weight)
    out_weight = low(out_weight)
    in_weight = low(in_weight)
    down_weight = low(down_weight)
    sent_count = sent_rows.shape[0]
    flat_rows = sent_rows.reshape(sent_count * LEN, D)
    pieces = [vectors[index * D:(index + 1) * D] for index in range(8)]
    bias_qkv = jnp.stack([pieces[0], jnp.zeros((D,), jnp.float32), pieces[1]])
    qkv_value = jnp.einsum('rd,cde->cre', flat_rows, qkv_weight, precision=highest) + bias_qkv[:, None, :]
    qkv_value = low(low_back(qkv_value))
    qkv_parts = qkv_value.reshape(3, sent_count, LEN, HEADS, HEAD)
    scores = jnp.einsum('gqhe,gkhe->ghqk', qkv_parts[0], qkv_parts[1], precision=highest) * HEAD ** (-0.5)
    scores = low_back(scores)
    key_valid = jnp.arange(LEN)[None, :] < sent_lengths[:, None]
    scores = jnp.where(key_valid[:, None, None, :], scores, masked_score)
    row_top = lax.optimization_barrier(jnp.max(scores, axis=-1, keepdims=True))
    expon = jnp.exp(scores - row_top)
    attn_probs = low(expon / lax.optimization_barrier(jnp.sum(expon, axis=-1, keepdims=True)))
    attended = jnp.einsum('ghqk,gkhe->gqhe', attn_probs, qkv_parts[2], precision=highest).reshape(sent_count * LEN, D)
    attended = low(low_back(attended))
    attn_mixed = low_back(jnp.dot(attended, out_weight, precision=highest) + pieces[2])
    hidden = layer_norm(flat_rows + attn_mixed, pieces[4], pieces[5])
    pre_gelu = low_back(jnp.dot(low(hidden), in_weight, precision=highest) + vectors[8 * D:])
    activated = low(gelu_tanh(pre_gelu))
    ffn_value = low_back(jnp.dot(activated, down_weight, precision=highest) + pieces[3])
    normed = layer_norm(hidden + ffn_value, pieces[6], pieces[7]).reshape(sent_count, LEN, D)
    row_weight = key_valid.astype(jnp.float32)
    return lax.optimization_barrier(jnp.sum(normed * row_weight[:, :, None], axis=1)) / sent_lengths[:, None].astype(jnp.float32)

def matrix_squares(qkv_part, out_part, in_part, down_part):
    return jnp.concatenate([lax.optimization_barrier(jnp.sum(qkv_part * qkv_part, axis=(1, 2))), jnp.sum(out_part * out_part)[None], jnp.sum(in_part * in_part)[None], jnp.sum(down_part * down_part)[None]])

def reference(tokens, lengths, send_order, pooled_grad, qkv_weight, out_weight, in_weight, down_weight, vectors, qkv_moment, out_moment, in_moment, down_moment, vec_moment, qkv_square, out_square, in_square, down_square, vec_square, qkv_average, out_average, in_average, down_average, vec_average):
    position = jnp.arange(SENTS, dtype=jnp.int32)
    within = position % SENT_DEV
    source_dev = within // SHARE
    send_slot = position // SENT_DEV * SHARE + position % SHARE
    sentence = (source_dev * SENT_DEV + send_order[source_dev * SENT_DEV + send_slot]).astype(jnp.int32)
    pair_grad = jnp.zeros((SENTS, D), jnp.float32).at[sentence].set(pooled_grad)
    params = (qkv_weight, out_weight, in_weight, down_weight, vectors)
    groups = SENTS // SENT_DEV

    def step_group(totals, group_data):
        sent_rows, sent_lengths, group_back = group_data
        pooled_part, pullback = jax.vjp(lambda weights_in, rows_in: encode(weights_in, rows_in, sent_lengths), params, sent_rows.astype(jnp.float32))
        grad_tree, rows_grad = pullback(group_back)
        return (jax.tree.map(lambda left, right: left + right, totals, grad_tree), (pooled_part, rows_grad))
    zero_tree = jax.tree.map(jnp.zeros_like, params)
    totals, (embedded, tokens_grad) = lax.scan(step_group, zero_tree, (tokens.reshape(groups, SENT_DEV, LEN, D), lengths.reshape(groups, SENT_DEV), pair_grad.reshape(groups, SENT_DEV, D)))
    embedded = embedded.reshape(SENTS, D)
    pooled = embedded[sentence]
    tokens_grad = tokens_grad.reshape(SENTS, LEN, D)
    qkv_grad, out_grad, in_grad, down_grad, vec_grad = totals
    qkv_m, qkv_s, qkv_n = adam_moments(qkv_grad, qkv_moment, qkv_square)
    out_m, out_s, out_n = adam_moments(out_grad, out_moment, out_square)
    in_m, in_s, in_n = adam_moments(in_grad, in_moment, in_square)
    down_m, down_s, down_n = adam_moments(down_grad, down_moment, down_square)
    vec_m, vec_s, vec_n = adam_moments(vec_grad, vec_moment, vec_square)
    qkv_u = qkv_n + weight_decay * qkv_weight
    out_u = out_n + weight_decay * out_weight
    in_u = in_n + weight_decay * in_weight
    down_u = down_n + weight_decay * down_weight
    weight_norm = jnp.sqrt(matrix_squares(qkv_weight, out_weight, in_weight, down_weight))
    update_norm = jnp.sqrt(matrix_squares(qkv_u, out_u, in_u, down_u))
    trust_ratio = weight_norm / update_norm
    new_qkv = qkv_weight - learn_rate * trust_ratio[:3, None, None] * qkv_u
    new_out = out_weight - learn_rate * trust_ratio[3] * out_u
    new_in = in_weight - learn_rate * trust_ratio[4] * in_u
    new_down = down_weight - learn_rate * trust_ratio[5] * down_u
    new_vec = vectors - vector_rate * vec_n
    return (pooled, tokens_grad, qkv_grad, out_grad, in_grad, down_grad, vec_grad, trust_ratio, weight_norm, update_norm, qkv_m, out_m, in_m, down_m, vec_m, qkv_s, out_s, in_s, down_s, vec_s, new_qkv, new_out, new_in, new_down, new_vec, ema_keep * qkv_average + (1.0 - ema_keep) * new_qkv, ema_keep * out_average + (1.0 - ema_keep) * new_out, ema_keep * in_average + (1.0 - ema_keep) * new_in, ema_keep * down_average + (1.0 - ema_keep) * new_down, ema_keep * vec_average + (1.0 - ema_keep) * new_vec)
```

```python
import jax
import jax.numpy as jnp
from jax import lax
from jax.experimental import pallas as pl
from jax.experimental.pallas import tpu as pltpu
from jax.sharding import PartitionSpec as P

HEAD = 64
STEP = 10
TILE = 256
BLOCK = 128

beta_one = 0.9
beta_two = 0.999
adam_eps = 1e-06
weight_decay = 0.01
learn_rate = 0.3
vector_rate = 0.05
ema_keep = 0.9
norm_eps = 1e-12
masked_score = -1000000000.0
gelu_in = 0.7978845608028654
gelu_cube = 0.044715

BF = jnp.bfloat16
F32 = jnp.float32
VMEM_LIMIT = 60 * 1024 * 1024


def dp_dims(count):
    known = {16: ((4, 4), (2, 2), (2, 1)), 128: ((4, 32), (8, 4), (4, 1))}
    return known.get(count, ((count, 1),))


def dp_shift(value, dim, step):
    size, stride = dim
    count = lax.axis_size("dp")
    pairs = []
    for index in range(count):
        place = index // stride % size
        pairs.append((index, index + ((place + step) % size - place) * stride))
    return lax.ppermute(value, "dp", pairs)


def dp_place(dim):
    size, stride = dim
    return lax.rem(lax.div(lax.axis_index("dp"), stride), size)


def swap_core(value):
    return lax.ppermute(value, "mp", [(0, 1), (1, 0)])


def arrange(pieces, dim, axis):
    size, _ = dim
    place = dp_place(dim)
    if size == 2:
        return jnp.where(place == 0, jnp.stack(pieces, axis), jnp.stack(pieces[::-1], axis))
    twice = jnp.stack(pieces + pieces, axis)
    return lax.dynamic_slice_in_dim(twice, size - place, size, axis)


def gather_send(value, dim):
    return [value] + [dp_shift(value, dim, -step) for step in range(1, dim[0])]


def scatter_slabs(value, dim, axis):
    size, _ = dim
    place = dp_place(dim)
    return [
        lax.dynamic_index_in_dim(value, lax.rem(place + step, size), axis, keepdims=False).astype(BF)
        for step in range(1, size)
    ]


def scatter_send(slabs, dim):
    return [dp_shift(slab, dim, step) for step, slab in enumerate(slabs, 1)]


def scatter_sum(value, arrived, dim, axis):
    total = lax.dynamic_index_in_dim(value, dp_place(dim), axis, keepdims=False)
    for slab in arrived:
        total = total + slab.astype(F32)
    return total


def sum_all(value, dims):
    value = value + swap_core(value)
    count = lax.axis_size("dp")
    for size, stride in dims:
        bit = 1
        while bit < size:
            pairs = []
            for index in range(count):
                place = index // stride % size
                pairs.append((index, index + ((place ^ bit) - place) * stride))
            value = value + lax.ppermute(value, "dp", pairs)
            bit *= 2
    return value


def dot_nn(left, right):
    return jnp.dot(left, right, preferred_element_type=F32)


def dot_nt(left, right):
    return lax.dot_general(left, right, (((1,), (1,)), ((), ())), preferred_element_type=F32)


def dot_tn(left, right):
    return lax.dot_general(left, right, (((0,), (0,)), ((), ())), preferred_element_type=F32)


def vec_at(index, width, core=None, part=0, cols=None):
    if core is None:
        return slice(index * width, (index + 1) * width)
    which = core if part == 0 else 1 - core
    return pl.ds(pl.multiple_of(index * width + which * cols, BLOCK), cols)


def column_sums(value):
    rows, cols = value.shape
    return jnp.sum(value.reshape(rows // 8, 8, cols), axis=0)


def pack_kernel(
    core_ref, order_ref, len_ref, tok_ref, rows_ref, seg_ref, off_ref, tiles_ref, *stage
):
    core = core_ref[0]
    half = order_ref.shape[0] // 2
    total = rows_ref.shape[0]

    def clear(step, carry):
        rows = pl.ds(pl.multiple_of(step * BLOCK, BLOCK), BLOCK)
        for column in stage:
            column[rows, :] = jnp.zeros((BLOCK, BLOCK), F32)
        seg_ref[rows, :] = jnp.full((BLOCK, BLOCK), -1.0, F32)
        return carry

    lax.fori_loop(0, total // BLOCK, clear, 0)

    def start_of(cursor, count):
        inside = cursor & (BLOCK - 1)
        return jnp.where(inside + count > BLOCK, cursor - inside + BLOCK, cursor)

    def place(slot, cursor):
        sentence = order_ref[2 * slot + core]
        count = len_ref[sentence]
        start = start_of(cursor, count)
        off_ref[0, slot] = start
        span = tok_ref.shape[1]
        value = tok_ref[sentence].astype(F32)
        for index, column in enumerate(stage):
            column[pl.ds(start, span), :] = value[:, index * BLOCK : (index + 1) * BLOCK]
        row = lax.broadcasted_iota(jnp.int32, (span, BLOCK), 0)
        seg_ref[pl.ds(start, span), :] = jnp.where(row < count, slot.astype(F32), -1.0)
        return start + count

    used = lax.fori_loop(0, half, place, 0)
    tiles_ref[0] = (used + TILE - 1) // TILE

    def partner(slot, cursor):
        count = len_ref[order_ref[2 * slot + 1 - core]]
        start = start_of(cursor, count)
        off_ref[1, slot] = start
        return start + count

    lax.fori_loop(0, half, partner, 0)

    def low(step, carry):
        rows = pl.ds(pl.multiple_of(step * BLOCK, BLOCK), BLOCK)
        for index, column in enumerate(stage):
            rows_ref[rows, index * BLOCK : (index + 1) * BLOCK] = column[rows, :].astype(BF)
        return carry

    lax.fori_loop(0, total // BLOCK, low, 0)


def head_masks():
    lane = lax.broadcasted_iota(jnp.int32, (1, 2 * HEAD), 1)
    first = jnp.where(lane < HEAD, 1.0, 0.0)
    return first.astype(BF), (1.0 - first).astype(BF)


def two_heads(value, masks):
    return jnp.concatenate([value * masks[0], value * masks[1]], axis=0)


def same_sentence(seg):
    across = jnp.transpose(seg)
    return jnp.concatenate([seg, seg], axis=1) == jnp.concatenate([across, across], axis=1)


def attention_probs(query_two, key, mask):
    scores = jnp.where(mask, dot_nt(key, query_two), masked_score)
    expon = jnp.exp(scores - jnp.max(scores, axis=0, keepdims=True))
    return expon * (1.0 / jnp.sum(expon, axis=0, keepdims=True))


def one_above_other(value):
    return jnp.concatenate([value[:, :BLOCK], value[:, BLOCK:]], axis=0)


def attn_forward_kernel(
    last, core_ref, rows_ref, seg_ref, vec_ref, qk0, vo0, qk1, vo1, qkv_ref, att_ref, norm_ref, inv_ref
):
    width = rows_ref.shape[1]
    half = width // 2
    core = core_ref[0]
    rows = rows_ref[...]
    weights = ((qk0, vo0), (qk1, vo1))
    for part, (qk, vo) in enumerate(weights):
        base = part * 3 * half
        value = dot_nn(rows, qk[...])
        query = value[:, :half] + vec_ref[:, vec_at(0, width, core, part, half)]
        qkv_ref[:, base : base + half] = query.astype(BF)
        qkv_ref[:, base + half : base + width] = value[:, half:].astype(BF)
        value = dot_nn(rows, vo[:, :half]) + vec_ref[:, vec_at(1, width, core, part, half)]
        qkv_ref[:, base + width : base + 3 * half] = value.astype(BF)
    masks = head_masks()
    for block in range(TILE // BLOCK):
        span = slice(block * BLOCK, (block + 1) * BLOCK)
        mask = same_sentence(seg_ref[span, :])
        for part in range(2):
            for pair in range(half // (2 * HEAD)):
                at = part * 3 * half + pair * 2 * HEAD
                query = qkv_ref[span, at : at + 2 * HEAD] * BF(HEAD**-0.5)
                key = qkv_ref[span, at + half : at + half + 2 * HEAD]
                value = qkv_ref[span, at + width : at + width + 2 * HEAD]
                probs = attention_probs(two_heads(query, masks), key, mask).astype(BF)
                mixed = dot_tn(one_above_other(probs), two_heads(value, masks))
                to = part * half + pair * 2 * HEAD
                att_ref[span, to : to + 2 * HEAD] = mixed.astype(BF)
    mixed = dot_nt(att_ref[:, :half], vo0[:, half:]) + dot_nt(att_ref[:, half:], vo1[:, half:])
    pre = rows.astype(F32) + (mixed + vec_ref[:, vec_at(2, width)])
    centre = pre - jnp.mean(pre, axis=-1, keepdims=True)
    inverse = lax.rsqrt(jnp.mean(centre * centre, axis=-1, keepdims=True) + norm_eps)
    norm_ref[...] = centre * inverse
    inv_ref[...] = jnp.broadcast_to(inverse, inv_ref.shape)


def norm_back(grad, normed, inverse, gain):
    scaled = grad * gain
    first = jnp.mean(scaled, axis=-1, keepdims=True)
    second = jnp.mean(scaled * normed, axis=-1, keepdims=True)
    return (scaled - first - normed * second) * inverse


def ffn_kernel(
    last, core_ref, norm_ref, inv_ref, seg_ref, vec_ref, high_ref, rest_ref,
    w1_0, w1_1, w1_2, w1_3, w2_0, w2_1, w2_2, w2_3,
    grad_ref, emb_ref, sums_ref, down_own, down_other, in_own, in_other,
    sum1, sum2, act, slope, emb, counts, stage, sems,
):
    step = pl.program_id(0)
    core = core_ref[0]
    width = norm_ref.shape[1]
    w1 = (w1_0, w1_1, w1_2, w1_3)
    w2 = (w2_0, w2_1, w2_2, w2_3)
    hidden_at = [
        pl.ds(
            pl.multiple_of(8 * width + (2 * (core if part < 2 else 1 - core) + part % 2) * width, BLOCK),
            width,
        )
        for part in range(4)
    ]

    @pl.when(step == 0)
    def _():
        emb[...] = jnp.zeros_like(emb)
        counts[...] = jnp.zeros_like(counts)
        sums_ref[...] = jnp.zeros_like(sums_ref)
        sum1[...] = jnp.zeros_like(sum1)
        sum2[...] = jnp.zeros_like(sum2)

    gain_one, shift_one = vec_ref[:, vec_at(4, width)], vec_ref[:, vec_at(5, width)]
    gain_two, shift_two = vec_ref[:, vec_at(6, width)], vec_ref[:, vec_at(7, width)]
    bias_ffn = vec_ref[:, vec_at(3, width)]
    hidden_low = (norm_ref[...] * gain_one + shift_one).astype(BF)
    for part in range(4):
        pre = dot_nn(hidden_low, w1[part][...]) + vec_ref[:, hidden_at[part]]
        square = pre * pre
        tanh = jnp.tanh(pre * (gelu_in + gelu_in * gelu_cube * square))
        gate = 0.5 + 0.5 * tanh
        out = pre * gate
        act[part] = out.astype(BF)
        slope[part] = gate + out * (1.0 - tanh) * (gelu_in + 3.0 * gelu_in * gelu_cube * square)
    total = dot_nt(act[0], w2[0][...])
    for part in range(1, 4):
        total = total + dot_nt(act[part], w2[part][...])
    pre = (norm_ref[...] * gain_one + shift_one) + (total + bias_ffn)
    centre = pre - jnp.mean(pre, axis=-1, keepdims=True)
    inverse = lax.rsqrt(jnp.mean(centre * centre, axis=-1, keepdims=True) + norm_eps)
    normed = centre * inverse
    final = normed * gain_two + shift_two
    final_high = final.astype(BF)
    final_rest = (final - final_high.astype(F32)).astype(BF)
    seg = seg_ref[...]
    lane = lax.broadcasted_iota(jnp.int32, seg.shape, 1).astype(F32)
    pick = jnp.where(seg == lane, 1.0, 0.0)
    pick_across = jnp.transpose(pick).astype(BF)
    pick = pick.astype(BF)
    emb[...] += dot_nn(pick_across, final_high) + dot_nn(pick_across, final_rest)
    counts[...] += dot_nn(pick_across, jnp.ones((TILE, BLOCK), BF))
    back = dot_nn(pick, high_ref[...]) + dot_nn(pick, rest_ref[...])
    sums_ref[:, vec_at(6, width)] += column_sums(back * normed)
    sums_ref[:, vec_at(7, width)] += column_sums(back)
    grad_two = norm_back(back, normed, inverse, gain_two)
    ffn_low = grad_two.astype(BF)
    sums_ref[:, vec_at(3, width)] += column_sums(ffn_low.astype(F32))
    grad_hidden = grad_two
    for part in range(4):
        grad_act = dot_nn(ffn_low, w2[part][...])
        grad_pre = (grad_act * slope[part]).astype(BF)
        sums_ref[:, hidden_at[part]] += column_sums(grad_pre.astype(F32))
        grad_hidden = grad_hidden + dot_nt(grad_pre, w1[part][...])
        sum1[part] += dot_tn(hidden_low, grad_pre)
        sum2[part] += dot_tn(ffn_low, act[part])
    normed_one = norm_ref[...]
    sums_ref[:, vec_at(4, width)] += column_sums(grad_hidden * normed_one)
    sums_ref[:, vec_at(5, width)] += column_sums(grad_hidden)
    grad_one = norm_back(grad_hidden, normed_one, inv_ref[:, :1], gain_one)
    grad_ref[...] = grad_one
    sums_ref[:, vec_at(2, width)] += column_sums(grad_one.astype(BF).astype(F32))

    @pl.when(last)
    def _():
        places = [
            (sums.at[index], out.at[:, pl.ds(index % 2 * width, width)])
            for sums, outs in ((sum2, (down_other, down_own)), (sum1, (in_other, in_own)))
            for index, out in zip((2, 3, 0, 1), (outs[0], outs[0], outs[1], outs[1]))
        ]
        store_sums(places, stage, sems)
        held = emb_ref.shape[0]
        number = jnp.maximum(counts[:held], 1.0)
        emb_ref[...] = emb[:held] / jnp.concatenate([number] * (width // BLOCK), axis=1)


def attn_backward_kernel(
    last, core_ref, grad_ref, qkv_ref, seg_ref, before_ref, vo0, vo1, dqkv_ref, total_ref, sums
):
    width = grad_ref.shape[1]
    half = width // 2
    core = core_ref[0]

    @pl.when(pl.program_id(0) == 0)
    def _():
        sums[...] = before_ref[...]

    grad_low = grad_ref[...].astype(BF)
    masks = head_masks()
    mask = [same_sentence(seg_ref[b * BLOCK : (b + 1) * BLOCK, :]) for b in range(TILE // BLOCK)]
    for part, vo in enumerate((vo0, vo1)):
        base = part * 3 * half
        grad_att = dot_nn(grad_low, vo[:, half:]).astype(BF)
        for block in range(TILE // BLOCK):
            span = slice(block * BLOCK, (block + 1) * BLOCK)
            for pair in range(half // (2 * HEAD)):
                lanes = slice(pair * 2 * HEAD, (pair + 1) * 2 * HEAD)
                at = base + pair * 2 * HEAD
                query_at = slice(at, at + 2 * HEAD)
                key_at = slice(at + half, at + half + 2 * HEAD)
                value_at = slice(at + width, at + width + 2 * HEAD)
                query_two = two_heads(qkv_ref[span, query_at] * BF(HEAD**-0.5), masks)
                key = qkv_ref[span, key_at]
                probs = attention_probs(query_two, key, mask[block])
                att_two = two_heads(grad_att[span, lanes], masks)
                grad_probs = dot_nt(qkv_ref[span, value_at], att_two)
                inner = jnp.sum(grad_probs * probs, axis=0, keepdims=True)
                grad_scores = (probs * (grad_probs - inner)).astype(BF)
                grad_query = dot_tn(one_above_other(grad_scores), two_heads(key, masks)) * HEAD**-0.5
                dqkv_ref[span, query_at] = grad_query.astype(BF)
                dqkv_ref[span, key_at] = dot_nn(grad_scores, query_two).astype(BF)
                dqkv_ref[span, value_at] = dot_nn(probs.astype(BF), att_two).astype(BF)
        sums[:, vec_at(0, width, core, part, half)] += column_sums(
            dqkv_ref[:, base : base + half].astype(F32)
        )
        sums[:, vec_at(1, width, core, part, half)] += column_sums(
            dqkv_ref[:, base + width : base + 3 * half].astype(F32)
        )

    @pl.when(last)
    def _():
        for row in range(total_ref.shape[0]):
            lanes = sums[:, row * BLOCK : (row + 1) * BLOCK]
            total_ref[row : row + 1, :] = jnp.sum(lanes, axis=0, keepdims=True)


def attn_weight_kernel(
    last, core_ref, grad_ref, rows_ref, dqkv_ref, att_ref, qk0, vo0, qk1, vo1,
    mine_ref, dx_ref, own, other, sums, dx, stage, sems,
):
    core = core_ref[0]
    width = rows_ref.shape[1]
    half = width // 2

    @pl.when(pl.program_id(0) == 0)
    def _():
        sums[...] = jnp.zeros_like(sums)

    rows = rows_ref[...]
    grad_low = grad_ref[...].astype(BF)
    total = grad_ref[...]
    for part, (qk, vo) in enumerate(((qk0, vo0), (qk1, vo1))):
        base = part * 3 * half
        total = total + dot_nt(dqkv_ref[:, base : base + width], qk[...])
        total = total + dot_nt(dqkv_ref[:, base + width : base + 3 * half], vo[:, :half])
    dx[...] = total
    mine_ref[...] = dx[:, pl.ds(pl.multiple_of(core * half, half), half)]
    dx_ref[...] = dx[:, pl.ds(pl.multiple_of((1 - core) * half, half), half)].astype(BF)
    for part in range(2):
        base = part * 3 * half
        sums[2 * part] += dot_tn(rows, dqkv_ref[:, base : base + width])
        sums[2 * part + 1, :, :half] += dot_tn(rows, dqkv_ref[:, base + width : base + 3 * half])
        sums[2 * part + 1, :, half:] += dot_tn(grad_low, att_ref[:, part * half : (part + 1) * half])

    @pl.when(last)
    def _():
        places = [
            (sums.at[index], out.at[:, pl.ds(index % 2 * width, width)])
            for index, out in zip((2, 3, 0, 1), (other, other, own, own))
        ]
        store_sums(places, stage, sems)


def store_sums(places, stage, sems):
    copies = []
    for index, (source, target) in enumerate(places):
        slot = index % 2
        if index >= 2:
            copies[index - 2].wait()
        stage[slot] = source[...].astype(BF)
        copies.append(pltpu.make_async_copy(stage.at[slot], target, sems.at[slot]))
        copies[index].start()
    copies[-2].wait()
    copies[-1].wait()


def unpack_kernel(core_ref, order_ref, len_ref, off_ref, mine_ref, recv_ref, out_ref, *columns):
    core = core_ref[0]
    half = order_ref.shape[0] // 2
    span, cols = out_ref.shape[1], out_ref.shape[2]
    each = cols // BLOCK

    def spread(step, carry):
        rows = pl.ds(pl.multiple_of(step * BLOCK, BLOCK), BLOCK)
        for index in range(each):
            lanes = slice(index * BLOCK, (index + 1) * BLOCK)
            columns[index][rows, :] = mine_ref[rows, lanes]
            columns[each + index][rows, :] = recv_ref[rows, lanes].astype(F32)
        return carry

    lax.fori_loop(0, recv_ref.shape[0] // BLOCK, spread, 0)
    row = lax.broadcasted_iota(jnp.int32, (span, BLOCK), 0)

    def place(slot, carry):
        for which in range(2):
            parity = core if which == 0 else 1 - core
            sentence = order_ref[2 * slot + parity]
            count = len_ref[sentence]
            start = off_ref[which, slot]
            for index in range(each):
                value = columns[which * each + index][pl.ds(start, span), :]
                out_ref[sentence, :, index * BLOCK : (index + 1) * BLOCK] = jnp.where(
                    row < count, value, 0.0
                )
        return carry

    lax.fori_loop(0, half, place, 0)


SMEM_SPEC = pl.BlockSpec(memory_space=pltpu.SMEM)
VMEM_SPEC = pl.BlockSpec(memory_space=pltpu.VMEM)
HBM_SPEC = pl.BlockSpec(memory_space=pl.ANY)


def params():
    return pltpu.CompilerParams(vmem_limit_bytes=VMEM_LIMIT)


def tile_spec(cols):
    return pl.BlockSpec((TILE, cols), lambda step, tiles: (jnp.minimum(step, tiles[0] - 1), 0))


def held_spec(*shape):
    return pl.BlockSpec(
        shape, lambda step, tiles: (0,) * len(shape), pipeline_mode=pl.Buffered(1)
    )


def tiled_call(kernel, out_shape, in_specs, out_specs, scratch_shapes, cost_estimate):
    def body(tiles_ref, *refs):
        @pl.when(pl.program_id(0) < tiles_ref[0])
        def _():
            kernel(pl.program_id(0) == tiles_ref[0] - 1, *refs)

    def call(tiles, most, *operands):
        return pl.pallas_call(
            body,
            grid_spec=pltpu.PrefetchScalarGridSpec(
                num_scalar_prefetch=1,
                grid=(most // TILE,),
                in_specs=in_specs,
                out_specs=out_specs,
                scratch_shapes=scratch_shapes,
            ),
            out_shape=out_shape,
            compiler_params=params(),
            cost_estimate=cost_estimate,
        )(tiles, *operands)

    return call


def shape_of(shape, dtype):
    return jax.ShapeDtypeStruct(shape, dtype)


def cost(flops, read):
    return pl.CostEstimate(flops=int(flops), bytes_accessed=int(read), transcendentals=0)


def adam_moments(grad_value, moment, square):
    moment_new = beta_one * moment + (1.0 - beta_one) * grad_value
    square_new = beta_two * square + (1.0 - beta_two) * grad_value * grad_value
    scaled = (
        moment_new
        / (1.0 - beta_one**STEP)
        / (jnp.sqrt(square_new / (1.0 - beta_two**STEP)) + adam_eps)
    )
    return (moment_new, square_new, scaled)


def matrix_squares(qkv_part, out_part, in_part, down_part):
    return jnp.concatenate(
        [
            jnp.sum(qkv_part * qkv_part, axis=(1, 2)),
            jnp.sum(out_part * out_part)[None],
            jnp.sum(in_part * in_part)[None],
            jnp.sum(down_part * down_part)[None],
        ]
    )


def shards(
    tokens, lengths, send_order, pooled_grad,
    qkv_weight, out_weight, in_weight, down_weight, vectors,
    qkv_moment, out_moment, in_moment, down_moment, vec_moment,
    qkv_square, out_square, in_square, down_square, vec_square,
    qkv_average, out_average, in_average, down_average, vec_average,
):
    core = lax.axis_index("mp")
    count = lax.axis_size("dp")
    dims = dp_dims(count)
    sents, span, width = tokens.shape
    half = width // 2
    mine = sents // 2
    most = mine * span
    shard_rows = qkv_weight.shape[1]
    core_word = core.reshape(1).astype(jnp.int32)

    def flip(value):
        return jnp.where(core == 0, value, value[::-1])

    chunks = [
        jnp.concatenate([qkv_weight[0], qkv_weight[1], qkv_weight[2], out_weight.T], axis=1),
        in_weight,
        down_weight.T,
    ]
    first, others = dims[0], dims[1:]
    orders = (others, others[::-1])
    sides = (0, 1)

    def side_of(value, side):
        return value[..., side * width : (side + 1) * width]

    def gather_start(pieces):
        value = arrange(pieces, first, 0)
        return [(side_of(value, side), [first], orders[side]) for side in sides]

    def gather_out(state):
        return [gather_send(value, order[0]) if order else [value] for value, _, order in state]

    def gather_in(state, pieces):
        after = []
        for (value, done, order), come in zip(state, pieces):
            if order:
                axis = sum(1 for other in done if other[1] > order[0][1])
                value = arrange(come, order[0], axis)
                done = done + [order[0]]
            after.append((value, done, order[1:]))
        return after

    def gather_end(state):
        return [value.reshape(width, width) for value, _, _ in state]

    pieces0 = gather_send(chunks[0].astype(BF), first)
    share = sents // count
    if share % 2 == 0:
        own = lax.dynamic_index_in_dim(
            pooled_grad.reshape(count, share // 2, 2, width), core, 2, keepdims=False
        )
        pair_grad = lax.all_to_all(own, "dp", 0, 0, tiled=True).reshape(mine, width)
    else:
        own = lax.all_to_all(pooled_grad, "dp", 0, 0, tiled=True)
        pair_grad = lax.dynamic_index_in_dim(
            own.reshape(mine, 2, width), core, 1, keepdims=False
        )
    own_order = lax.dynamic_index_in_dim(send_order.reshape(mine, 2), core, 1, keepdims=False)
    own_count = lengths[own_order].astype(F32)[:, None]
    back = jnp.pad(pair_grad / own_count, ((0, BLOCK - mine), (0, 0)))
    back_high = back.astype(BF)
    back_rest = (back - back_high.astype(F32)).astype(BF)

    qkvo = gather_start(pieces0)
    pieces0 = gather_out(qkvo)
    held = pieces0[0][0]
    own, held = lax.optimization_barrier((chunks[1].astype(BF), held))
    pieces1 = gather_send(own, first)
    own, held = lax.optimization_barrier((chunks[2].astype(BF), pieces1[-1]))
    pieces2 = gather_send(own, first)
    qkvo = gather_in(qkvo, pieces0)
    pieces0 = gather_out(qkvo)

    order_word, _ = lax.optimization_barrier((send_order, [pieces[0] for pieces in pieces0]))
    packed = pl.pallas_call(
        pack_kernel,
        out_shape=(
            shape_of((most, width), BF),
            shape_of((most, BLOCK), F32),
            shape_of((2, mine), jnp.int32),
            shape_of((1,), jnp.int32),
        ),
        in_specs=[SMEM_SPEC, SMEM_SPEC, SMEM_SPEC, VMEM_SPEC],
        out_specs=(VMEM_SPEC, VMEM_SPEC, SMEM_SPEC, SMEM_SPEC),
        scratch_shapes=[pltpu.VMEM((most, BLOCK), F32)] * (width // BLOCK),
        compiler_params=params(),
        cost_estimate=cost(0, 30e6),
    )(core_word, order_word, lengths, tokens)
    packed, pieces0 = lax.optimization_barrier((packed, pieces0))
    rows, seg, offsets, tiles = packed
    qk, vo = [(value, swap_core(value)) for value in gather_end(gather_in(qkvo, pieces0))]

    gather1 = gather_start(pieces1)
    pieces1 = gather_out(gather1)
    gather1 = gather_in(gather1, pieces1)
    pieces1 = gather_out(gather1)
    gather2 = gather_start(pieces2)
    pieces2 = gather_out(gather2)

    square_spec = held_spec(width, width)
    vec_spec = held_spec(1, vectors.shape[0])
    vec_row = vectors.reshape(1, -1)
    row_total = most * 0.6
    starts = [pieces[0] for pieces in pieces1 + pieces2]
    tiles, _, _, _ = lax.optimization_barrier((tiles, starts, back_high, back_rest))
    qkv, att, normed, inverse = tiled_call(
        attn_forward_kernel,
        out_shape=(
            shape_of((most, 3 * width), BF),
            shape_of((most, width), BF),
            shape_of((most, width), F32),
            shape_of((most, BLOCK), F32),
        ),
        in_specs=[SMEM_SPEC, tile_spec(width), tile_spec(BLOCK), vec_spec] + [square_spec] * 4,
        out_specs=(tile_spec(3 * width), tile_spec(width), tile_spec(width), tile_spec(BLOCK)),
        scratch_shapes=[],
        cost_estimate=cost(2 * row_total * 4 * width * width * 2, 30e6),
    )(tiles, most, core_word, rows, seg, vec_row, qk[0], vo[0], qk[1], vo[1])
    normed, pieces1, pieces2 = lax.optimization_barrier((normed, pieces1, pieces2))

    gather2 = gather_in(gather2, pieces2)
    pieces2 = gather_out(gather2)
    full_in = gather_end(gather_in(gather1, pieces1))
    full_down = gather_end(gather_in(gather2, pieces2))
    w1 = full_in + [swap_core(value) for value in full_in]
    w2 = full_down + [swap_core(value) for value in full_down]
    grad_shape = shape_of((width, 2 * width), BF)
    grad_one, emb, vec_ffn, down_own, down_other, in_own, in_other = tiled_call(
        ffn_kernel,
        out_shape=(
            shape_of((most, width), F32),
            shape_of((mine, width), F32),
            shape_of((8, vectors.shape[0]), F32),
        )
        + (grad_shape,) * 4,
        in_specs=[SMEM_SPEC, tile_spec(width), tile_spec(BLOCK), tile_spec(BLOCK), vec_spec]
        + [held_spec(BLOCK, width)] * 2
        + [square_spec] * 8,
        out_specs=(tile_spec(width), held_spec(mine, width), held_spec(8, vectors.shape[0])) + (HBM_SPEC,) * 4,
        scratch_shapes=[
            pltpu.VMEM((4, width, width), F32),
            pltpu.VMEM((4, width, width), F32),
            pltpu.VMEM((4, TILE, width), BF),
            pltpu.VMEM((4, TILE, width), F32),
            pltpu.VMEM((BLOCK, width), F32),
            pltpu.VMEM((BLOCK, BLOCK), F32),
            pltpu.VMEM((2, width, width), BF),
            pltpu.SemaphoreType.DMA((2,)),
        ],
        cost_estimate=cost(2 * row_total * 24 * width * width, 30e6),
    )(tiles, most, core_word, normed, inverse, seg, vec_row, back_high, back_rest, *w1, *w2)

    def scatter_start(parts):
        state = []
        for side, (own, come) in enumerate(parts):
            value = own.astype(F32) + come.astype(F32)
            value = value.reshape(*[size for size, _ in dims], shard_rows, own.shape[-1])
            state.append((value, list(dims), orders[side][::-1]))
        return state

    def scatter_out(state):
        return [
            scatter_slabs(value, order[0], left.index(order[0])) if order else []
            for value, left, order in state
        ]

    def scatter_go(state, slabs):
        return [scatter_send(sent, order[0]) if order else [] for (_, _, order), sent in zip(state, slabs)]

    def scatter_in(state, arrived):
        after = []
        for (value, left, order), come in zip(state, arrived):
            if order:
                value = scatter_sum(value, come, order[0], left.index(order[0]))
                left = [dim for dim in left if dim != order[0]]
            after.append((value, left, order[1:]))
        return after

    def scatter_rest(state, after=None):
        while state[0][2]:
            state = scatter_in(state, lax.optimization_barrier(scatter_go(state, scatter_out(state))))
        return state

    def scatter_end(state):
        value = jnp.concatenate([value for value, _, _ in state], axis=-1)
        return scatter_sum(value, scatter_send(scatter_slabs(value, first, 0), first), first, 0)

    ffn_send = scatter_start(((down_own, swap_core(down_other)), (in_own, swap_core(in_other))))
    slabs = scatter_out(ffn_send)
    tiles, slabs = lax.optimization_barrier((tiles, slabs))
    dqkv, vec_local = tiled_call(
        attn_backward_kernel,
        out_shape=(
            shape_of((most, 3 * width), BF),
            shape_of((vectors.shape[0] // BLOCK, BLOCK), F32),
        ),
        in_specs=[
            SMEM_SPEC, tile_spec(width), tile_spec(3 * width), tile_spec(BLOCK), held_spec(8, vectors.shape[0]),
        ]
        + [square_spec] * 2,
        out_specs=(tile_spec(3 * width), held_spec(vectors.shape[0] // BLOCK, BLOCK)),
        scratch_shapes=[pltpu.VMEM((8, vectors.shape[0]), F32)],
        cost_estimate=cost(2 * row_total * 8 * width * width * 1.5, 30e6),
    )(tiles, most, core_word, grad_one, qkv, seg, vec_ffn, vo[0], vo[1])
    arrived, dqkv, emb = lax.optimization_barrier((scatter_go(ffn_send, slabs), dqkv, emb))
    ffn_send = scatter_in(ffn_send, arrived)
    slabs = scatter_out(ffn_send)
    tiles, slabs = lax.optimization_barrier((tiles, slabs))

    dx_mine, dx_other, own, other = tiled_call(
        attn_weight_kernel,
        out_shape=(shape_of((most, half), F32), shape_of((most, half), BF)) + (grad_shape,) * 2,
        in_specs=[SMEM_SPEC, tile_spec(width), tile_spec(width), tile_spec(3 * width), tile_spec(width)]
        + [square_spec] * 4,
        out_specs=(tile_spec(half), tile_spec(half)) + (HBM_SPEC,) * 2,
        scratch_shapes=[
            pltpu.VMEM((4, width, width), F32),
            pltpu.VMEM((TILE, width), F32),
            pltpu.VMEM((2, width, width), BF),
            pltpu.SemaphoreType.DMA((2,)),
        ],
        cost_estimate=cost(2 * row_total * 8 * width * width * 1.5, 30e6),
    )(tiles, most, core_word, grad_one, rows, dqkv, att, qk[0], vo[0], qk[1], vo[1])
    arrived, own, other, emb = lax.optimization_barrier((scatter_go(ffn_send, slabs), own, other, emb))

    come = swap_core(other)
    qkvo_send = scatter_start([(side_of(own, side), side_of(come, side)) for side in sides])
    slabs = scatter_out(qkvo_send)
    ffn_send = scatter_in(ffn_send, arrived)
    ffn_all = jnp.concatenate([value for value, _, _ in ffn_send], axis=-1)
    last_slabs = scatter_slabs(ffn_all, first, 0)
    order_word, slabs, last_slabs = lax.optimization_barrier((send_order, slabs, last_slabs))
    go = scatter_go(qkvo_send, slabs)
    last_go = scatter_send(last_slabs, first)

    tokens_grad = pl.pallas_call(
        unpack_kernel,
        out_shape=shape_of((sents, span, half), F32),
        in_specs=[SMEM_SPEC] * 4 + [VMEM_SPEC] * 2,
        out_specs=VMEM_SPEC,
        scratch_shapes=[pltpu.VMEM((most, BLOCK), F32)] * (2 * half // BLOCK),
        compiler_params=params(),
        cost_estimate=cost(0, 20e6),
    )(core_word, order_word, lengths, offsets, dx_mine, swap_core(dx_other))
    go, last_go, tokens_grad, emb = lax.optimization_barrier((go, last_go, tokens_grad, emb))
    ffn_grad = scatter_sum(ffn_all, last_go, first, 0)
    qkvo_grad = scatter_end(scatter_rest(scatter_in(qkvo_send, go)))

    if share % 2 == 0:
        arrived = lax.all_to_all(emb.reshape(count, share // 2, width), "dp", 0, 0, tiled=True)
        both = flip(jnp.stack([arrived, swap_core(arrived)]))
        pooled = jnp.moveaxis(both, 0, 2).reshape(sents, width)
    else:
        both = flip(jnp.stack([emb, swap_core(emb)]))
        both = jnp.moveaxis(both, 0, 1).reshape(sents, width)
        pooled = lax.all_to_all(both, "dp", 0, 0, tiled=True)

    qkv_grad = jnp.stack([qkvo_grad[:, index * half : (index + 1) * half] for index in range(3)])
    out_grad = qkvo_grad[:, 3 * half :].T
    down_grad = ffn_grad[:, : 2 * width].T
    in_grad = ffn_grad[:, 2 * width :]

    qkv_m, qkv_s, qkv_n = adam_moments(qkv_grad, qkv_moment, qkv_square)
    out_m, out_s, out_n = adam_moments(out_grad, out_moment, out_square)
    in_m, in_s, in_n = adam_moments(in_grad, in_moment, in_square)
    down_m, down_s, down_n = adam_moments(down_grad, down_moment, down_square)
    qkv_u = qkv_n + weight_decay * qkv_weight
    out_u = out_n + weight_decay * out_weight
    in_u = in_n + weight_decay * in_weight
    down_u = down_n + weight_decay * down_weight
    weight_local = matrix_squares(qkv_weight, out_weight, in_weight, down_weight)
    update_local = matrix_squares(qkv_u, out_u, in_u, down_u)
    norms = jnp.pad(jnp.stack([weight_local, update_local]), ((0, 6), (0, BLOCK - 6)))
    totals = sum_all(jnp.concatenate([vec_local, norms]), dims)
    vec_grad = totals[:-8].reshape(-1)
    vec_m, vec_s, vec_n = adam_moments(vec_grad, vec_moment, vec_square)
    weight_norm = jnp.sqrt(totals[-8, :6])
    update_norm = jnp.sqrt(totals[-7, :6])
    trust_ratio = weight_norm / update_norm
    new_qkv = qkv_weight - learn_rate * trust_ratio[:3, None, None] * qkv_u
    new_out = out_weight - learn_rate * trust_ratio[3] * out_u
    new_in = in_weight - learn_rate * trust_ratio[4] * in_u
    new_down = down_weight - learn_rate * trust_ratio[5] * down_u
    new_vec = vectors - vector_rate * vec_n
    return (
        pooled, tokens_grad, qkv_grad, out_grad, in_grad, down_grad, vec_grad,
        trust_ratio, weight_norm, update_norm,
        qkv_m, out_m, in_m, down_m, vec_m,
        qkv_s, out_s, in_s, down_s, vec_s,
        new_qkv, new_out, new_in, new_down, new_vec,
        ema_keep * qkv_average + (1.0 - ema_keep) * new_qkv,
        ema_keep * out_average + (1.0 - ema_keep) * new_out,
        ema_keep * in_average + (1.0 - ema_keep) * new_in,
        ema_keep * down_average + (1.0 - ema_keep) * new_down,
        ema_keep * vec_average + (1.0 - ema_keep) * new_vec,
    )


def solution(mesh):
    matrices = (P(None, "dp", "mp"), P("mp", "dp"), P("dp", "mp"), P("mp", "dp"), P())
    return jax.shard_map(
        shards,
        mesh=mesh,
        in_specs=(P("dp", None, None), P("dp"), P("dp"), P("dp", None)) + matrices * 4,
        out_specs=(P("dp", None), P("dp", None, "mp")) + matrices + (P(), P(), P()) + matrices * 4,
        check_vma=False,
    )
```

```python
import jax
import jax.numpy as jnp
from jax import lax
from jax.experimental import pallas as pl
from jax.experimental.pallas import tpu as pltpu
from jax.sharding import PartitionSpec as P

HEAD = 64
STEP = 10
TILE = 256
BLOCK = 128

beta_one = 0.9
beta_two = 0.999
adam_eps = 1e-06
weight_decay = 0.01
learn_rate = 0.3
vector_rate = 0.05
ema_keep = 0.9
norm_eps = 1e-12
masked_score = -1000000000.0
gelu_in = 0.7978845608028654
gelu_cube = 0.044715

BF = jnp.bfloat16
F32 = jnp.float32
VMEM_LIMIT = 60 * 1024 * 1024


def dp_dims(count):
    known = {16: ((4, 4), (2, 2), (2, 1)), 128: ((4, 32), (8, 4), (4, 1))}
    return known.get(count, ((count, 1),))


def dp_shift(value, dim, step):
    size, stride = dim
    count = lax.axis_size("dp")
    pairs = []
    for index in range(count):
        place = index // stride % size
        pairs.append((index, index + ((place + step) % size - place) * stride))
    return lax.ppermute(value, "dp", pairs)


def dp_place(dim):
    size, stride = dim
    return lax.rem(lax.div(lax.axis_index("dp"), stride), size)


def swap_core(value):
    return lax.ppermute(value, "mp", [(0, 1), (1, 0)])


def arrange(pieces, dim, axis):
    size, _ = dim
    place = dp_place(dim)
    if size == 2:
        return jnp.where(place == 0, jnp.stack(pieces, axis), jnp.stack(pieces[::-1], axis))
    ordered = []
    for target in range(size):
        which = lax.rem(target - place + size, size)
        chosen = pieces[0]
        for step in range(1, size):
            chosen = jnp.where(which == step, pieces[step], chosen)
        ordered.append(chosen)
    return jnp.stack(ordered, axis)


def gather_send(value, dim):
    return [value] + [dp_shift(value, dim, -step) for step in range(1, dim[0])]


def scatter_send(slabs, dim):
    return [dp_shift(slab, dim, step) for step, slab in enumerate(slabs, 1)]


def sum_all(value, dims):
    value = value + swap_core(value)
    count = lax.axis_size("dp")
    for size, stride in dims:
        bit = 1
        while bit < size:
            pairs = []
            for index in range(count):
                place = index // stride % size
                pairs.append((index, index + ((place ^ bit) - place) * stride))
            value = value + lax.ppermute(value, "dp", pairs)
            bit *= 2
    return value


def dot_nn(left, right):
    return jnp.dot(left, right, preferred_element_type=F32)


def dot_nt(left, right):
    return lax.dot_general(left, right, (((1,), (1,)), ((), ())), preferred_element_type=F32)


def dot_tn(left, right):
    return lax.dot_general(left, right, (((0,), (0,)), ((), ())), preferred_element_type=F32)


def vec_at(index, width, core=None, part=0, cols=None):
    if core is None:
        return slice(index * width, (index + 1) * width)
    which = core if part == 0 else 1 - core
    return pl.ds(pl.multiple_of(index * width + which * cols, BLOCK), cols)


def column_sums(value):
    rows, cols = value.shape
    return jnp.sum(value.reshape(rows // 8, 8, cols), axis=0)


def pack_kernel(
    core_ref, order_ref, len_ref, tok_ref, rows_ref, seg_ref, off_ref, tiles_ref, *stage
):
    core = core_ref[0]
    half = order_ref.shape[0] // 2
    total = rows_ref.shape[0]

    def clear(step, carry):
        rows = pl.ds(pl.multiple_of(step * BLOCK, BLOCK), BLOCK)
        for column in stage:
            column[rows, :] = jnp.zeros((BLOCK, BLOCK), F32)
        seg_ref[rows, :] = jnp.full((BLOCK, BLOCK), -1.0, F32)
        return carry

    lax.fori_loop(0, total // BLOCK, clear, 0)

    def start_of(cursor, count):
        inside = cursor & (BLOCK - 1)
        return jnp.where(inside + count > BLOCK, cursor - inside + BLOCK, cursor)

    def place(slot, cursor):
        sentence = order_ref[2 * slot + core]
        count = len_ref[sentence]
        start = start_of(cursor, count)
        off_ref[0, slot] = start
        span = tok_ref.shape[1]
        value = tok_ref[sentence].astype(F32)
        for index, column in enumerate(stage):
            column[pl.ds(start, span), :] = value[:, index * BLOCK : (index + 1) * BLOCK]
        row = lax.broadcasted_iota(jnp.int32, (span, BLOCK), 0)
        seg_ref[pl.ds(start, span), :] = jnp.where(row < count, slot.astype(F32), -1.0)
        return start + count

    used = lax.fori_loop(0, half, place, 0)
    tiles_ref[0] = (used + TILE - 1) // TILE

    def partner(slot, cursor):
        count = len_ref[order_ref[2 * slot + 1 - core]]
        start = start_of(cursor, count)
        off_ref[1, slot] = start
        return start + count

    lax.fori_loop(0, half, partner, 0)

    def low(step, carry):
        rows = pl.ds(pl.multiple_of(step * BLOCK, BLOCK), BLOCK)
        for index, column in enumerate(stage):
            rows_ref[rows, index * BLOCK : (index + 1) * BLOCK] = column[rows, :].astype(BF)
        return carry

    lax.fori_loop(0, total // BLOCK, low, 0)


def head_masks():
    lane = lax.broadcasted_iota(jnp.int32, (1, 2 * HEAD), 1)
    first = jnp.where(lane < HEAD, 1.0, 0.0)
    return first.astype(BF), (1.0 - first).astype(BF)


def two_heads(value, masks):
    return jnp.concatenate([value * masks[0], value * masks[1]], axis=0)


def same_sentence(seg):
    across = jnp.transpose(seg)
    return jnp.concatenate([seg, seg], axis=1) == jnp.concatenate([across, across], axis=1)


def attention_probs(query_two, key, mask):
    scores = jnp.where(mask, dot_nt(key, query_two), masked_score)
    expon = jnp.exp(scores - jnp.max(scores, axis=0, keepdims=True))
    return expon * (1.0 / jnp.sum(expon, axis=0, keepdims=True))


def one_above_other(value):
    return jnp.concatenate([value[:, :BLOCK], value[:, BLOCK:]], axis=0)


def attn_forward_kernel(
    last, core_ref, rows_ref, seg_ref, vec_ref, qk0, vo0, qk1, vo1, qkv_ref, att_ref, norm_ref, inv_ref
):
    width = rows_ref.shape[1]
    half = width // 2
    core = core_ref[0]
    rows = rows_ref[...]
    weights = ((qk0, vo0), (qk1, vo1))
    for part, (qk, vo) in enumerate(weights):
        base = part * 3 * half
        value = dot_nn(rows, qk[...])
        query = value[:, :half] + vec_ref[:, vec_at(0, width, core, part, half)]
        qkv_ref[:, base : base + half] = query.astype(BF)
        qkv_ref[:, base + half : base + width] = value[:, half:].astype(BF)
        value = dot_nn(rows, vo[:, :half]) + vec_ref[:, vec_at(1, width, core, part, half)]
        qkv_ref[:, base + width : base + 3 * half] = value.astype(BF)
    masks = head_masks()
    for block in range(TILE // BLOCK):
        span = slice(block * BLOCK, (block + 1) * BLOCK)
        mask = same_sentence(seg_ref[span, :])
        for part in range(2):
            for pair in range(half // (2 * HEAD)):
                at = part * 3 * half + pair * 2 * HEAD
                query = qkv_ref[span, at : at + 2 * HEAD] * BF(HEAD**-0.5)
                key = qkv_ref[span, at + half : at + half + 2 * HEAD]
                value = qkv_ref[span, at + width : at + width + 2 * HEAD]
                probs = attention_probs(two_heads(query, masks), key, mask).astype(BF)
                mixed = dot_tn(one_above_other(probs), two_heads(value, masks))
                to = part * half + pair * 2 * HEAD
                att_ref[span, to : to + 2 * HEAD] = mixed.astype(BF)
    mixed = dot_nt(att_ref[:, :half], vo0[:, half:]) + dot_nt(att_ref[:, half:], vo1[:, half:])
    pre = rows.astype(F32) + (mixed + vec_ref[:, vec_at(2, width)])
    centre = pre - jnp.mean(pre, axis=-1, keepdims=True)
    inverse = lax.rsqrt(jnp.mean(centre * centre, axis=-1, keepdims=True) + norm_eps)
    norm_ref[...] = centre * inverse
    inv_ref[...] = jnp.broadcast_to(inverse, inv_ref.shape)


def norm_back(grad, normed, inverse, gain):
    scaled = grad * gain
    first = jnp.mean(scaled, axis=-1, keepdims=True)
    second = jnp.mean(scaled * normed, axis=-1, keepdims=True)
    return (scaled - first - normed * second) * inverse


def hidden_pieces(core, width):
    return [
        pl.ds(
            pl.multiple_of(8 * width + (2 * (core if part < 2 else 1 - core) + part % 2) * width, BLOCK),
            width,
        )
        for part in range(4)
    ]


def ffn_kernel(
    last, core_ref, norm_ref, inv_ref, seg_ref, att_ref, vec_ref, high_ref, rest_ref,
    w1_own, w1_other, w2_own, w2_other,
    grad_ref, emb_ref, sums_ref, down_own, down_other, in_own, in_other,
    sum1, sum2, sum3, act, slope, emb, counts, stage, sems,
):
    step = pl.program_id(0)
    width = norm_ref.shape[1]
    half = width // 2
    lanes = [slice(part % 2 * width, (part % 2 + 1) * width) for part in range(4)]
    w1 = [(w1_own, w1_other)[part // 2].at[:, lanes[part]] for part in range(4)]
    w2 = [(w2_own, w2_other)[part // 2].at[:, lanes[part]] for part in range(4)]
    hidden_at = hidden_pieces(core_ref[0], width)

    @pl.when(step == 0)
    def _():
        emb[...] = jnp.zeros_like(emb)
        counts[...] = jnp.zeros_like(counts)
        sums_ref[...] = jnp.zeros_like(sums_ref)
        sum1[...] = jnp.zeros_like(sum1)
        sum2[...] = jnp.zeros_like(sum2)
        sum3[...] = jnp.zeros_like(sum3)

    gain_one, shift_one = vec_ref[:, vec_at(4, width)], vec_ref[:, vec_at(5, width)]
    gain_two, shift_two = vec_ref[:, vec_at(6, width)], vec_ref[:, vec_at(7, width)]
    bias_ffn = vec_ref[:, vec_at(3, width)]
    hidden_low = (norm_ref[...] * gain_one + shift_one).astype(BF)
    for part in range(4):
        pre = dot_nn(hidden_low, w1[part][...]) + vec_ref[:, hidden_at[part]]
        square = pre * pre
        tanh = jnp.tanh(pre * (gelu_in + gelu_in * gelu_cube * square))
        gate = 0.5 + 0.5 * tanh
        out = pre * gate
        act[part] = out.astype(BF)
        slope[part] = gate + out * (1.0 - tanh) * (gelu_in + 3.0 * gelu_in * gelu_cube * square)
    total = dot_nt(act[0], w2[0][...])
    for part in range(1, 4):
        total = total + dot_nt(act[part], w2[part][...])
    pre = (norm_ref[...] * gain_one + shift_one) + (total + bias_ffn)
    centre = pre - jnp.mean(pre, axis=-1, keepdims=True)
    inverse = lax.rsqrt(jnp.mean(centre * centre, axis=-1, keepdims=True) + norm_eps)
    normed = centre * inverse
    final = normed * gain_two + shift_two
    final_high = final.astype(BF)
    final_rest = (final - final_high.astype(F32)).astype(BF)
    seg = seg_ref[...]
    lane = lax.broadcasted_iota(jnp.int32, seg.shape, 1).astype(F32)
    pick = jnp.where(seg == lane, 1.0, 0.0)
    pick_across = jnp.transpose(pick).astype(BF)
    pick = pick.astype(BF)
    emb[...] += dot_nn(pick_across, final_high) + dot_nn(pick_across, final_rest)
    counts[...] += dot_nn(pick_across, jnp.ones((TILE, BLOCK), BF))
    back = dot_nn(pick, high_ref[...]) + dot_nn(pick, rest_ref[...])
    sums_ref[:, vec_at(6, width)] += column_sums(back * normed)
    sums_ref[:, vec_at(7, width)] += column_sums(back)
    grad_two = norm_back(back, normed, inverse, gain_two)
    ffn_low = grad_two.astype(BF)
    sums_ref[:, vec_at(3, width)] += column_sums(ffn_low.astype(F32))
    grad_hidden = grad_two
    for part in range(4):
        grad_act = dot_nn(ffn_low, w2[part][...])
        grad_pre = (grad_act * slope[part]).astype(BF)
        sums_ref[:, hidden_at[part]] += column_sums(grad_pre.astype(F32))
        grad_hidden = grad_hidden + dot_nt(grad_pre, w1[part][...])
        sum1[part] += dot_tn(hidden_low, grad_pre)
        sum2[part] += dot_tn(ffn_low, act[part])
    normed_one = norm_ref[...]
    sums_ref[:, vec_at(4, width)] += column_sums(grad_hidden * normed_one)
    sums_ref[:, vec_at(5, width)] += column_sums(grad_hidden)
    grad_one = norm_back(grad_hidden, normed_one, inv_ref[:, :1], gain_one)
    grad_ref[...] = grad_one
    grad_low = grad_one.astype(BF)
    for part in range(2):
        sum3[part] += dot_tn(grad_low, att_ref[:, part * half : (part + 1) * half])
    sums_ref[:, vec_at(2, width)] += column_sums(grad_low.astype(F32))

    @pl.when(last)
    def _():
        places = []
        for outs, sums in (((down_own, down_other), sum2), ((in_own, in_other), sum1)):
            for index in (2, 3, 0, 1):
                target = outs[index // 2].at[:, pl.ds(index % 2 * width, width)]
                places.append((sums.at[index], target))
        for index in (1, 0):
            target = (down_own, down_other)[index].at[:, pl.ds(2 * width, half)]
            places.append((sum3.at[index], target))
        store_sums(places, stage, sems)
        held = emb_ref.shape[0]
        number = jnp.maximum(counts[:held], 1.0)
        emb_ref[...] = emb[:held] / jnp.concatenate([number] * (width // BLOCK), axis=1)


def attn_backward_kernel(
    last, core_ref, grad_ref, qkv_ref, seg_ref, before_ref, vo0, vo1, dqkv_ref, total_ref, sums
):
    width = grad_ref.shape[1]
    half = width // 2
    core = core_ref[0]

    @pl.when(pl.program_id(0) == 0)
    def _():
        sums[...] = before_ref[...]

    grad_low = grad_ref[...].astype(BF)
    masks = head_masks()
    mask = [same_sentence(seg_ref[b * BLOCK : (b + 1) * BLOCK, :]) for b in range(TILE // BLOCK)]
    for part, vo in enumerate((vo0, vo1)):
        base = part * 3 * half
        grad_att = dot_nn(grad_low, vo[:, half:]).astype(BF)
        for block in range(TILE // BLOCK):
            span = slice(block * BLOCK, (block + 1) * BLOCK)
            for pair in range(half // (2 * HEAD)):
                lanes = slice(pair * 2 * HEAD, (pair + 1) * 2 * HEAD)
                at = base + pair * 2 * HEAD
                query_at = slice(at, at + 2 * HEAD)
                key_at = slice(at + half, at + half + 2 * HEAD)
                value_at = slice(at + width, at + width + 2 * HEAD)
                query_two = two_heads(qkv_ref[span, query_at] * BF(HEAD**-0.5), masks)
                key = qkv_ref[span, key_at]
                probs = attention_probs(query_two, key, mask[block])
                att_two = two_heads(grad_att[span, lanes], masks)
                grad_probs = dot_nt(qkv_ref[span, value_at], att_two)
                inner = jnp.sum(grad_probs * probs, axis=0, keepdims=True)
                grad_scores = (probs * (grad_probs - inner)).astype(BF)
                grad_query = dot_tn(one_above_other(grad_scores), two_heads(key, masks)) * HEAD**-0.5
                dqkv_ref[span, query_at] = grad_query.astype(BF)
                dqkv_ref[span, key_at] = dot_nn(grad_scores, query_two).astype(BF)
                dqkv_ref[span, value_at] = dot_nn(probs.astype(BF), att_two).astype(BF)
        sums[:, vec_at(0, width, core, part, half)] += column_sums(
            dqkv_ref[:, base : base + half].astype(F32)
        )
        sums[:, vec_at(1, width, core, part, half)] += column_sums(
            dqkv_ref[:, base + width : base + 3 * half].astype(F32)
        )

    @pl.when(last)
    def _():
        for row in range(total_ref.shape[0]):
            lanes = sums[:, row * BLOCK : (row + 1) * BLOCK]
            total_ref[row : row + 1, :] = jnp.sum(lanes, axis=0, keepdims=True)


def attn_weight_kernel(
    last, core_ref, grad_ref, rows_ref, dqkv_ref, qk0, vo0, qk1, vo1,
    mine_ref, dx_ref, own, other, sums, dx, stage, sems,
):
    core = core_ref[0]
    width = rows_ref.shape[1]
    half = width // 2

    @pl.when(pl.program_id(0) == 0)
    def _():
        sums[...] = jnp.zeros_like(sums)

    rows = rows_ref[...]
    total = grad_ref[...]
    for part, (qk, vo) in enumerate(((qk0, vo0), (qk1, vo1))):
        base = part * 3 * half
        total = total + dot_nt(dqkv_ref[:, base : base + width], qk[...])
        total = total + dot_nt(dqkv_ref[:, base + width : base + 3 * half], vo[:, :half])
    dx[...] = total
    mine_ref[...] = dx[:, pl.ds(pl.multiple_of(core * half, half), half)]
    dx_ref[...] = dx[:, pl.ds(pl.multiple_of((1 - core) * half, half), half)].astype(BF)
    for part in range(2):
        sums[part] += dot_tn(rows, dqkv_ref[:, part * 3 * half : (part + 1) * 3 * half])

    @pl.when(last)
    def _():
        store_sums([(sums.at[1], other), (sums.at[0], own)], stage, sems)


def store_sums(places, stage, sems):
    copies = []
    for index, (source, target) in enumerate(places):
        slot = index % 2
        if index >= 2:
            copies[index - 2].wait()
        cols = source.shape[-1]
        stage[slot, :, :cols] = source[...].astype(BF)
        copies.append(pltpu.make_async_copy(stage.at[slot, :, pl.ds(0, cols)], target, sems.at[slot]))
        copies[index].start()
    copies[-2].wait()
    copies[-1].wait()


def unpack_kernel(core_ref, order_ref, len_ref, off_ref, mine_ref, recv_ref, out_ref, *columns):
    core = core_ref[0]
    half = order_ref.shape[0] // 2
    span, cols = out_ref.shape[1], out_ref.shape[2]
    each = cols // BLOCK

    def spread(step, carry):
        rows = pl.ds(pl.multiple_of(step * BLOCK, BLOCK), BLOCK)
        for index in range(each):
            lanes = slice(index * BLOCK, (index + 1) * BLOCK)
            columns[index][rows, :] = mine_ref[rows, lanes]
            columns[each + index][rows, :] = recv_ref[rows, lanes].astype(F32)
        return carry

    lax.fori_loop(0, recv_ref.shape[0] // BLOCK, spread, 0)
    row = lax.broadcasted_iota(jnp.int32, (span, BLOCK), 0)

    def place(slot, carry):
        for which in range(2):
            parity = core if which == 0 else 1 - core
            sentence = order_ref[2 * slot + parity]
            count = len_ref[sentence]
            start = off_ref[which, slot]
            for index in range(each):
                value = columns[which * each + index][pl.ds(start, span), :]
                out_ref[sentence, :, index * BLOCK : (index + 1) * BLOCK] = jnp.where(
                    row < count, value, 0.0
                )
        return carry

    lax.fori_loop(0, half, place, 0)


SMEM_SPEC = pl.BlockSpec(memory_space=pltpu.SMEM)
VMEM_SPEC = pl.BlockSpec(memory_space=pltpu.VMEM)
HBM_SPEC = pl.BlockSpec(memory_space=pl.ANY)


def params():
    return pltpu.CompilerParams(vmem_limit_bytes=VMEM_LIMIT)


def tile_spec(cols):
    return pl.BlockSpec((TILE, cols), lambda step, tiles: (jnp.minimum(step, tiles[0] - 1), 0))


def held_spec(*shape):
    return pl.BlockSpec(
        shape, lambda step, tiles: (0,) * len(shape), pipeline_mode=pl.Buffered(1)
    )


def tiled_call(kernel, out_shape, in_specs, out_specs, scratch_shapes, cost_estimate):
    def body(tiles_ref, *refs):
        @pl.when(pl.program_id(0) < tiles_ref[0])
        def _():
            kernel(pl.program_id(0) == tiles_ref[0] - 1, *refs)

    def call(tiles, most, *operands):
        return pl.pallas_call(
            body,
            grid_spec=pltpu.PrefetchScalarGridSpec(
                num_scalar_prefetch=1,
                grid=(most // TILE,),
                in_specs=in_specs,
                out_specs=out_specs,
                scratch_shapes=scratch_shapes,
            ),
            out_shape=out_shape,
            compiler_params=params(),
            cost_estimate=cost_estimate,
        )(tiles, *operands)

    return call


def shape_of(shape, dtype):
    return jax.ShapeDtypeStruct(shape, dtype)


def cost(flops, read):
    return pl.CostEstimate(flops=int(flops), bytes_accessed=int(read), transcendentals=0)


class Side:
    def __init__(self, terms, order):
        self.terms, self.order = terms, order

    def cols(self):
        _, _, lanes = self.terms[0]
        return lanes.stop - lanes.start


def slab_sums(sides, dims, joined=False):
    first = dims[0]
    places = jnp.stack([dp_place(dim) for dim in dims]).astype(jnp.int32)
    at_of = {dim: index for index, dim in enumerate(dims)}
    nexts = [first if joined else side.order[0] for side in sides]
    lead = 1 if joined else first[0]
    operands, in_specs, plan = [], [], []
    out_shape, out_specs, targets = [], [], []

    def index_map(term_dims, current, step, size, fixed):
        def of(grid, at):
            index = []
            for dim in term_dims:
                if dim == current:
                    index.append(lax.rem(at[at_of[dim]] + step, size))
                elif dim == first:
                    index.append(grid)
                else:
                    index.append(at[at_of[dim]] if dim in fixed else 0)
            return (*index, 0, 0)

        return of

    for number, (side, current) in enumerate(zip(sides, nexts)):
        size = current[0]
        rows = side.terms[0][0].shape[-2]
        left = [dim for dim in side.terms[-1][1] if dim != current]
        fixed = [dim for dim in dims if dim != current and dim not in left]
        steps = range(size) if joined else range(1, size)
        for step in steps:
            ids = []
            for array, term_dims, lanes in side.terms:
                block, pick = [], []
                for dim in term_dims:
                    whole = dim in left and dim != first
                    block.append(dim[0] if whole else 1)
                    pick.append(slice(None) if whole else 0)
                ids.append((len(operands), tuple(pick), lanes))
                operands.append(array)
                in_specs.append(
                    pl.BlockSpec((*block, rows, array.shape[-1]), index_map(term_dims, current, step, size, fixed))
                )
            plan.append((ids, number, step))
        if not joined:
            rest = [dim[0] for dim in left if dim != first]
            for step in steps:
                shape = (lead, *rest, rows, side.cols())
                out_shape.append(shape_of(shape, BF))
                out_specs.append(pl.BlockSpec((1, *shape[1:]), lambda grid, at, n=len(shape): (grid,) + (0,) * (n - 1)))
                targets.append((number, step))
    if joined:
        width = sum(side.cols() for side in sides)
        rows = sides[0].terms[0][0].shape[-2]
        for step in range(first[0]):
            out_shape.append(shape_of((rows, width), BF if step else F32))
            out_specs.append(pl.BlockSpec((rows, width), lambda grid, at: (0, 0)))
            targets.append((None, step))
    starts = [sum(side.cols() for side in sides[:number]) for number in range(len(sides))]

    def kernel(places_ref, *refs):
        ins, outs = refs[: len(operands)], refs[len(operands) :]
        for ids, number, step in plan:
            total = None
            for index, pick, lanes in ids:
                value = ins[index][(*pick, slice(None), lanes)].astype(F32)
                total = value if total is None else total + value
            if joined:
                out = outs[targets.index((None, step))]
                out[:, starts[number] : starts[number] + sides[number].cols()] = total.astype(out.dtype)
            else:
                out = outs[targets.index((number, step))]
                out[0] = total.astype(BF)

    sums = pl.pallas_call(
        kernel,
        grid_spec=pltpu.PrefetchScalarGridSpec(
            num_scalar_prefetch=1, grid=(lead,), in_specs=in_specs, out_specs=out_specs
        ),
        out_shape=out_shape,
        compiler_params=params(),
        cost_estimate=cost(0, 8e6),
    )(places, *operands)
    if joined:
        return sums
    return [[value for value, (which, _) in zip(sums, targets) if which == number] for number in range(len(sides))]


def adam_moments(grad_value, moment, square):
    moment_new = beta_one * moment + (1.0 - beta_one) * grad_value
    square_new = beta_two * square + (1.0 - beta_two) * grad_value * grad_value
    scaled = (
        moment_new
        / (1.0 - beta_one**STEP)
        / (jnp.sqrt(square_new / (1.0 - beta_two**STEP)) + adam_eps)
    )
    return (moment_new, square_new, scaled)


def matrix_squares(qkv_part, out_part, in_part, down_part):
    return jnp.concatenate(
        [
            jnp.sum(qkv_part * qkv_part, axis=(1, 2)),
            jnp.sum(out_part * out_part)[None],
            jnp.sum(in_part * in_part)[None],
            jnp.sum(down_part * down_part)[None],
        ]
    )


def shards(
    tokens, lengths, send_order, pooled_grad,
    qkv_weight, out_weight, in_weight, down_weight, vectors,
    qkv_moment, out_moment, in_moment, down_moment, vec_moment,
    qkv_square, out_square, in_square, down_square, vec_square,
    qkv_average, out_average, in_average, down_average, vec_average,
):
    core = lax.axis_index("mp")
    count = lax.axis_size("dp")
    dims = dp_dims(count)
    sents, span, width = tokens.shape
    half = width // 2
    mine = sents // 2
    most = mine * span
    shard_rows = qkv_weight.shape[1]
    core_word = core.reshape(1).astype(jnp.int32)

    def flip(value):
        return jnp.where(core == 0, value, value[::-1])

    chunks = [
        jnp.concatenate([qkv_weight[0], qkv_weight[1], qkv_weight[2], out_weight.T], axis=1),
        in_weight,
        down_weight.T,
    ]
    first, others = dims[0], dims[1:]
    orders = (others, others[::-1])
    sides = (0, 1)

    def gather_start(pieces):
        value = arrange(pieces, first, 0)
        cols = value.shape[-1] // 2
        return [
            (value[..., side * cols : (side + 1) * cols], [first], orders[side]) for side in sides
        ]

    def gather_out(state):
        return [gather_send(value, order[0]) if order else [value] for value, _, order in state]

    def gather_in(state, pieces):
        after = []
        for (value, done, order), come in zip(state, pieces):
            if order:
                axis = sum(1 for other in done if other[1] > order[0][1])
                value = arrange(come, order[0], axis)
                done = done + [order[0]]
            after.append((value, done, order[1:]))
        return after

    def gather_end(state):
        return [value.reshape(width, -1) for value, _, _ in state]

    share = sents // count
    if share % 2 == 0:
        own = lax.dynamic_index_in_dim(
            pooled_grad.reshape(count, share // 2, 2, width), core, 2, keepdims=False
        )
        pair_grad = lax.all_to_all(own, "dp", 0, 0, tiled=True).reshape(mine, width)
    else:
        own = lax.all_to_all(pooled_grad, "dp", 0, 0, tiled=True)
        pair_grad = lax.dynamic_index_in_dim(
            own.reshape(mine, 2, width), core, 1, keepdims=False
        )

    pieces0 = gather_send(chunks[0].astype(BF), first)
    qkvo = gather_start(pieces0)
    pieces0 = gather_out(qkvo)
    held = [pieces[0] for pieces in pieces0]
    own, held = lax.optimization_barrier((chunks[1].astype(BF), held))
    pieces1 = gather_send(own, first)
    pieces0, pieces1, pair_grad = lax.optimization_barrier((pieces0, pieces1, pair_grad))
    qkvo = gather_in(qkvo, pieces0)
    pieces0 = gather_out(qkvo)
    held = [pieces[0] for pieces in pieces0]
    own, held = lax.optimization_barrier((chunks[2].astype(BF), held))
    pieces2 = gather_send(own, first)

    order_word, _ = lax.optimization_barrier((send_order, [pieces[0] for pieces in pieces0]))
    packed = pl.pallas_call(
        pack_kernel,
        out_shape=(
            shape_of((most, width), BF),
            shape_of((most, BLOCK), F32),
            shape_of((2, mine), jnp.int32),
            shape_of((1,), jnp.int32),
        ),
        in_specs=[SMEM_SPEC, SMEM_SPEC, SMEM_SPEC, VMEM_SPEC],
        out_specs=(VMEM_SPEC, VMEM_SPEC, SMEM_SPEC, SMEM_SPEC),
        scratch_shapes=[pltpu.VMEM((most, BLOCK), F32)] * (width // BLOCK),
        compiler_params=params(),
        cost_estimate=cost(0, 30e6),
    )(core_word, order_word, lengths, tokens)
    packed, pieces0, pieces2 = lax.optimization_barrier((packed, pieces0, pieces2))
    rows, seg, offsets, tiles = packed
    full = gather_end(gather_in(qkvo, pieces0))
    qk, vo = [(value, swap_core(value)) for value in full]
    ffn = [
        (arrange(pieces, first, 0), [first], orders[side]) for side, pieces in enumerate((pieces1, pieces2))
    ]
    pieces12 = gather_out(ffn)
    ffn = gather_in(ffn, pieces12)
    pieces12 = gather_out(ffn)

    own_order = lax.dynamic_index_in_dim(send_order.reshape(mine, 2), core, 1, keepdims=False)
    own_count = lengths[own_order].astype(F32)[:, None]
    back = jnp.pad(pair_grad / own_count, ((0, BLOCK - mine), (0, 0)))
    back_high = back.astype(BF)
    back_rest = (back - back_high.astype(F32)).astype(BF)
    square_spec = held_spec(width, width)
    long_spec = held_spec(width, 2 * width)
    vec_spec = held_spec(1, vectors.shape[0])
    vec_row = vectors.reshape(1, -1)
    row_total = most * 0.6
    starts = [pieces[0] for pieces in pieces12]
    tiles, starts, _, _ = lax.optimization_barrier((tiles, starts, back_high, back_rest))
    qkv, att, normed, inverse = tiled_call(
        attn_forward_kernel,
        out_shape=(
            shape_of((most, 3 * width), BF),
            shape_of((most, width), BF),
            shape_of((most, width), F32),
            shape_of((most, BLOCK), F32),
        ),
        in_specs=[SMEM_SPEC, tile_spec(width), tile_spec(BLOCK), vec_spec] + [square_spec] * 4,
        out_specs=(tile_spec(3 * width), tile_spec(width), tile_spec(width), tile_spec(BLOCK)),
        scratch_shapes=[],
        cost_estimate=cost(2 * row_total * 4 * width * width * 2, 30e6),
    )(tiles, most, core_word, rows, seg, vec_row, qk[0], vo[0], qk[1], vo[1])
    normed, pieces12 = lax.optimization_barrier((normed, pieces12))

    w1, w2 = [(value, swap_core(value)) for value in gather_end(gather_in(ffn, pieces12))]
    down_shape = shape_of((width, 2 * width + half), BF)
    in_shape = shape_of((width, 2 * width), BF)
    grad_one, emb, vec_ffn, down_own, down_other, in_own, in_other = tiled_call(
        ffn_kernel,
        out_shape=(
            shape_of((most, width), F32),
            shape_of((mine, width), F32),
            shape_of((8, vectors.shape[0]), F32),
            down_shape,
            down_shape,
            in_shape,
            in_shape,
        ),
        in_specs=[
            SMEM_SPEC, tile_spec(width), tile_spec(BLOCK), tile_spec(BLOCK), tile_spec(width), vec_spec,
        ]
        + [held_spec(BLOCK, width)] * 2
        + [long_spec] * 4,
        out_specs=(tile_spec(width), held_spec(mine, width), held_spec(8, vectors.shape[0])) + (HBM_SPEC,) * 4,
        scratch_shapes=[
            pltpu.VMEM((4, width, width), F32),
            pltpu.VMEM((4, width, width), F32),
            pltpu.VMEM((2, width, half), F32),
            pltpu.VMEM((4, TILE, width), BF),
            pltpu.VMEM((4, TILE, width), F32),
            pltpu.VMEM((BLOCK, width), F32),
            pltpu.VMEM((BLOCK, BLOCK), F32),
            pltpu.VMEM((2, width, width), BF),
            pltpu.SemaphoreType.DMA((2,)),
        ],
        cost_estimate=cost(2 * row_total * 24 * width * width, 30e6),
    )(
        tiles, most, core_word, normed, inverse, seg, att, vec_row, back_high, back_rest, *w1, *w2
    )

    def scatter_start(parts):
        sides = []
        for side, (lanes, *arrays) in enumerate(parts):
            terms = [
                (array.reshape(*[size for size, _ in dims], shard_rows, -1), list(dims), lanes)
                for array in arrays
            ]
            sides.append(Side(terms, orders[side][::-1]))
        return sides

    def scatter_out(sides):
        if len({side.order[0][0] for side in sides}) == 1:
            return slab_sums(sides, dims)
        return [slab_sums([side], dims)[0] for side in sides]

    def scatter_go(sides, slabs):
        return [scatter_send(sent, side.order[0]) for side, sent in zip(sides, slabs)]

    def scatter_in(sides, arrived):
        after = []
        for side, come in zip(sides, arrived):
            left = [dim for dim in side.terms[-1][1] if dim != side.order[0]]
            new = [(array, left, slice(0, side.cols())) for array in come]
            after.append(Side(side.terms + new, side.order[1:]))
        return after

    def last_in(own, arrived):
        for slab in arrived:
            own = own + slab.astype(F32)
        return own

    def go_pooled(value):
        return lax.all_to_all(value, "dp", 0, 0, tiled=True)

    come = [swap_core(down_other), swap_core(in_other)]
    pooled = go_pooled(emb.reshape(count, share // 2, width)) if share % 2 == 0 else emb
    ffn_send = scatter_start(
        ((slice(0, 2 * width + half), down_own, come[0]), (slice(0, 2 * width), in_own, come[1]))
    )
    slabs = scatter_out(ffn_send)
    tiles, slabs = lax.optimization_barrier((tiles, slabs))
    dqkv, vec_local = tiled_call(
        attn_backward_kernel,
        out_shape=(
            shape_of((most, 3 * width), BF),
            shape_of((vectors.shape[0] // BLOCK, BLOCK), F32),
        ),
        in_specs=[
            SMEM_SPEC, tile_spec(width), tile_spec(3 * width), tile_spec(BLOCK), held_spec(8, vectors.shape[0]),
        ]
        + [square_spec] * 2,
        out_specs=(tile_spec(3 * width), held_spec(vectors.shape[0] // BLOCK, BLOCK)),
        scratch_shapes=[pltpu.VMEM((8, vectors.shape[0]), F32)],
        cost_estimate=cost(2 * row_total * 8 * width * width * 1.5, 30e6),
    )(tiles, most, core_word, grad_one, qkv, seg, vec_ffn, vo[0], vo[1])
    arrived, dqkv, pooled = lax.optimization_barrier((scatter_go(ffn_send, slabs), dqkv, pooled))
    both = [pooled, swap_core(pooled)]
    ffn_send = scatter_in(ffn_send, arrived)
    slabs = scatter_out(ffn_send)
    tiles, slabs = lax.optimization_barrier((tiles, slabs))
    qkv_shape = shape_of((width, 3 * half), BF)
    dx_mine, dx_other, own, other = tiled_call(
        attn_weight_kernel,
        out_shape=(shape_of((most, half), F32), shape_of((most, half), BF), qkv_shape, qkv_shape),
        in_specs=[SMEM_SPEC, tile_spec(width), tile_spec(width), tile_spec(3 * width)] + [square_spec] * 4,
        out_specs=(tile_spec(half), tile_spec(half)) + (HBM_SPEC,) * 2,
        scratch_shapes=[
            pltpu.VMEM((2, width, 3 * half), F32),
            pltpu.VMEM((TILE, width), F32),
            pltpu.VMEM((2, width, 3 * half), BF),
            pltpu.SemaphoreType.DMA((2,)),
        ],
        cost_estimate=cost(2 * row_total * 8 * width * width * 1.5, 30e6),
    )(tiles, most, core_word, grad_one, rows, dqkv, qk[0], vo[0], qk[1], vo[1])
    arrived, own, other, both = lax.optimization_barrier((scatter_go(ffn_send, slabs), own, other, both))
    both = flip(jnp.stack(both))

    come = swap_core(other)
    cut = 3 * half // (2 * BLOCK) * BLOCK
    qkv_send = scatter_start(
        ((slice(0, cut), own, come), (slice(cut, 3 * half), own, come))
    )
    slabs = scatter_out(qkv_send)
    ffn_send = scatter_in(ffn_send, arrived)
    ffn_grad, *last_slabs = slab_sums(ffn_send, dims, joined=True)
    order_word, slabs, last_slabs = lax.optimization_barrier((send_order, slabs, last_slabs))
    go = scatter_go(qkv_send, slabs)
    last_go = scatter_send(last_slabs, first)

    tokens_grad = pl.pallas_call(
        unpack_kernel,
        out_shape=shape_of((sents, span, half), F32),
        in_specs=[SMEM_SPEC] * 4 + [VMEM_SPEC] * 2,
        out_specs=VMEM_SPEC,
        scratch_shapes=[pltpu.VMEM((most, BLOCK), F32)] * (2 * half // BLOCK),
        compiler_params=params(),
        cost_estimate=cost(0, 20e6),
    )(core_word, order_word, lengths, offsets, dx_mine, swap_core(dx_other))
    go, tokens_grad = lax.optimization_barrier((go, tokens_grad))
    qkv_send = scatter_in(qkv_send, go)
    while qkv_send[0].order:
        go = scatter_go(qkv_send, scatter_out(qkv_send))
        go, last_go = lax.optimization_barrier((go, last_go))
        qkv_send = scatter_in(qkv_send, go)
    ffn_grad = last_in(ffn_grad, last_go)
    qkv_grad, *slabs = slab_sums(qkv_send, dims, joined=True)
    go = scatter_send(slabs, first)

    if share % 2 == 0:
        pooled = jnp.moveaxis(both, 0, 2).reshape(sents, width)
    else:
        both = jnp.moveaxis(both, 0, 1).reshape(sents, width)
        pooled = go_pooled(both)

    go, pooled = lax.optimization_barrier((go, pooled))
    qkv_grad = last_in(qkv_grad, go)
    qkv_grad = jnp.stack([qkv_grad[:, index * half : (index + 1) * half] for index in range(3)])
    ffn_cols = in_weight.shape[1]
    down_grad = ffn_grad[:, :ffn_cols].T
    out_grad = ffn_grad[:, ffn_cols : ffn_cols + half].T
    in_grad = ffn_grad[:, ffn_cols + half :]

    qkv_m, qkv_s, qkv_n = adam_moments(qkv_grad, qkv_moment, qkv_square)
    out_m, out_s, out_n = adam_moments(out_grad, out_moment, out_square)
    in_m, in_s, in_n = adam_moments(in_grad, in_moment, in_square)
    down_m, down_s, down_n = adam_moments(down_grad, down_moment, down_square)
    qkv_u = qkv_n + weight_decay * qkv_weight
    out_u = out_n + weight_decay * out_weight
    in_u = in_n + weight_decay * in_weight
    down_u = down_n + weight_decay * down_weight
    weight_local = matrix_squares(qkv_weight, out_weight, in_weight, down_weight)
    update_local = matrix_squares(qkv_u, out_u, in_u, down_u)
    norms = jnp.pad(jnp.stack([weight_local, update_local]), ((0, 6), (0, BLOCK - 6)))
    totals = sum_all(jnp.concatenate([vec_local, norms]), dims)
    vec_grad = totals[:-8].reshape(-1)
    vec_m, vec_s, vec_n = adam_moments(vec_grad, vec_moment, vec_square)
    weight_norm = jnp.sqrt(totals[-8, :6])
    update_norm = jnp.sqrt(totals[-7, :6])
    trust_ratio = weight_norm / update_norm
    new_qkv = qkv_weight - learn_rate * trust_ratio[:3, None, None] * qkv_u
    new_out = out_weight - learn_rate * trust_ratio[3] * out_u
    new_in = in_weight - learn_rate * trust_ratio[4] * in_u
    new_down = down_weight - learn_rate * trust_ratio[5] * down_u
    new_vec = vectors - vector_rate * vec_n
    return (
        pooled, tokens_grad, qkv_grad, out_grad, in_grad, down_grad, vec_grad,
        trust_ratio, weight_norm, update_norm,
        qkv_m, out_m, in_m, down_m, vec_m,
        qkv_s, out_s, in_s, down_s, vec_s,
        new_qkv, new_out, new_in, new_down, new_vec,
        ema_keep * qkv_average + (1.0 - ema_keep) * new_qkv,
        ema_keep * out_average + (1.0 - ema_keep) * new_out,
        ema_keep * in_average + (1.0 - ema_keep) * new_in,
        ema_keep * down_average + (1.0 - ema_keep) * new_down,
        ema_keep * vec_average + (1.0 - ema_keep) * new_vec,
    )


def solution(mesh):
    matrices = (P(None, "dp", "mp"), P("mp", "dp"), P("dp", "mp"), P("mp", "dp"), P())
    return jax.shard_map(
        shards,
        mesh=mesh,
        in_specs=(P("dp", None, None), P("dp"), P("dp"), P("dp", None)) + matrices * 4,
        out_specs=(P("dp", None), P("dp", None, "mp")) + matrices + (P(), P(), P()) + matrices * 4,
        check_vma=False,
    )
```

```python
import jax
import jax.numpy as jnp
from jax import lax
from jax.experimental import pallas as pl
from jax.experimental.pallas import tpu as pltpu
from jax.sharding import PartitionSpec as P

HEAD = 64
STEP = 10
TILE = 256
BLOCK = 128
GROUP = 6

beta_one = 0.9
beta_two = 0.999
adam_eps = 1e-06
weight_decay = 0.01
learn_rate = 0.3
vector_rate = 0.05
ema_keep = 0.9
norm_eps = 1e-12
masked_score = -1000000000.0
gelu_in = 0.7978845608028654
gelu_cube = 0.044715

BF = jnp.bfloat16
F32 = jnp.float32
VMEM_LIMIT = 62 * 1024 * 1024
SMALL_LIMIT = 14 * 1024 * 1024


def dp_dims(count):
    known = {16: ((4, 4), (2, 2), (2, 1)), 128: ((4, 32), (8, 4), (4, 1))}
    return known.get(count, ((count, 1),))


def dp_shift(value, dim, step):
    size, stride = dim
    count = lax.axis_size("dp")
    pairs = []
    for index in range(count):
        place = index // stride % size
        pairs.append((index, index + ((place + step) % size - place) * stride))
    return lax.ppermute(value, "dp", pairs)


def dp_place(dim):
    size, stride = dim
    return lax.rem(lax.div(lax.axis_index("dp"), stride), size)


def swap_core(value):
    return lax.ppermute(value, "mp", [(0, 1), (1, 0)])


def arrange(pieces, dim, axis):
    size, _ = dim
    place = dp_place(dim)
    if size == 2:
        return jnp.where(place == 0, jnp.stack(pieces, axis), jnp.stack(pieces[::-1], axis))
    ordered = []
    for target in range(size):
        which = lax.rem(target - place + size, size)
        chosen = pieces[0]
        for step in range(1, size):
            chosen = jnp.where(which == step, pieces[step], chosen)
        ordered.append(chosen)
    return jnp.stack(ordered, axis)


def gather_send(value, dim):
    return [value] + [dp_shift(value, dim, -step) for step in range(1, dim[0])]


def scatter_send(slabs, dim):
    return [dp_shift(slab, dim, step) for step, slab in enumerate(slabs, 1)]


def sum_all(value, dims):
    value = value + swap_core(value)
    count = lax.axis_size("dp")
    for size, stride in dims:
        bit = 1
        while bit < size:
            pairs = []
            for index in range(count):
                place = index // stride % size
                pairs.append((index, index + ((place ^ bit) - place) * stride))
            value = value + lax.ppermute(value, "dp", pairs)
            bit *= 2
    return value


def dot_nn(left, right):
    return jnp.dot(left, right, preferred_element_type=F32)


def dot_nt(left, right):
    return lax.dot_general(left, right, (((1,), (1,)), ((), ())), preferred_element_type=F32)


def dot_tn(left, right):
    return lax.dot_general(left, right, (((0,), (0,)), ((), ())), preferred_element_type=F32)


def vec_at(index, width, core=None, part=0, cols=None):
    if core is None:
        return slice(index * width, (index + 1) * width)
    which = core if part == 0 else 1 - core
    return pl.ds(pl.multiple_of(index * width + which * cols, BLOCK), cols)


def column_sums(value):
    rows, cols = value.shape
    return jnp.sum(value.reshape(rows // 8, 8, cols), axis=0)


def pack_kernel(
    core_ref, order_ref, len_ref, tok_ref, rows_ref, seg_ref, off_ref, tiles_ref, *stage
):
    core = core_ref[0]
    half = order_ref.shape[0] // 2
    total = rows_ref.shape[0]

    def clear(step, carry):
        rows = pl.ds(pl.multiple_of(step * BLOCK, BLOCK), BLOCK)
        for column in stage:
            column[rows, :] = jnp.zeros((BLOCK, BLOCK), F32)
        seg_ref[rows, :] = jnp.full((BLOCK, BLOCK), -1.0, F32)
        return carry

    lax.fori_loop(0, total // BLOCK, clear, 0)

    def start_of(cursor, count):
        inside = cursor & (BLOCK - 1)
        return jnp.where(inside + count > BLOCK, cursor - inside + BLOCK, cursor)

    def place(slot, cursor):
        sentence = order_ref[2 * slot + core]
        count = len_ref[sentence]
        start = start_of(cursor, count)
        off_ref[0, slot] = start
        span = tok_ref.shape[1]
        value = tok_ref[sentence].astype(F32)
        for index, column in enumerate(stage):
            column[pl.ds(start, span), :] = value[:, index * BLOCK : (index + 1) * BLOCK]
        row = lax.broadcasted_iota(jnp.int32, (span, BLOCK), 0)
        seg_ref[pl.ds(start, span), :] = jnp.where(row < count, slot.astype(F32), -1.0)
        return start + count

    used = lax.fori_loop(0, half, place, 0)
    tiles_ref[0] = (used + TILE - 1) // TILE

    def partner(slot, cursor):
        count = len_ref[order_ref[2 * slot + 1 - core]]
        start = start_of(cursor, count)
        off_ref[1, slot] = start
        return start + count

    lax.fori_loop(0, half, partner, 0)

    def low(step, carry):
        rows = pl.ds(pl.multiple_of(step * BLOCK, BLOCK), BLOCK)
        for index, column in enumerate(stage):
            rows_ref[rows, index * BLOCK : (index + 1) * BLOCK] = column[rows, :].astype(BF)
        return carry

    lax.fori_loop(0, total // BLOCK, low, 0)


def head_masks():
    lane = lax.broadcasted_iota(jnp.int32, (1, 2 * HEAD), 1)
    first = jnp.where(lane < HEAD, 1.0, 0.0)
    return first.astype(BF), (1.0 - first).astype(BF)


def two_heads(value, masks):
    return jnp.concatenate([value * masks[0], value * masks[1]], axis=0)


def same_sentence(seg):
    across = jnp.transpose(seg)
    return jnp.concatenate([seg, seg], axis=1) == jnp.concatenate([across, across], axis=1)


def softmax_rows(scores, mask):
    scores = jnp.where(mask, scores, masked_score)
    expon = jnp.exp(scores - jnp.max(scores, axis=0, keepdims=True))
    return expon * (1.0 / jnp.sum(expon, axis=0, keepdims=True))


def one_above_other(value):
    return jnp.concatenate([value[:, :BLOCK], value[:, BLOCK:]], axis=0)


def attn_forward_kernel(
    last, core_ref, rows_ref, seg_ref, vec_ref, qk0, vo0, qk1, vo1, qkv_ref, att_ref, norm_ref, inv_ref
):
    width = rows_ref.shape[1]
    half = width // 2
    core = core_ref[0]
    rows = rows_ref[...]
    weights = ((qk0, vo0), (qk1, vo1))
    for part, (qk, vo) in enumerate(weights):
        base = part * 3 * half
        value = dot_nn(rows, qk[...])
        query = value[:, :half] + vec_ref[:, vec_at(0, width, core, part, half)]
        qkv_ref[:, base : base + half] = query.astype(BF)
        qkv_ref[:, base + half : base + width] = value[:, half:].astype(BF)
        value = dot_nn(rows, vo[:, :half]) + vec_ref[:, vec_at(1, width, core, part, half)]
        qkv_ref[:, base + width : base + 3 * half] = value.astype(BF)
    masks = head_masks()
    for block in range(TILE // BLOCK):
        span = slice(block * BLOCK, (block + 1) * BLOCK)
        mask = same_sentence(seg_ref[span, :])
        for part in range(2):
            for pair in range(half // (2 * HEAD)):
                at = part * 3 * half + pair * 2 * HEAD
                query = qkv_ref[span, at : at + 2 * HEAD] * BF(HEAD**-0.5)
                key = qkv_ref[span, at + half : at + half + 2 * HEAD]
                value = qkv_ref[span, at + width : at + width + 2 * HEAD]
                probs = softmax_rows(dot_nt(key, two_heads(query, masks)), mask).astype(BF)
                mixed = dot_tn(one_above_other(probs), two_heads(value, masks))
                to = part * half + pair * 2 * HEAD
                att_ref[span, to : to + 2 * HEAD] = mixed.astype(BF)
    mixed = dot_nt(att_ref[:, :half], vo0[:, half:]) + dot_nt(att_ref[:, half:], vo1[:, half:])
    pre = rows.astype(F32) + (mixed + vec_ref[:, vec_at(2, width)])
    centre = pre - jnp.mean(pre, axis=-1, keepdims=True)
    inverse = lax.rsqrt(jnp.mean(centre * centre, axis=-1, keepdims=True) + norm_eps)
    norm_ref[...] = centre * inverse
    inv_ref[...] = jnp.broadcast_to(inverse, inv_ref.shape)


def norm_back(grad, normed, inverse, gain):
    scaled = grad * gain
    first = jnp.mean(scaled, axis=-1, keepdims=True)
    second = jnp.mean(scaled * normed, axis=-1, keepdims=True)
    return (scaled - first - normed * second) * inverse


def hidden_pieces(core, width):
    return [
        pl.ds(
            pl.multiple_of(8 * width + (2 * (core if part < 2 else 1 - core) + part % 2) * width, BLOCK),
            width,
        )
        for part in range(4)
    ]


def ffn_kernel(
    last, core_ref, norm_ref, inv_ref, seg_ref, att_ref, vec_ref, high_ref, rest_ref,
    w1_own, w1_other, w2_own, w2_other,
    grad_ref, emb_ref, sums_ref, down_own, down_other, in_own, in_other,
    sum1, sum2, sum3, act, slope, emb, counts, stage, sems,
):
    step = pl.program_id(0)
    width = norm_ref.shape[1]
    half = width // 2
    lanes = [slice(part % 2 * width, (part % 2 + 1) * width) for part in range(4)]
    w1 = [(w1_own, w1_other)[part // 2].at[:, lanes[part]] for part in range(4)]
    w2 = [(w2_own, w2_other)[part // 2].at[:, lanes[part]] for part in range(4)]
    hidden_at = hidden_pieces(core_ref[0], width)

    @pl.when(step == 0)
    def _():
        emb[...] = jnp.zeros_like(emb)
        counts[...] = jnp.zeros_like(counts)
        sums_ref[...] = jnp.zeros_like(sums_ref)
        sum1[...] = jnp.zeros_like(sum1)
        sum2[...] = jnp.zeros_like(sum2)
        sum3[...] = jnp.zeros_like(sum3)

    gain_one, shift_one = vec_ref[:, vec_at(4, width)], vec_ref[:, vec_at(5, width)]
    gain_two, shift_two = vec_ref[:, vec_at(6, width)], vec_ref[:, vec_at(7, width)]
    bias_ffn = vec_ref[:, vec_at(3, width)]
    hidden_low = (norm_ref[...] * gain_one + shift_one).astype(BF)
    for part in range(4):
        pre = dot_nn(hidden_low, w1[part][...]) + vec_ref[:, hidden_at[part]]
        square = pre * pre
        tanh = jnp.tanh(pre * (gelu_in + gelu_in * gelu_cube * square))
        gate = 0.5 + 0.5 * tanh
        out = pre * gate
        act[part] = out.astype(BF)
        slope[part] = gate + out * (1.0 - tanh) * (gelu_in + 3.0 * gelu_in * gelu_cube * square)
    total = dot_nt(act[0], w2[0][...])
    for part in range(1, 4):
        total = total + dot_nt(act[part], w2[part][...])
    pre = (norm_ref[...] * gain_one + shift_one) + (total + bias_ffn)
    centre = pre - jnp.mean(pre, axis=-1, keepdims=True)
    inverse = lax.rsqrt(jnp.mean(centre * centre, axis=-1, keepdims=True) + norm_eps)
    normed = centre * inverse
    final = normed * gain_two + shift_two
    final_high = final.astype(BF)
    final_rest = (final - final_high.astype(F32)).astype(BF)
    seg = seg_ref[...]
    lane = lax.broadcasted_iota(jnp.int32, seg.shape, 1).astype(F32)
    pick = jnp.where(seg == lane, 1.0, 0.0)
    pick_across = jnp.transpose(pick).astype(BF)
    pick = pick.astype(BF)
    emb[...] += dot_nn(pick_across, final_high) + dot_nn(pick_across, final_rest)
    counts[...] += dot_nn(pick_across, jnp.ones((TILE, BLOCK), BF))
    back = dot_nn(pick, high_ref[...]) + dot_nn(pick, rest_ref[...])
    sums_ref[:, vec_at(6, width)] += column_sums(back * normed)
    sums_ref[:, vec_at(7, width)] += column_sums(back)
    grad_two = norm_back(back, normed, inverse, gain_two)
    ffn_low = grad_two.astype(BF)
    sums_ref[:, vec_at(3, width)] += column_sums(ffn_low.astype(F32))
    grad_hidden = grad_two
    for part in range(4):
        grad_act = dot_nn(ffn_low, w2[part][...])
        grad_pre = (grad_act * slope[part]).astype(BF)
        sums_ref[:, hidden_at[part]] += column_sums(grad_pre.astype(F32))
        grad_hidden = grad_hidden + dot_nt(grad_pre, w1[part][...])
        sum1[part] += dot_tn(hidden_low, grad_pre)
        sum2[part] += dot_tn(ffn_low, act[part])
    normed_one = norm_ref[...]
    sums_ref[:, vec_at(4, width)] += column_sums(grad_hidden * normed_one)
    sums_ref[:, vec_at(5, width)] += column_sums(grad_hidden)
    grad_one = norm_back(grad_hidden, normed_one, inv_ref[:, :1], gain_one)
    grad_ref[...] = grad_one
    grad_low = grad_one.astype(BF)
    for part in range(2):
        sum3[part] += dot_tn(grad_low, att_ref[:, part * half : (part + 1) * half])
    sums_ref[:, vec_at(2, width)] += column_sums(grad_low.astype(F32))

    @pl.when(last)
    def _():
        places = []
        for outs, sums in (((down_own, down_other), sum2), ((in_own, in_other), sum1)):
            for index in (2, 3, 0, 1):
                target = outs[index // 2].at[:, pl.ds(index % 2 * width, width)]
                places.append((sums.at[index], target))
            if sums is sum2:
                for index in (1, 0):
                    places.append((sum3.at[index], outs[index].at[:, pl.ds(2 * width, half)]))
        store_sums(places, stage, sems)
        held = emb_ref.shape[0]
        number = jnp.maximum(counts[:held], 1.0)
        emb_ref[...] = emb[:held] / jnp.concatenate([number] * (width // BLOCK), axis=1)


def attn_backward_kernel(
    last, core_ref, grad_ref, rows_ref, qkv_ref, seg_ref, before_ref, qk0, vo0, qk1, vo1,
    mine_ref, dx_ref, total_ref, own, other, dqkv_ref, dx, sums, weights, stage, sems,
):
    width = grad_ref.shape[1]
    half = width // 2
    core = core_ref[0]

    @pl.when(pl.program_id(0) == 0)
    def _():
        sums[...] = before_ref[...]
        weights[...] = jnp.zeros_like(weights)

    grad_low = grad_ref[...].astype(BF)
    masks = head_masks()
    mask = [same_sentence(seg_ref[b * BLOCK : (b + 1) * BLOCK, :]) for b in range(TILE // BLOCK)]
    for part, vo in enumerate((vo0, vo1)):
        base = part * 3 * half
        grad_att = dot_nn(grad_low, vo[:, half:]).astype(BF)
        units = [(block, pair) for block in range(TILE // BLOCK) for pair in range(half // (2 * HEAD))]
        for start in range(0, len(units), GROUP):
            group = units[start : start + GROUP]
            spans = [slice(block * BLOCK, (block + 1) * BLOCK) for block, _ in group]
            ats = [pair * 2 * HEAD for _, pair in group]
            query_at = [slice(base + at, base + at + 2 * HEAD) for at in ats]
            key_at = [slice(base + half + at, base + half + at + 2 * HEAD) for at in ats]
            value_at = [slice(base + width + at, base + width + at + 2 * HEAD) for at in ats]
            each = range(len(group))
            query_two = [
                two_heads(qkv_ref[spans[i], query_at[i]] * BF(HEAD**-0.5), masks) for i in each
            ]
            att_two = [two_heads(grad_att[spans[i], ats[i] : ats[i] + 2 * HEAD], masks) for i in each]
            scores = [dot_nt(qkv_ref[spans[i], key_at[i]], query_two[i]) for i in each]
            grad_probs = [dot_nt(qkv_ref[spans[i], value_at[i]], att_two[i]) for i in each]
            probs = [softmax_rows(scores[i], mask[group[i][0]]) for i in each]
            for i in each:
                dqkv_ref[spans[i], value_at[i]] = dot_nn(probs[i].astype(BF), att_two[i]).astype(BF)
            inner = [jnp.sum(grad_probs[i] * probs[i], axis=0, keepdims=True) for i in each]
            grad_scores = [(probs[i] * (grad_probs[i] - inner[i])).astype(BF) for i in each]
            for i in each:
                dqkv_ref[spans[i], key_at[i]] = dot_nn(grad_scores[i], query_two[i]).astype(BF)
            for i in each:
                key_two = two_heads(qkv_ref[spans[i], key_at[i]], masks)
                grad_query = dot_tn(one_above_other(grad_scores[i]), key_two) * HEAD**-0.5
                dqkv_ref[spans[i], query_at[i]] = grad_query.astype(BF)
        sums[:, vec_at(0, width, core, part, half)] += column_sums(
            dqkv_ref[:, base : base + half].astype(F32)
        )
        sums[:, vec_at(1, width, core, part, half)] += column_sums(
            dqkv_ref[:, base + width : base + 3 * half].astype(F32)
        )

    rows = rows_ref[...]
    total = grad_ref[...]
    for part, (qk, vo) in enumerate(((qk0, vo0), (qk1, vo1))):
        base = part * 3 * half
        total = total + dot_nt(dqkv_ref[:, base : base + width], qk[...])
        total = total + dot_nt(dqkv_ref[:, base + width : base + 3 * half], vo[:, :half])
    dx[...] = total
    mine_ref[...] = dx[:, pl.ds(pl.multiple_of(core * half, half), half)]
    dx_ref[...] = dx[:, pl.ds(pl.multiple_of((1 - core) * half, half), half)].astype(BF)
    for part in range(2):
        weights[part] += dot_tn(rows, dqkv_ref[:, part * 3 * half : (part + 1) * 3 * half])

    @pl.when(last)
    def _():
        store_sums([(weights.at[1], other), (weights.at[0], own)], stage, sems)
        for row in range(total_ref.shape[0]):
            lanes = sums[:, row * BLOCK : (row + 1) * BLOCK]
            total_ref[row : row + 1, :] = jnp.sum(lanes, axis=0, keepdims=True)


def store_sums(places, stage, sems):
    copies = []
    for index, (source, target) in enumerate(places):
        slot = index % 2
        if index >= 2:
            copies[index - 2].wait()
        cols = source.shape[-1]
        stage[slot, :, :cols] = source[...].astype(BF)
        copies.append(pltpu.make_async_copy(stage.at[slot, :, pl.ds(0, cols)], target, sems.at[slot]))
        copies[index].start()
    copies[-2].wait()
    copies[-1].wait()


def unpack_kernel(core_ref, order_ref, len_ref, off_ref, mine_ref, recv_ref, out_ref, *columns):
    core = core_ref[0]
    half = order_ref.shape[0] // 2
    span, cols = out_ref.shape[1], out_ref.shape[2]
    each = cols // BLOCK

    def spread(step, carry):
        rows = pl.ds(pl.multiple_of(step * BLOCK, BLOCK), BLOCK)
        for index in range(each):
            lanes = slice(index * BLOCK, (index + 1) * BLOCK)
            columns[index][rows, :] = mine_ref[rows, lanes]
            columns[each + index][rows, :] = recv_ref[rows, lanes].astype(F32)
        return carry

    lax.fori_loop(0, recv_ref.shape[0] // BLOCK, spread, 0)
    row = lax.broadcasted_iota(jnp.int32, (span, BLOCK), 0)

    def place(slot, carry):
        for which in range(2):
            parity = core if which == 0 else 1 - core
            sentence = order_ref[2 * slot + parity]
            count = len_ref[sentence]
            start = off_ref[which, slot]
            for index in range(each):
                value = columns[which * each + index][pl.ds(start, span), :]
                out_ref[sentence, :, index * BLOCK : (index + 1) * BLOCK] = jnp.where(
                    row < count, value, 0.0
                )
        return carry

    lax.fori_loop(0, half, place, 0)


SMEM_SPEC = pl.BlockSpec(memory_space=pltpu.SMEM)
VMEM_SPEC = pl.BlockSpec(memory_space=pltpu.VMEM)
HBM_SPEC = pl.BlockSpec(memory_space=pl.ANY)


def params(limit=VMEM_LIMIT):
    return pltpu.CompilerParams(vmem_limit_bytes=limit)


def tile_spec(cols):
    return pl.BlockSpec((TILE, cols), lambda step, tiles: (jnp.minimum(step, tiles[0] - 1), 0))


def held_spec(*shape):
    return pl.BlockSpec(
        shape, lambda step, tiles: (0,) * len(shape), pipeline_mode=pl.Buffered(1)
    )


def column_spec(width, column):
    return pl.BlockSpec((width, width), lambda step, tiles: (0, column), pipeline_mode=pl.Buffered(1))


def tiled_call(kernel, out_shape, in_specs, out_specs, scratch_shapes, cost_estimate):
    def body(tiles_ref, *refs):
        @pl.when(pl.program_id(0) < tiles_ref[0])
        def _():
            kernel(pl.program_id(0) == tiles_ref[0] - 1, *refs)

    def call(tiles, most, *operands):
        return pl.pallas_call(
            body,
            grid_spec=pltpu.PrefetchScalarGridSpec(
                num_scalar_prefetch=1,
                grid=(most // TILE,),
                in_specs=in_specs,
                out_specs=out_specs,
                scratch_shapes=scratch_shapes,
            ),
            out_shape=out_shape,
            compiler_params=params(),
            cost_estimate=cost_estimate,
        )(tiles, *operands)

    return call


def shape_of(shape, dtype):
    return jax.ShapeDtypeStruct(shape, dtype)


def cost(flops, read):
    return pl.CostEstimate(flops=int(flops), bytes_accessed=int(read), transcendentals=0)


class Side:
    def __init__(self, terms, order):
        self.terms, self.order = terms, order

    def cols(self):
        _, _, lanes = self.terms[0]
        return lanes.stop - lanes.start


def slab_sums(sides, dims, joined=False, limit=SMALL_LIMIT):
    first = dims[0]
    places = jnp.stack([dp_place(dim) for dim in dims]).astype(jnp.int32)
    at_of = {dim: index for index, dim in enumerate(dims)}
    nexts = [first if joined else side.order[0] for side in sides]
    lead = 1 if joined else first[0]
    operands, in_specs, plan = [], [], []
    out_shape, out_specs, targets = [], [], []

    def index_map(term_dims, current, step, size, fixed):
        def of(grid, at):
            index = []
            for dim in term_dims:
                if dim == current:
                    index.append(lax.rem(at[at_of[dim]] + step, size))
                elif dim == first:
                    index.append(grid)
                else:
                    index.append(at[at_of[dim]] if dim in fixed else 0)
            return (*index, 0, 0)

        return of

    for number, (side, current) in enumerate(zip(sides, nexts)):
        size = current[0]
        rows = side.terms[0][0].shape[-2]
        left = [dim for dim in side.terms[-1][1] if dim != current]
        fixed = [dim for dim in dims if dim != current and dim not in left]
        steps = range(size) if joined else range(1, size)
        for step in steps:
            ids = []
            for array, term_dims, lanes in side.terms:
                block, pick = [], []
                for dim in term_dims:
                    whole = dim in left and dim != first
                    block.append(dim[0] if whole else 1)
                    pick.append(slice(None) if whole else 0)
                ids.append((len(operands), tuple(pick), lanes))
                operands.append(array)
                in_specs.append(
                    pl.BlockSpec((*block, rows, array.shape[-1]), index_map(term_dims, current, step, size, fixed))
                )
            plan.append((ids, number, step))
        if not joined:
            rest = [dim[0] for dim in left if dim != first]
            for step in steps:
                shape = (lead, *rest, rows, side.cols())
                out_shape.append(shape_of(shape, BF))
                out_specs.append(pl.BlockSpec((1, *shape[1:]), lambda grid, at, n=len(shape): (grid,) + (0,) * (n - 1)))
                targets.append((number, step))
    if joined:
        width = sum(side.cols() for side in sides)
        rows = sides[0].terms[0][0].shape[-2]
        for step in range(first[0]):
            out_shape.append(shape_of((rows, width), BF if step else F32))
            out_specs.append(pl.BlockSpec((rows, width), lambda grid, at: (0, 0)))
            targets.append((None, step))
    starts = [sum(side.cols() for side in sides[:number]) for number in range(len(sides))]

    def kernel(places_ref, *refs):
        ins, outs = refs[: len(operands)], refs[len(operands) :]
        for ids, number, step in plan:
            total = None
            for index, pick, lanes in ids:
                value = ins[index][(*pick, slice(None), lanes)].astype(F32)
                total = value if total is None else total + value
            if joined:
                out = outs[targets.index((None, step))]
                out[:, starts[number] : starts[number] + sides[number].cols()] = total.astype(out.dtype)
            else:
                out = outs[targets.index((number, step))]
                out[0] = total.astype(BF)

    sums = pl.pallas_call(
        kernel,
        grid_spec=pltpu.PrefetchScalarGridSpec(
            num_scalar_prefetch=1, grid=(lead,), in_specs=in_specs, out_specs=out_specs
        ),
        out_shape=out_shape,
        compiler_params=params(limit),
        cost_estimate=cost(0, 8e6),
    )(places, *operands)
    if joined:
        return sums
    return [[value for value, (which, _) in zip(sums, targets) if which == number] for number in range(len(sides))]


def adam_moments(grad_value, moment, square):
    moment_new = beta_one * moment + (1.0 - beta_one) * grad_value
    square_new = beta_two * square + (1.0 - beta_two) * grad_value * grad_value
    scaled = (
        moment_new
        / (1.0 - beta_one**STEP)
        / (jnp.sqrt(square_new / (1.0 - beta_two**STEP)) + adam_eps)
    )
    return (moment_new, square_new, scaled)


def square_sum(value):
    return jnp.sum(jnp.sum(value * value, axis=0, keepdims=True), axis=1, keepdims=True)


def note_norms(norms, matrix, weight, update):
    row = lax.broadcasted_iota(jnp.int32, norms.shape, 0)
    lane = lax.broadcasted_iota(jnp.int32, norms.shape, 1)
    here = jnp.where(row == 0, square_sum(weight), square_sum(update))
    return norms + jnp.where(jnp.logical_and(row < 2, lane == matrix), here, 0.0)


def ffn_update_kernel(own_ref, *refs):
    states, arrived, outs = refs[:9], refs[9:-13], refs[-13:]
    total = own_ref[...]
    for ref in arrived:
        total = total + ref[...].astype(F32)
    norms = jnp.zeros(outs[12].shape, F32)
    down = states[6].shape[1]
    out = states[0].shape[1]
    lanes = (slice(down, down + out), slice(down + out, total.shape[1]), slice(0, down))
    for index in range(3):
        weight, moment, square = states[3 * index : 3 * index + 3]
        grad = total[:, lanes[index]]
        moment_new, square_new, scaled = adam_moments(grad, moment[...], square[...])
        update = scaled + weight_decay * weight[...]
        for target, value in zip(outs[4 * index :], (grad, moment_new, square_new, update)):
            target[...] = value
        norms = note_norms(norms, 3 + index, weight[...], update)
    outs[12][...] = norms


def qkv_update_kernel(
    own_ref, weight_ref, moment_ref, square_ref, vec_ref, norms_ref, *refs
):
    arrived, (grad_out, moment_out, square_out, update_out, totals_ref) = refs[:-5], refs[-5:]
    cols = weight_ref.shape[2]
    total = own_ref[...]
    for ref in arrived:
        total = total + ref[...].astype(F32)
    rows = vec_ref.shape[0]
    norms = norms_ref[...]
    for index in range(3):
        grad = total[:, index * cols : (index + 1) * cols]
        moment, square, scaled = adam_moments(grad, moment_ref[index], square_ref[index])
        update = scaled + weight_decay * weight_ref[index]
        grad_out[index] = grad
        moment_out[index] = moment
        square_out[index] = square
        update_out[index] = update
        norms = note_norms(norms, index, weight_ref[index], update)
    totals_ref[:rows, :] = vec_ref[...]
    totals_ref[rows:, :] = norms


def finish_kernel(totals_ref, *refs):
    ins, outs = refs[:16], refs[16:]
    rows = totals_ref.shape[0] - 8
    weight_norm = jnp.sqrt(totals_ref[rows : rows + 1, :])
    update_norm = jnp.sqrt(totals_ref[rows + 1 : rows + 2, :])
    trust = weight_norm / update_norm
    lane = lax.broadcasted_iota(jnp.int32, trust.shape, 1)
    outs[12][0:1, :] = trust
    outs[12][1:2, :] = weight_norm
    outs[12][2:3, :] = update_norm

    def step(matrix):
        return learn_rate * jnp.sum(jnp.where(lane == matrix, trust, 0.0), axis=1, keepdims=True)

    for index in range(4):
        update, weight, average = ins[3 * index : 3 * index + 3]
        for piece in range(3 if index == 0 else 1):
            at = (piece,) if index == 0 else (Ellipsis,)
            new = weight[at] - step(piece if index == 0 else index + 2) * update[at]
            outs[2 * index][at] = new
            outs[2 * index + 1][at] = ema_keep * average[at] + (1.0 - ema_keep) * new
    vectors, moment, square, average = ins[12:16]
    grad = totals_ref[:rows, :]
    moment_new, square_new, scaled = adam_moments(grad, moment[...], square[...])
    new = vectors[...] - vector_rate * scaled
    outs[8][...] = moment_new
    outs[9][...] = square_new
    outs[10][...] = new
    outs[11][...] = ema_keep * average[...] + (1.0 - ema_keep) * new


def shards(
    tokens, lengths, send_order, pooled_grad,
    qkv_weight, out_weight, in_weight, down_weight, vectors,
    qkv_moment, out_moment, in_moment, down_moment, vec_moment,
    qkv_square, out_square, in_square, down_square, vec_square,
    qkv_average, out_average, in_average, down_average, vec_average,
):
    core = lax.axis_index("mp")
    count = lax.axis_size("dp")
    dims = dp_dims(count)
    sents, span, width = tokens.shape
    half = width // 2
    mine = sents // 2
    most = mine * span
    shard_rows = qkv_weight.shape[1]
    core_word = core.reshape(1).astype(jnp.int32)

    def flip(value):
        return jnp.where(core == 0, value, value[::-1])

    chunk = jnp.concatenate([qkv_weight[0], qkv_weight[1], qkv_weight[2], out_weight.T], axis=1)
    down_t = down_weight.T.astype(BF)
    first, others = dims[0], dims[1:]
    orders = (others, others[::-1])
    sides = (0, 1)

    def gather_start(pieces):
        value = arrange(pieces, first, 0)
        cols = value.shape[-1] // 2
        return [
            (value[..., side * cols : (side + 1) * cols], [first], orders[side]) for side in sides
        ]

    def gather_out(state):
        return [gather_send(value, order[0]) if order else [value] for value, _, order in state]

    def gather_in(state, pieces):
        after = []
        for (value, done, order), come in zip(state, pieces):
            if order:
                axis = sum(1 for other in done if other[1] > order[0][1])
                value = arrange(come, order[0], axis)
                done = done + [order[0]]
            after.append((value, done, order[1:]))
        return after

    def gather_end(state):
        return [value.reshape(width, -1) for value, _, _ in state]

    share = sents // count
    if share % 2 == 0:
        own = lax.dynamic_index_in_dim(
            pooled_grad.reshape(count, share // 2, 2, width), core, 2, keepdims=False
        )
        pair_grad = lax.all_to_all(own, "dp", 0, 0, tiled=True).reshape(mine, width)
    else:
        own = lax.all_to_all(pooled_grad, "dp", 0, 0, tiled=True)
        pair_grad = lax.dynamic_index_in_dim(
            own.reshape(mine, 2, width), core, 1, keepdims=False
        )

    pieces0 = gather_send(chunk.astype(BF), first)
    qkvo = gather_start(pieces0)
    pieces0 = gather_out(qkvo)
    own, held = lax.optimization_barrier((in_weight.astype(BF), [pieces[0] for pieces in pieces0]))
    pieces1 = gather_send(own, first)
    pieces0, pieces1, pair_grad = lax.optimization_barrier((pieces0, pieces1, pair_grad))
    qkvo = gather_in(qkvo, pieces0)
    pieces0 = gather_out(qkvo)
    held = [pieces[0] for pieces in pieces0]
    own, held = lax.optimization_barrier((down_t, held))
    pieces2 = gather_send(own, first)

    order_word, _ = lax.optimization_barrier((send_order, [pieces[0] for pieces in pieces0]))
    packed = pl.pallas_call(
        pack_kernel,
        out_shape=(
            shape_of((most, width), BF),
            shape_of((most, BLOCK), F32),
            shape_of((2, mine), jnp.int32),
            shape_of((1,), jnp.int32),
        ),
        in_specs=[SMEM_SPEC, SMEM_SPEC, SMEM_SPEC, VMEM_SPEC],
        out_specs=(VMEM_SPEC, VMEM_SPEC, SMEM_SPEC, SMEM_SPEC),
        scratch_shapes=[pltpu.VMEM((most, BLOCK), F32)] * (width // BLOCK),
        compiler_params=params(),
        cost_estimate=cost(0, 30e6),
    )(core_word, order_word, lengths, tokens)
    packed, pieces0, pieces2 = lax.optimization_barrier((packed, pieces0, pieces2))
    rows, seg, offsets, tiles = packed
    full = jnp.concatenate(gather_end(gather_in(qkvo, pieces0)), axis=1)
    full = (full, swap_core(full))
    weights = (full[0], full[0], full[1], full[1])
    ffn = [
        (arrange(pieces, first, 0), [first], orders[side]) for side, pieces in enumerate((pieces1, pieces2))
    ]
    ffn = gather_in(ffn, gather_out(ffn))
    ffn_pieces = gather_out(ffn)

    own_order = lax.dynamic_index_in_dim(send_order.reshape(mine, 2), core, 1, keepdims=False)
    own_count = lengths[own_order].astype(F32)[:, None]
    back = jnp.pad(pair_grad / own_count, ((0, BLOCK - mine), (0, 0)))
    back_high = back.astype(BF)
    back_rest = (back - back_high.astype(F32)).astype(BF)
    weight_specs = [column_spec(width, 0), column_spec(width, 1)] * 2
    long_spec = held_spec(width, 2 * width)
    vec_spec = held_spec(1, vectors.shape[0])
    vec_row = vectors.reshape(1, -1)
    row_total = most * 0.6
    mids = [pieces[0] for pieces in ffn_pieces]
    tiles, mids, _, _ = lax.optimization_barrier((tiles, mids, back_high, back_rest))
    qkv, att, normed, inverse = tiled_call(
        attn_forward_kernel,
        out_shape=(
            shape_of((most, 3 * width), BF),
            shape_of((most, width), BF),
            shape_of((most, width), F32),
            shape_of((most, BLOCK), F32),
        ),
        in_specs=[SMEM_SPEC, tile_spec(width), tile_spec(BLOCK), vec_spec] + weight_specs,
        out_specs=(tile_spec(3 * width), tile_spec(width), tile_spec(width), tile_spec(BLOCK)),
        scratch_shapes=[],
        cost_estimate=cost(2 * row_total * 4 * width * width * 2, 30e6),
    )(tiles, most, core_word, rows, seg, vec_row, *weights)
    normed, ffn_pieces = lax.optimization_barrier((normed, ffn_pieces))

    w1, w2 = [(value, swap_core(value)) for value in gather_end(gather_in(ffn, ffn_pieces))]
    down_shape = shape_of((width, 2 * width + half), BF)
    in_shape = shape_of((width, 2 * width), BF)
    grad_one, emb, vec_ffn, down_own, down_other, in_own, in_other = tiled_call(
        ffn_kernel,
        out_shape=(
            shape_of((most, width), F32),
            shape_of((mine, width), F32),
            shape_of((8, vectors.shape[0]), F32),
            down_shape,
            down_shape,
            in_shape,
            in_shape,
        ),
        in_specs=[
            SMEM_SPEC, tile_spec(width), tile_spec(BLOCK), tile_spec(BLOCK), tile_spec(width), vec_spec,
        ]
        + [held_spec(BLOCK, width)] * 2
        + [long_spec] * 4,
        out_specs=(tile_spec(width), held_spec(mine, width), held_spec(8, vectors.shape[0])) + (HBM_SPEC,) * 4,
        scratch_shapes=[
            pltpu.VMEM((4, width, width), F32),
            pltpu.VMEM((4, width, width), F32),
            pltpu.VMEM((2, width, half), F32),
            pltpu.VMEM((4, TILE, width), BF),
            pltpu.VMEM((4, TILE, width), F32),
            pltpu.VMEM((BLOCK, width), F32),
            pltpu.VMEM((BLOCK, BLOCK), F32),
            pltpu.VMEM((2, width, width), BF),
            pltpu.SemaphoreType.DMA((2,)),
        ],
        cost_estimate=cost(2 * row_total * 24 * width * width, 30e6),
    )(
        tiles, most, core_word, normed, inverse, seg, att, vec_row, back_high, back_rest, *w1, *w2
    )

    def scatter_start(parts):
        sides = []
        for side, (lanes, *arrays) in enumerate(parts):
            terms = [
                (array.reshape(*[size for size, _ in dims], shard_rows, -1), list(dims), lanes)
                for array in arrays
            ]
            sides.append(Side(terms, orders[side][::-1]))
        return sides

    def scatter_out(sides, limit=SMALL_LIMIT):
        if len({side.order[0][0] for side in sides}) == 1:
            return slab_sums(sides, dims, limit=limit)
        return [slab_sums([side], dims, limit=limit)[0] for side in sides]

    def scatter_go(sides, slabs):
        return [scatter_send(sent, side.order[0]) for side, sent in zip(sides, slabs)]

    def scatter_in(sides, arrived):
        after = []
        for side, come in zip(sides, arrived):
            left = [dim for dim in side.terms[-1][1] if dim != side.order[0]]
            new = [(array, left, slice(0, side.cols())) for array in come]
            after.append(Side(side.terms + new, side.order[1:]))
        return after

    def go_pooled(value):
        return lax.all_to_all(value, "dp", 0, 0, tiled=True)

    come = [swap_core(down_other), swap_core(in_other)]
    grad_send = scatter_start(
        ((slice(0, 2 * width + half), down_own, come[0]), (slice(0, 2 * width), in_own, come[1]))
    )
    slabs = scatter_out(grad_send, VMEM_LIMIT)
    pooled = go_pooled(emb.reshape(count, share // 2, width)) if share % 2 == 0 else emb
    tiles, slabs, pooled = lax.optimization_barrier((tiles, slabs, pooled))
    qkv_shape = shape_of((width, 3 * half), BF)
    dx_mine, dx_other, vec_local, own, other = tiled_call(
        attn_backward_kernel,
        out_shape=(
            shape_of((most, half), F32),
            shape_of((most, half), BF),
            shape_of((vectors.shape[0] // BLOCK, BLOCK), F32),
            qkv_shape,
            qkv_shape,
        ),
        in_specs=[
            SMEM_SPEC, tile_spec(width), tile_spec(width), tile_spec(3 * width), tile_spec(BLOCK),
            held_spec(8, vectors.shape[0]),
        ]
        + weight_specs,
        out_specs=(tile_spec(half), tile_spec(half), held_spec(vectors.shape[0] // BLOCK, BLOCK))
        + (HBM_SPEC,) * 2,
        scratch_shapes=[
            pltpu.VMEM((TILE, 3 * width), BF),
            pltpu.VMEM((TILE, width), F32),
            pltpu.VMEM((8, vectors.shape[0]), F32),
            pltpu.VMEM((2, width, 3 * half), F32),
            pltpu.VMEM((2, width, 3 * half), BF),
            pltpu.SemaphoreType.DMA((2,)),
        ],
        cost_estimate=cost(2 * row_total * 18 * width * width, 30e6),
    )(tiles, most, core_word, grad_one, rows, qkv, seg, vec_ffn, *weights)
    arrived, own, other, dx_other = lax.optimization_barrier(
        (scatter_go(grad_send, slabs), own, other, dx_other)
    )
    grad_send = scatter_in(grad_send, arrived)
    slabs = scatter_out(grad_send, VMEM_LIMIT)
    come = swap_core(other)
    own, come, slabs = lax.optimization_barrier((own, come, slabs))
    cut = 3 * half // (2 * BLOCK) * BLOCK
    qkv_send = scatter_start(((slice(0, cut), own, come), (slice(cut, 3 * half), own, come)))
    qkv_slabs = scatter_out(qkv_send)
    order_word, slabs = lax.optimization_barrier((send_order, slabs))

    tokens_grad = pl.pallas_call(
        unpack_kernel,
        out_shape=shape_of((sents, span, half), F32),
        in_specs=[SMEM_SPEC] * 4 + [VMEM_SPEC] * 2,
        out_specs=VMEM_SPEC,
        scratch_shapes=[pltpu.VMEM((most, BLOCK), F32)] * (2 * half // BLOCK),
        compiler_params=params(),
        cost_estimate=cost(0, 20e6),
    )(core_word, order_word, lengths, offsets, dx_mine, swap_core(dx_other))
    arrived, tokens_grad, qkv_slabs = lax.optimization_barrier(
        (scatter_go(grad_send, slabs), tokens_grad, qkv_slabs)
    )
    grad_send = scatter_in(grad_send, arrived)
    ffn_grad, *slabs = slab_sums(grad_send, dims, joined=True, limit=VMEM_LIMIT)
    qkv_slabs, slabs = lax.optimization_barrier((qkv_slabs, slabs))
    last_go = scatter_send(slabs, first)
    go = scatter_go(qkv_send, qkv_slabs)
    qkv_send = scatter_in(qkv_send, go)
    while qkv_send[0].order:
        go = scatter_go(qkv_send, scatter_out(qkv_send))
        go, last_go, pooled = lax.optimization_barrier((go, last_go, pooled))
        qkv_send = scatter_in(qkv_send, go)
    qkv_grad, *slabs = slab_sums(qkv_send, dims, joined=True)
    go = scatter_send(slabs, first)

    both = flip(jnp.stack([pooled, swap_core(pooled)]))
    if share % 2 == 0:
        pooled = jnp.moveaxis(both, 0, 2).reshape(sents, width)
    else:
        both = jnp.moveaxis(both, 0, 1).reshape(sents, width)
        pooled = go_pooled(both)

    go, pooled = lax.optimization_barrier((go, pooled))
    ffn_states = [
        (out_weight.T, out_moment.T, out_square.T),
        (in_weight, in_moment, in_square),
        (down_weight.T, down_moment.T, down_square.T),
    ]
    shapes = [shape_of(state[0].shape, F32) for state in ffn_states for _ in range(4)]
    *ffn_new, norms = pl.pallas_call(
        ffn_update_kernel,
        out_shape=shapes + [shape_of((8, BLOCK), F32)],
        in_specs=[VMEM_SPEC] * (10 + len(last_go)),
        out_specs=[VMEM_SPEC] * 13,
        compiler_params=params(SMALL_LIMIT),
        cost_estimate=cost(0, 4e6),
    )(ffn_grad, *[value for state in ffn_states for value in state], *last_go)
    out_grad, out_m, out_s, out_u, in_grad, in_m, in_s, in_u, down_grad, down_m, down_s, down_u = ffn_new
    lines = vectors.shape[0] // BLOCK
    like = [shape_of(qkv_weight.shape, F32)]
    qkv_grad, qkv_m, qkv_s, qkv_u, totals = pl.pallas_call(
        qkv_update_kernel,
        out_shape=like * 4 + [shape_of((lines + 8, BLOCK), F32)],
        in_specs=[VMEM_SPEC] * (6 + len(go)),
        out_specs=[VMEM_SPEC] * 5,
        compiler_params=params(SMALL_LIMIT),
        cost_estimate=cost(0, 4e6),
    )(qkv_grad, qkv_weight, qkv_moment, qkv_square, vec_local, norms, *go)
    totals = sum_all(totals, dims)
    states = [
        (qkv_u, qkv_weight, qkv_average),
        (out_u, out_weight.T, out_average.T),
        (in_u, in_weight, in_average),
        (down_u, down_weight.T, down_average.T),
    ]
    pieces = [value.reshape(lines, BLOCK) for value in (vectors, vec_moment, vec_square, vec_average)]
    shapes = [shape_of(update.shape, F32) for update, _, _ in states for _ in range(2)]
    shapes += [shape_of((lines, BLOCK), F32)] * 4 + [shape_of((8, BLOCK), F32)]
    (
        new_qkv, qkv_a, new_out, out_a, new_in, in_a, new_down, down_a, vec_m, vec_s, new_vec, vec_a, ratios,
    ) = pl.pallas_call(
        finish_kernel,
        out_shape=shapes,
        in_specs=[VMEM_SPEC] * 17,
        out_specs=[VMEM_SPEC] * len(shapes),
        compiler_params=params(SMALL_LIMIT),
        cost_estimate=cost(0, 4e6),
    )(totals, *[value for state in states for value in state], *pieces)
    vec_grad, vec_m, vec_s, new_vec, vec_a = [
        value.reshape(-1) for value in (totals[:lines], vec_m, vec_s, new_vec, vec_a)
    ]
    trust_ratio, weight_norm, update_norm = [ratios[index, :6] for index in range(3)]
    out_grad, out_m, out_s, new_out, out_a = [value.T for value in (out_grad, out_m, out_s, new_out, out_a)]
    down_grad, down_m, down_s, new_down, down_a = [
        value.T for value in (down_grad, down_m, down_s, new_down, down_a)
    ]
    return (
        pooled, tokens_grad, qkv_grad, out_grad, in_grad, down_grad, vec_grad,
        trust_ratio, weight_norm, update_norm,
        qkv_m, out_m, in_m, down_m, vec_m,
        qkv_s, out_s, in_s, down_s, vec_s,
        new_qkv, new_out, new_in, new_down, new_vec,
        qkv_a, out_a, in_a, down_a, vec_a,
    )


def solution(mesh):
    matrices = (P(None, "dp", "mp"), P("mp", "dp"), P("dp", "mp"), P("mp", "dp"), P())
    return jax.shard_map(
        shards,
        mesh=mesh,
        in_specs=(P("dp", None, None), P("dp"), P("dp"), P("dp", None)) + matrices * 4,
        out_specs=(P("dp", None), P("dp", None, "mp")) + matrices + (P(), P(), P()) + matrices * 4,
        check_vma=False,
    )
```

```python
import functools

import jax
import jax.numpy as jnp
from jax import lax
from jax.experimental import pallas as pl
from jax.experimental.pallas import tpu as pltpu
from jax.sharding import PartitionSpec as P

HEAD = 64
STEP = 10
TILE = 256
BLOCK = 128
GROUP = 6

beta_one = 0.9
beta_two = 0.999
adam_eps = 1e-06
weight_decay = 0.01
learn_rate = 0.3
vector_rate = 0.05
ema_keep = 0.9
norm_eps = 1e-12
masked_score = -1000000000.0
gelu_in = 0.7978845608028654
gelu_cube = 0.044715

BF = jnp.bfloat16
F32 = jnp.float32
VMEM_LIMIT = 62 * 1024 * 1024
SMALL_LIMIT = 14 * 1024 * 1024


def dp_dims(count):
    known = {16: ((4, 4), (2, 2), (2, 1)), 128: ((4, 32), (8, 4), (4, 1))}
    return known.get(count, ((count, 1),))


def dp_shift(value, dim, step):
    size, stride = dim
    count = lax.axis_size("dp")
    pairs = []
    for index in range(count):
        place = index // stride % size
        pairs.append((index, index + ((place + step) % size - place) * stride))
    return lax.ppermute(value, "dp", pairs)


def dp_place(dim):
    size, stride = dim
    return lax.rem(lax.div(lax.axis_index("dp"), stride), size)


def swap_core(value):
    return lax.ppermute(value, "mp", [(0, 1), (1, 0)])


def arrange(pieces, dim, axis):
    size, _ = dim
    place = dp_place(dim)
    if size == 2:
        return jnp.where(place == 0, jnp.stack(pieces, axis), jnp.stack(pieces[::-1], axis))
    ordered = []
    for target in range(size):
        which = lax.rem(target - place + size, size)
        chosen = pieces[0]
        for step in range(1, size):
            chosen = jnp.where(which == step, pieces[step], chosen)
        ordered.append(chosen)
    return jnp.stack(ordered, axis)


def gather_send(value, dim):
    return [value] + [dp_shift(value, dim, -step) for step in range(1, dim[0])]


def scatter_send(slabs, dim):
    return [dp_shift(slab, dim, step) for step, slab in enumerate(slabs, 1)]


def sum_all(value, dims):
    value = value + swap_core(value)
    count = lax.axis_size("dp")
    for size, stride in dims:
        bit = 1
        while bit < size:
            pairs = []
            for index in range(count):
                place = index // stride % size
                pairs.append((index, index + ((place ^ bit) - place) * stride))
            value = value + lax.ppermute(value, "dp", pairs)
            bit *= 2
    return value


def dot_nn(left, right):
    return jnp.dot(left, right, preferred_element_type=F32)


def dot_nt(left, right):
    return lax.dot_general(left, right, (((1,), (1,)), ((), ())), preferred_element_type=F32)


def dot_tn(left, right):
    return lax.dot_general(left, right, (((0,), (0,)), ((), ())), preferred_element_type=F32)


def vec_at(index, width, core=None, part=0, cols=None):
    if core is None:
        return slice(index * width, (index + 1) * width)
    which = core if part == 0 else 1 - core
    return pl.ds(pl.multiple_of(index * width + which * cols, BLOCK), cols)


def column_sums(value):
    rows, cols = value.shape
    return jnp.sum(value.reshape(rows // 8, 8, cols), axis=0)


def pack_kernel(
    core_ref, order_ref, len_ref, tok_ref, rows_ref, seg_ref, off_ref, tiles_ref, *stage
):
    core = core_ref[0]
    half = order_ref.shape[0] // 2
    total = rows_ref.shape[0]

    def clear(step, carry):
        rows = pl.ds(pl.multiple_of(step * BLOCK, BLOCK), BLOCK)
        for column in stage:
            column[rows, :] = jnp.zeros((BLOCK, BLOCK), F32)
        seg_ref[rows, :] = jnp.full((BLOCK, BLOCK), -1.0, F32)
        return carry

    lax.fori_loop(0, total // BLOCK, clear, 0)

    def start_of(cursor, count):
        inside = cursor & (BLOCK - 1)
        return jnp.where(inside + count > BLOCK, cursor - inside + BLOCK, cursor)

    def place(slot, cursor):
        sentence = order_ref[2 * slot + core]
        count = len_ref[sentence]
        start = start_of(cursor, count)
        off_ref[0, slot] = start
        span = tok_ref.shape[1]
        value = tok_ref[sentence].astype(F32)
        for index, column in enumerate(stage):
            column[pl.ds(start, span), :] = value[:, index * BLOCK : (index + 1) * BLOCK]
        row = lax.broadcasted_iota(jnp.int32, (span, BLOCK), 0)
        seg_ref[pl.ds(start, span), :] = jnp.where(row < count, slot.astype(F32), -1.0)
        return start + count

    used = lax.fori_loop(0, half, place, 0)
    tiles_ref[0] = (used + TILE - 1) // TILE

    def partner(slot, cursor):
        count = len_ref[order_ref[2 * slot + 1 - core]]
        start = start_of(cursor, count)
        off_ref[1, slot] = start
        return start + count

    lax.fori_loop(0, half, partner, 0)

    def low(step, carry):
        rows = pl.ds(pl.multiple_of(step * BLOCK, BLOCK), BLOCK)
        for index, column in enumerate(stage):
            rows_ref[rows, index * BLOCK : (index + 1) * BLOCK] = column[rows, :].astype(BF)
        return carry

    lax.fori_loop(0, total // BLOCK, low, 0)


def head_masks():
    lane = lax.broadcasted_iota(jnp.int32, (1, 2 * HEAD), 1)
    first = jnp.where(lane < HEAD, 1.0, 0.0)
    return first.astype(BF), (1.0 - first).astype(BF)


def two_heads(value, masks):
    return jnp.concatenate([value * masks[0], value * masks[1]], axis=0)


def same_sentence(seg):
    across = jnp.transpose(seg)
    return jnp.concatenate([seg, seg], axis=1) == jnp.concatenate([across, across], axis=1)


def softmax_rows(scores, mask):
    scores = jnp.where(mask, scores, masked_score)
    expon = jnp.exp(scores - jnp.max(scores, axis=0, keepdims=True))
    return expon * (1.0 / jnp.sum(expon, axis=0, keepdims=True))


def one_above_other(value):
    return jnp.concatenate([value[:, :BLOCK], value[:, BLOCK:]], axis=0)


def attn_forward_kernel(
    last, core_ref, rows_ref, seg_ref, vec_ref, qk0, vo0, qk1, vo1, qkv_ref, att_ref, norm_ref, inv_ref
):
    width = rows_ref.shape[1]
    half = width // 2
    core = core_ref[0]
    rows = rows_ref[...]
    weights = ((qk0, vo0), (qk1, vo1))
    for part, (qk, vo) in enumerate(weights):
        base = part * 3 * half
        value = dot_nn(rows, qk[...])
        query = value[:, :half] + vec_ref[:, vec_at(0, width, core, part, half)]
        qkv_ref[:, base : base + half] = query.astype(BF)
        qkv_ref[:, base + half : base + width] = value[:, half:].astype(BF)
        value = dot_nn(rows, vo[:, :half]) + vec_ref[:, vec_at(1, width, core, part, half)]
        qkv_ref[:, base + width : base + 3 * half] = value.astype(BF)
    masks = head_masks()
    for block in range(TILE // BLOCK):
        span = slice(block * BLOCK, (block + 1) * BLOCK)
        mask = same_sentence(seg_ref[span, :])
        for part in range(2):
            for pair in range(half // (2 * HEAD)):
                at = part * 3 * half + pair * 2 * HEAD
                query = qkv_ref[span, at : at + 2 * HEAD] * BF(HEAD**-0.5)
                key = qkv_ref[span, at + half : at + half + 2 * HEAD]
                value = qkv_ref[span, at + width : at + width + 2 * HEAD]
                probs = softmax_rows(dot_nt(key, two_heads(query, masks)), mask).astype(BF)
                mixed = dot_tn(one_above_other(probs), two_heads(value, masks))
                to = part * half + pair * 2 * HEAD
                att_ref[span, to : to + 2 * HEAD] = mixed.astype(BF)
    mixed = dot_nt(att_ref[:, :half], vo0[:, half:]) + dot_nt(att_ref[:, half:], vo1[:, half:])
    pre = rows.astype(F32) + (mixed + vec_ref[:, vec_at(2, width)])
    centre = pre - jnp.mean(pre, axis=-1, keepdims=True)
    inverse = lax.rsqrt(jnp.mean(centre * centre, axis=-1, keepdims=True) + norm_eps)
    norm_ref[...] = centre * inverse
    inv_ref[...] = jnp.broadcast_to(inverse, inv_ref.shape)


def norm_back(grad, normed, inverse, gain):
    scaled = grad * gain
    first = jnp.mean(scaled, axis=-1, keepdims=True)
    second = jnp.mean(scaled * normed, axis=-1, keepdims=True)
    return (scaled - first - normed * second) * inverse


def hidden_pieces(core, width):
    return [
        pl.ds(
            pl.multiple_of(8 * width + (2 * (core if part < 2 else 1 - core) + part % 2) * width, BLOCK),
            width,
        )
        for part in range(4)
    ]


def ffn_kernel(
    last, core_ref, norm_ref, inv_ref, seg_ref, att_ref, vec_ref, high_ref, low_ref,
    w1_own, w1_other, w2_own, w2_other,
    grad_ref, emb_ref, sums_ref, down_own, down_other, in_own, in_other, rest_own, rest_other,
    sum1, sum2, sum3, act, slope, emb, counts, stage, sems,
):
    step = pl.program_id(0)
    width = norm_ref.shape[1]
    half = width // 2
    lanes = [slice(part % 2 * width, (part % 2 + 1) * width) for part in range(4)]
    w1 = [(w1_own, w1_other)[part // 2].at[:, lanes[part]] for part in range(4)]
    w2 = [(w2_own, w2_other)[part // 2].at[:, lanes[part]] for part in range(4)]
    hidden_at = hidden_pieces(core_ref[0], width)

    @pl.when(step == 0)
    def _():
        emb[...] = jnp.zeros_like(emb)
        counts[...] = jnp.zeros_like(counts)
        sums_ref[...] = jnp.zeros_like(sums_ref)

    gain_one, shift_one = vec_ref[:, vec_at(4, width)], vec_ref[:, vec_at(5, width)]
    gain_two, shift_two = vec_ref[:, vec_at(6, width)], vec_ref[:, vec_at(7, width)]
    bias_ffn = vec_ref[:, vec_at(3, width)]
    hidden_low = (norm_ref[...] * gain_one + shift_one).astype(BF)
    for part in range(4):
        pre = dot_nn(hidden_low, w1[part][...]) + vec_ref[:, hidden_at[part]]
        square = pre * pre
        tanh = jnp.tanh(pre * (gelu_in + gelu_in * gelu_cube * square))
        gate = 0.5 + 0.5 * tanh
        out = pre * gate
        act[part] = out.astype(BF)
        slope[part] = gate + out * (1.0 - tanh) * (gelu_in + 3.0 * gelu_in * gelu_cube * square)
    total = dot_nt(act[0], w2[0][...])
    for part in range(1, 4):
        total = total + dot_nt(act[part], w2[part][...])
    pre = (norm_ref[...] * gain_one + shift_one) + (total + bias_ffn)
    centre = pre - jnp.mean(pre, axis=-1, keepdims=True)
    inverse = lax.rsqrt(jnp.mean(centre * centre, axis=-1, keepdims=True) + norm_eps)
    normed = centre * inverse
    final = normed * gain_two + shift_two
    final_high = final.astype(BF)
    final_rest = (final - final_high.astype(F32)).astype(BF)
    seg = seg_ref[...]
    lane = lax.broadcasted_iota(jnp.int32, seg.shape, 1).astype(F32)
    pick = jnp.where(seg == lane, 1.0, 0.0)
    pick_across = jnp.transpose(pick).astype(BF)
    pick = pick.astype(BF)
    emb[...] += dot_nn(pick_across, final_high) + dot_nn(pick_across, final_rest)
    counts[...] += dot_nn(pick_across, jnp.ones((TILE, BLOCK), BF))
    back = dot_nn(pick, high_ref[...]) + dot_nn(pick, low_ref[...])
    sums_ref[:, vec_at(6, width)] += column_sums(back * normed)
    sums_ref[:, vec_at(7, width)] += column_sums(back)
    grad_two = norm_back(back, normed, inverse, gain_two)
    ffn_low = grad_two.astype(BF)
    sums_ref[:, vec_at(3, width)] += column_sums(ffn_low.astype(F32))
    grad_hidden, pres = grad_two, []
    for part in range(4):
        grad_act = dot_nn(ffn_low, w2[part][...])
        grad_pre = (grad_act * slope[part]).astype(BF)
        sums_ref[:, hidden_at[part]] += column_sums(grad_pre.astype(F32))
        grad_hidden = grad_hidden + dot_nt(grad_pre, w1[part][...])
        pres.append(grad_pre)
    normed_one = norm_ref[...]
    sums_ref[:, vec_at(4, width)] += column_sums(grad_hidden * normed_one)
    sums_ref[:, vec_at(5, width)] += column_sums(grad_hidden)
    grad_one = norm_back(grad_hidden, normed_one, inv_ref[:, :1], gain_one)
    grad_ref[...] = grad_one
    grad_low = grad_one.astype(BF)
    sums_ref[:, vec_at(2, width)] += column_sums(grad_low.astype(F32))

    fresh = step == 0
    rest = (rest_own, rest_other)
    places, at = [], 0
    for outs, sums in (((down_own, down_other), sum2), ((in_own, in_other), sum1)):
        cut = outs[0].shape[1] - width
        for index in (2, 3, 0, 1):
            out = outs[index // 2]
            if index % 2 == 0:
                targets = [(0, out.at[:, pl.ds(0, width)])]
            else:
                targets = [(0, out.at[:, pl.ds(width, cut)]), (cut, rest[index // 2].at[:, pl.ds(at, width - cut)])]
            places.append((sums.at[index], targets))
        at += width - cut
    for index in (1, 0):
        places.append((sum3.at[index], [(0, rest[index].at[:, pl.ds(at, half)])]))
    for part in range(4):
        sum2[part] = jnp.where(fresh, 0.0, sum2[part]) + dot_tn(ffn_low, act[part])
    pl.when(last)(lambda: store_sums(places[:4], stage, sems))
    for part in range(4):
        sum1[part] = jnp.where(fresh, 0.0, sum1[part]) + dot_tn(hidden_low, pres[part])
    for part in range(2):
        sum3[part] = jnp.where(fresh, 0.0, sum3[part]) + dot_tn(
            grad_low, att_ref[:, part * half : (part + 1) * half]
        )

    @pl.when(last)
    def _():
        store_sums(places[4:], stage, sems, 4)
        stores_done(places, stage, sems)
        held = emb_ref.shape[0]
        number = jnp.maximum(counts[:held], 1.0)
        emb_ref[...] = emb[:held] / jnp.concatenate([number] * (width // BLOCK), axis=1)


def attn_backward_kernel(
    last, core_ref, grad_ref, rows_ref, qkv_ref, seg_ref, before_ref, qk0, vo0, qk1, vo1,
    mine_ref, dx_ref, total_ref, own, other, dqkv_ref, dx, sums, weights, stage, sems,
):
    width = grad_ref.shape[1]
    half = width // 2
    core = core_ref[0]

    @pl.when(pl.program_id(0) == 0)
    def _():
        sums[...] = before_ref[...]

    grad_low = grad_ref[...].astype(BF)
    masks = head_masks()
    mask = [same_sentence(seg_ref[b * BLOCK : (b + 1) * BLOCK, :]) for b in range(TILE // BLOCK)]
    for part, vo in enumerate((vo0, vo1)):
        base = part * 3 * half
        grad_att = dot_nn(grad_low, vo[:, half:]).astype(BF)
        units = [(block, pair) for block in range(TILE // BLOCK) for pair in range(half // (2 * HEAD))]
        for start in range(0, len(units), GROUP):
            group = units[start : start + GROUP]
            spans = [slice(block * BLOCK, (block + 1) * BLOCK) for block, _ in group]
            ats = [pair * 2 * HEAD for _, pair in group]
            query_at = [slice(base + at, base + at + 2 * HEAD) for at in ats]
            key_at = [slice(base + half + at, base + half + at + 2 * HEAD) for at in ats]
            value_at = [slice(base + width + at, base + width + at + 2 * HEAD) for at in ats]
            each = range(len(group))
            query_two = [
                two_heads(qkv_ref[spans[i], query_at[i]] * BF(HEAD**-0.5), masks) for i in each
            ]
            att_two = [two_heads(grad_att[spans[i], ats[i] : ats[i] + 2 * HEAD], masks) for i in each]
            scores = [dot_nt(qkv_ref[spans[i], key_at[i]], query_two[i]) for i in each]
            grad_probs = [dot_nt(qkv_ref[spans[i], value_at[i]], att_two[i]) for i in each]
            probs = [softmax_rows(scores[i], mask[group[i][0]]) for i in each]
            for i in each:
                dqkv_ref[spans[i], value_at[i]] = dot_nn(probs[i].astype(BF), att_two[i]).astype(BF)
            inner = [jnp.sum(grad_probs[i] * probs[i], axis=0, keepdims=True) for i in each]
            grad_scores = [(probs[i] * (grad_probs[i] - inner[i])).astype(BF) for i in each]
            for i in each:
                dqkv_ref[spans[i], key_at[i]] = dot_nn(grad_scores[i], query_two[i]).astype(BF)
            for i in each:
                key_two = two_heads(qkv_ref[spans[i], key_at[i]], masks)
                grad_query = dot_tn(one_above_other(grad_scores[i]), key_two) * HEAD**-0.5
                dqkv_ref[spans[i], query_at[i]] = grad_query.astype(BF)
        sums[:, vec_at(0, width, core, part, half)] += column_sums(
            dqkv_ref[:, base : base + half].astype(F32)
        )
        sums[:, vec_at(1, width, core, part, half)] += column_sums(
            dqkv_ref[:, base + width : base + 3 * half].astype(F32)
        )

    rows = rows_ref[...]
    total = grad_ref[...]
    for part, (qk, vo) in enumerate(((qk0, vo0), (qk1, vo1))):
        base = part * 3 * half
        total = total + dot_nt(dqkv_ref[:, base : base + width], qk[...])
        total = total + dot_nt(dqkv_ref[:, base + width : base + 3 * half], vo[:, :half])
    dx[...] = total
    mine_ref[...] = dx[:, pl.ds(pl.multiple_of(core * half, half), half)]
    dx_ref[...] = dx[:, pl.ds(pl.multiple_of((1 - core) * half, half), half)].astype(BF)
    for part in range(2):
        before = jnp.where(pl.program_id(0) == 0, 0.0, weights[part])
        weights[part] = before + dot_tn(rows, dqkv_ref[:, part * 3 * half : (part + 1) * 3 * half])

    @pl.when(last)
    def _():
        places = [(weights.at[1], [(0, other)]), (weights.at[0], [(0, own)])]
        store_sums(places, stage, sems)
        for row in range(total_ref.shape[0]):
            lanes = sums[:, row * BLOCK : (row + 1) * BLOCK]
            total_ref[row : row + 1, :] = jnp.sum(lanes, axis=0, keepdims=True)
        stores_done(places, stage, sems)


def store_sums(places, stage, sems, start=0):
    for slot, (source, targets) in enumerate(places, start):
        stage[slot, :, : source.shape[-1]] = source[...].astype(BF)
        for index, (at, target) in enumerate(targets):
            lanes = pl.ds(at, target.shape[-1])
            pltpu.make_async_copy(stage.at[slot, :, lanes], target, sems.at[slot, index]).start()


def stores_done(places, stage, sems):
    for slot, (_, targets) in enumerate(places):
        for index, (at, target) in enumerate(targets):
            lanes = pl.ds(at, target.shape[-1])
            pltpu.make_async_copy(stage.at[slot, :, lanes], target, sems.at[slot, index]).wait()


def unpack_kernel(core_ref, order_ref, len_ref, off_ref, mine_ref, recv_ref, out_ref, *columns):
    core = core_ref[0]
    half = order_ref.shape[0] // 2
    span, cols = out_ref.shape[1], out_ref.shape[2]
    each = cols // BLOCK

    def spread(step, carry):
        rows = pl.ds(pl.multiple_of(step * BLOCK, BLOCK), BLOCK)
        for index in range(each):
            lanes = slice(index * BLOCK, (index + 1) * BLOCK)
            columns[index][rows, :] = mine_ref[rows, lanes]
            columns[each + index][rows, :] = recv_ref[rows, lanes].astype(F32)
        return carry

    lax.fori_loop(0, recv_ref.shape[0] // BLOCK, spread, 0)
    row = lax.broadcasted_iota(jnp.int32, (span, BLOCK), 0)

    def place(slot, carry):
        for which in range(2):
            parity = core if which == 0 else 1 - core
            sentence = order_ref[2 * slot + parity]
            count = len_ref[sentence]
            start = off_ref[which, slot]
            for index in range(each):
                value = columns[which * each + index][pl.ds(start, span), :]
                out_ref[sentence, :, index * BLOCK : (index + 1) * BLOCK] = jnp.where(
                    row < count, value, 0.0
                )
        return carry

    lax.fori_loop(0, half, place, 0)


SMEM_SPEC = pl.BlockSpec(memory_space=pltpu.SMEM)
VMEM_SPEC = pl.BlockSpec(memory_space=pltpu.VMEM)
HBM_SPEC = pl.BlockSpec(memory_space=pl.ANY)


def params(limit=VMEM_LIMIT):
    return pltpu.CompilerParams(vmem_limit_bytes=limit)


def tile_spec(cols):
    return pl.BlockSpec((TILE, cols), lambda step, tiles: (jnp.minimum(step, tiles[0] - 1), 0))


def held_spec(*shape):
    return pl.BlockSpec(
        shape, lambda step, tiles: (0,) * len(shape), pipeline_mode=pl.Buffered(1)
    )


def column_spec(width, column):
    return pl.BlockSpec((width, width), lambda step, tiles: (0, column), pipeline_mode=pl.Buffered(1))


def tiled_call(kernel, out_shape, in_specs, out_specs, scratch_shapes, cost_estimate):
    def body(tiles_ref, *refs):
        @pl.when(pl.program_id(0) < tiles_ref[0])
        def _():
            kernel(pl.program_id(0) == tiles_ref[0] - 1, *refs)

    def call(tiles, most, *operands):
        return pl.pallas_call(
            body,
            grid_spec=pltpu.PrefetchScalarGridSpec(
                num_scalar_prefetch=1,
                grid=(most // TILE,),
                in_specs=in_specs,
                out_specs=out_specs,
                scratch_shapes=scratch_shapes,
            ),
            out_shape=out_shape,
            compiler_params=params(),
            cost_estimate=cost_estimate,
        )(tiles, *operands)

    return call


def shape_of(shape, dtype):
    return jax.ShapeDtypeStruct(shape, dtype)


def cost(flops, read):
    return pl.CostEstimate(flops=int(flops), bytes_accessed=int(read), transcendentals=0)


class Side:
    def __init__(self, terms, order):
        self.terms, self.order = terms, order

    def cols(self):
        _, _, lanes = self.terms[0]
        return lanes.stop - lanes.start


def slab_sums(sides, dims, joined=False, also=None, limit=SMALL_LIMIT):
    first = dims[0]
    places = jnp.stack([dp_place(dim) for dim in dims]).astype(jnp.int32)
    at_of = {dim: index for index, dim in enumerate(dims)}
    lead = 1 if joined else first[0]
    operands, in_specs, plan = [], [], []
    out_shape, out_specs, targets = [], [], []

    def index_map(term_dims, current, step, left):
        def of(grid, at):
            index = []
            for dim in term_dims:
                if dim == first and (dim in left or (dim == current and not joined)):
                    index.append(grid)
                elif dim == current:
                    index.append(lax.rem(at[at_of[dim]] + step, dim[0]))
                else:
                    index.append(0 if dim in left else at[at_of[dim]])
            return (*index, 0, 0)

        return of

    for number, side in enumerate([*sides, *([also] if also else [])]):
        main = number < len(sides)
        current = first if joined and main else side.order[0]
        rows = side.terms[0][0].shape[-2]
        left = [dim for dim in side.terms[-1][1] if dim != current]
        rest = [dim[0] for dim in left if dim != first]
        for step in range(current[0]) if joined else range(1, current[0]):
            ids = []
            shared = ids if current != first or joined or step == 1 else plan[-1][0]
            if shared is ids:
                for array, term_dims, lanes in side.terms:
                    block, pick = [], []
                    for dim in term_dims:
                        whole = dim in left and dim != first
                        block.append(dim[0] if whole else 1)
                        pick.append(slice(None) if whole else 0)
                    ids.append((len(operands), tuple(pick), lanes))
                    operands.append(array)
                    spec = (*block, rows, array.shape[-1])
                    in_specs.append(pl.BlockSpec(spec, index_map(term_dims, current, step, left)))
            plan.append((shared, number, step))
            if joined and main:
                continue
            over = main and not joined
            shape = (lead if over else 1, *rest, rows, side.cols())
            out_shape.append(shape_of(shape, F32 if step == 0 else BF))
            out_specs.append(
                pl.BlockSpec(
                    (1, *shape[1:]), lambda grid, at, n=len(shape), over=over: (grid if over else 0,) + (0,) * (n - 1)
                )
            )
            targets.append((number, step))
    if joined:
        width = sum(side.cols() for side in sides)
        rows = sides[0].terms[0][0].shape[-2]
        for step in range(first[0]):
            out_shape.append(shape_of((rows, width), BF if step else F32))
            out_specs.append(pl.BlockSpec((rows, width), lambda grid, at: (0, 0)))
            targets.append((None, step))
    starts = [sum(side.cols() for side in sides[:number]) for number in range(len(sides))]

    def kernel(places_ref, *refs):
        ins, outs = refs[: len(operands)], refs[len(operands) :]

        def total_of(ids):
            total = None
            for index, pick, lanes in ids:
                value = ins[index][(*pick, slice(None), lanes)].astype(F32)
                total = value if total is None else total + value
            return total

        def keep(out, ids):
            out[0] = total_of(ids).astype(out.dtype)

        for ids, number, step in plan:
            if number >= len(sides):
                out = outs[targets.index((number, step))]
                if also.order[0] == first:
                    here = lax.rem(places_ref[0] + step, first[0])
                else:
                    here = 0
                pl.when(pl.program_id(0) == here)(lambda out=out, ids=ids: keep(out, ids))
            elif joined:
                out = outs[targets.index((None, step))]
                out[:, starts[number] : starts[number] + sides[number].cols()] = total_of(ids).astype(out.dtype)
            else:
                keep(outs[targets.index((number, step))], ids)

    sums = pl.pallas_call(
        kernel,
        grid_spec=pltpu.PrefetchScalarGridSpec(
            num_scalar_prefetch=1, grid=(lead,), in_specs=in_specs, out_specs=out_specs
        ),
        out_shape=out_shape,
        compiler_params=params(limit),
        cost_estimate=cost(0, 8e6),
    )(places, *operands)
    more = [value[0] for value, (which, _) in zip(sums, targets) if which == len(sides)]
    if joined:
        return [value for value, (which, _) in zip(sums, targets) if which is None], more
    lists = [[value for value, (which, _) in zip(sums, targets) if which == number] for number in range(len(sides))]
    return [*lists, more] if also else lists


def adam_moments(grad_value, moment, square):
    moment_new = beta_one * moment + (1.0 - beta_one) * grad_value
    square_new = beta_two * square + (1.0 - beta_two) * grad_value * grad_value
    scaled = (
        moment_new
        / (1.0 - beta_one**STEP)
        / (jnp.sqrt(square_new / (1.0 - beta_two**STEP)) + adam_eps)
    )
    return (moment_new, square_new, scaled)


def square_sum(value):
    return jnp.sum(jnp.sum(value * value, axis=0, keepdims=True), axis=1, keepdims=True)


def note_norms(norms, matrix, weight, update):
    row = lax.broadcasted_iota(jnp.int32, norms.shape, 0)
    lane = lax.broadcasted_iota(jnp.int32, norms.shape, 1)
    here = jnp.where(row == 0, square_sum(weight), square_sum(update))
    return norms + jnp.where(jnp.logical_and(row < 2, lane == matrix), here, 0.0)


def ffn_update_kernel(count, own_ref, rest_ref, *refs):
    states, arrived, outs = refs[:9], refs[9:-13], refs[-13:]
    total, rest = own_ref[...], rest_ref[...]
    for ref in arrived[:count]:
        total = total + ref[...].astype(F32)
    for ref in arrived[count:]:
        rest = rest + ref[...].astype(F32)
    norms = jnp.zeros(outs[12].shape, F32)
    cut = states[6].shape[1] - BLOCK
    grads = (
        rest[:, 3 * BLOCK :],
        jnp.concatenate([total[:, cut:], rest[:, BLOCK : 3 * BLOCK]], axis=1),
        jnp.concatenate([total[:, :cut], rest[:, :BLOCK]], axis=1),
    )
    for index in range(3):
        weight, moment, square = states[3 * index : 3 * index + 3]
        grad = grads[index]
        moment_new, square_new, scaled = adam_moments(grad, moment[...], square[...])
        update = scaled + weight_decay * weight[...]
        for target, value in zip(outs[4 * index :], (grad, moment_new, square_new, update)):
            target[...] = value
        norms = note_norms(norms, 3 + index, weight[...], update)
    outs[12][...] = norms


def qkv_update_kernel(
    own_ref, weight_ref, moment_ref, square_ref, vec_ref, norms_ref, *refs
):
    arrived, (grad_out, moment_out, square_out, update_out, totals_ref) = refs[:-5], refs[-5:]
    cols = weight_ref.shape[2]
    total = own_ref[...]
    for ref in arrived:
        total = total + ref[...].astype(F32)
    rows = vec_ref.shape[0]
    norms = norms_ref[...]
    for index in range(3):
        grad = total[:, index * cols : (index + 1) * cols]
        moment, square, scaled = adam_moments(grad, moment_ref[index], square_ref[index])
        update = scaled + weight_decay * weight_ref[index]
        grad_out[index] = grad
        moment_out[index] = moment
        square_out[index] = square
        update_out[index] = update
        norms = note_norms(norms, index, weight_ref[index], update)
    totals_ref[:rows, :] = vec_ref[...]
    totals_ref[rows:, :] = norms


def finish_kernel(totals_ref, *refs):
    ins, outs = refs[:16], refs[16:]
    rows = totals_ref.shape[0] - 8
    weight_norm = jnp.sqrt(totals_ref[rows : rows + 1, :])
    update_norm = jnp.sqrt(totals_ref[rows + 1 : rows + 2, :])
    trust = weight_norm / update_norm
    lane = lax.broadcasted_iota(jnp.int32, trust.shape, 1)
    outs[12][0:1, :] = trust
    outs[12][1:2, :] = weight_norm
    outs[12][2:3, :] = update_norm

    def step(matrix):
        return learn_rate * jnp.sum(jnp.where(lane == matrix, trust, 0.0), axis=1, keepdims=True)

    for index in range(4):
        update, weight, average = ins[3 * index : 3 * index + 3]
        for piece in range(3 if index == 0 else 1):
            at = (piece,) if index == 0 else (Ellipsis,)
            new = weight[at] - step(piece if index == 0 else index + 2) * update[at]
            outs[2 * index][at] = new
            outs[2 * index + 1][at] = ema_keep * average[at] + (1.0 - ema_keep) * new
    vectors, moment, square, average = ins[12:16]
    grad = totals_ref[:rows, :]
    moment_new, square_new, scaled = adam_moments(grad, moment[...], square[...])
    new = vectors[...] - vector_rate * scaled
    outs[8][...] = moment_new
    outs[9][...] = square_new
    outs[10][...] = new
    outs[11][...] = ema_keep * average[...] + (1.0 - ema_keep) * new


def shards(
    tokens, lengths, send_order, pooled_grad,
    qkv_weight, out_weight, in_weight, down_weight, vectors,
    qkv_moment, out_moment, in_moment, down_moment, vec_moment,
    qkv_square, out_square, in_square, down_square, vec_square,
    qkv_average, out_average, in_average, down_average, vec_average,
):
    core = lax.axis_index("mp")
    count = lax.axis_size("dp")
    dims = dp_dims(count)
    sents, span, width = tokens.shape
    half = width // 2
    mine = sents // 2
    most = mine * span
    shard_rows = qkv_weight.shape[1]
    core_word = core.reshape(1).astype(jnp.int32)

    def flip(value):
        return jnp.where(core == 0, value, value[::-1])

    chunk = jnp.concatenate([qkv_weight[0], qkv_weight[1], qkv_weight[2], out_weight.T], axis=1)
    down_t = down_weight.T.astype(BF)
    first, others = dims[0], dims[1:]
    orders = (others, others[::-1])
    sides = (0, 1)

    def gather_start(pieces):
        value = arrange(pieces, first, 0)
        cols = value.shape[-1] // 2
        return [
            (value[..., side * cols : (side + 1) * cols], [first], orders[side]) for side in sides
        ]

    def gather_out(state):
        return [gather_send(value, order[0]) if order else [value] for value, _, order in state]

    def gather_in(state, pieces):
        after = []
        for (value, done, order), come in zip(state, pieces):
            if order:
                axis = sum(1 for other in done if other[1] > order[0][1])
                value = arrange(come, order[0], axis)
                done = done + [order[0]]
            after.append((value, done, order[1:]))
        return after

    def gather_end(state):
        return [value.reshape(width, -1) for value, _, _ in state]

    share = sents // count
    if share % 2 == 0:
        own = lax.dynamic_index_in_dim(
            pooled_grad.reshape(count, share // 2, 2, width), core, 2, keepdims=False
        )
        pair_grad = lax.all_to_all(own, "dp", 0, 0, tiled=True).reshape(mine, width)
    else:
        own = lax.all_to_all(pooled_grad, "dp", 0, 0, tiled=True)
        pair_grad = lax.dynamic_index_in_dim(
            own.reshape(mine, 2, width), core, 1, keepdims=False
        )

    pieces0 = gather_send(chunk.astype(BF), first)
    qkvo = gather_start(pieces0)
    pieces0 = gather_out(qkvo)
    own, held = lax.optimization_barrier((in_weight.astype(BF), [pieces[0] for pieces in pieces0]))
    pieces1 = gather_send(own, first)
    pieces0, pieces1, pair_grad = lax.optimization_barrier((pieces0, pieces1, pair_grad))
    qkvo = gather_in(qkvo, pieces0)
    pieces0 = gather_out(qkvo)
    held = [pieces[0] for pieces in pieces0]
    own, held = lax.optimization_barrier((down_t, held))
    pieces2 = gather_send(own, first)

    order_word, _ = lax.optimization_barrier((send_order, [pieces[0] for pieces in pieces0]))
    packed = pl.pallas_call(
        pack_kernel,
        out_shape=(
            shape_of((most, width), BF),
            shape_of((most, BLOCK), F32),
            shape_of((2, mine), jnp.int32),
            shape_of((1,), jnp.int32),
        ),
        in_specs=[SMEM_SPEC, SMEM_SPEC, SMEM_SPEC, VMEM_SPEC],
        out_specs=(VMEM_SPEC, VMEM_SPEC, SMEM_SPEC, SMEM_SPEC),
        scratch_shapes=[pltpu.VMEM((most, BLOCK), F32)] * (width // BLOCK),
        compiler_params=params(),
        cost_estimate=cost(0, 30e6),
    )(core_word, order_word, lengths, tokens)
    packed, pieces0, pieces2 = lax.optimization_barrier((packed, pieces0, pieces2))
    rows, seg, offsets, tiles = packed
    full = jnp.concatenate(gather_end(gather_in(qkvo, pieces0)), axis=1)
    full = (full, swap_core(full))
    weights = (full[0], full[0], full[1], full[1])
    ffn = [
        (arrange(pieces, first, 0), [first], orders[side]) for side, pieces in enumerate((pieces1, pieces2))
    ]
    ffn = gather_in(ffn, gather_out(ffn))
    ffn_pieces = gather_out(ffn)

    own_order = lax.dynamic_index_in_dim(send_order.reshape(mine, 2), core, 1, keepdims=False)
    own_count = lengths[own_order].astype(F32)[:, None]
    back = jnp.pad(pair_grad / own_count, ((0, BLOCK - mine), (0, 0)))
    back_high = back.astype(BF)
    back_rest = (back - back_high.astype(F32)).astype(BF)
    weight_specs = [column_spec(width, 0), column_spec(width, 1)] * 2
    long_spec = held_spec(width, 2 * width)
    vec_spec = held_spec(1, vectors.shape[0])
    vec_row = vectors.reshape(1, -1)
    row_total = most * 0.6
    mids = [pieces[0] for pieces in ffn_pieces]
    tiles, mids, _, _ = lax.optimization_barrier((tiles, mids, back_high, back_rest))
    qkv, att, normed, inverse = tiled_call(
        attn_forward_kernel,
        out_shape=(
            shape_of((most, 3 * width), BF),
            shape_of((most, width), BF),
            shape_of((most, width), F32),
            shape_of((most, BLOCK), F32),
        ),
        in_specs=[SMEM_SPEC, tile_spec(width), tile_spec(BLOCK), vec_spec] + weight_specs,
        out_specs=(tile_spec(3 * width), tile_spec(width), tile_spec(width), tile_spec(BLOCK)),
        scratch_shapes=[],
        cost_estimate=cost(2 * row_total * 4 * width * width * 2, 30e6),
    )(tiles, most, core_word, rows, seg, vec_row, *weights)
    normed, ffn_pieces = lax.optimization_barrier((normed, ffn_pieces))

    w1, w2 = [(value, swap_core(value)) for value in gather_end(gather_in(ffn, ffn_pieces))]
    down_shape = shape_of((width, 2 * width - BLOCK), BF)
    in_shape = shape_of((width, 2 * width - 2 * BLOCK), BF)
    rest_shape = shape_of((width, half + 3 * BLOCK), BF)
    (
        grad_one, emb, vec_ffn, down_own, down_other, in_own, in_other, rest_own, rest_other,
    ) = tiled_call(
        ffn_kernel,
        out_shape=(
            shape_of((most, width), F32),
            shape_of((mine, width), F32),
            shape_of((8, vectors.shape[0]), F32),
            down_shape,
            down_shape,
            in_shape,
            in_shape,
            rest_shape,
            rest_shape,
        ),
        in_specs=[
            SMEM_SPEC, tile_spec(width), tile_spec(BLOCK), tile_spec(BLOCK), tile_spec(width), vec_spec,
        ]
        + [held_spec(BLOCK, width)] * 2
        + [long_spec] * 4,
        out_specs=(tile_spec(width), held_spec(mine, width), held_spec(8, vectors.shape[0])) + (HBM_SPEC,) * 6,
        scratch_shapes=[
            pltpu.VMEM((4, width, width), F32),
            pltpu.VMEM((4, width, width), F32),
            pltpu.VMEM((2, width, half), F32),
            pltpu.VMEM((4, TILE, width), BF),
            pltpu.VMEM((4, TILE, width), F32),
            pltpu.VMEM((BLOCK, width), F32),
            pltpu.VMEM((BLOCK, BLOCK), F32),
            pltpu.VMEM((10, width, width), BF),
            pltpu.SemaphoreType.DMA((10, 2)),
        ],
        cost_estimate=cost(2 * row_total * 24 * width * width, 30e6),
    )(
        tiles, most, core_word, normed, inverse, seg, att, vec_row, back_high, back_rest, *w1, *w2
    )

    def scatter_start(parts):
        sides = []
        for side, (lanes, *arrays) in enumerate(parts):
            terms = [
                (array.reshape(*[size for size, _ in dims], shard_rows, -1), list(dims), lanes)
                for array in arrays
            ]
            sides.append(Side(terms, orders[side][::-1]))
        return sides

    def scatter_out(sides, limit=SMALL_LIMIT, also=None):
        if len({side.order[0][0] for side in sides}) == 1:
            return slab_sums(sides, dims, also=also, limit=limit)
        heads = [slab_sums([side], dims, limit=limit)[0] for side in sides[:-1]]
        return heads + slab_sums(sides[-1:], dims, also=also, limit=limit)

    def scatter_go(sides, slabs):
        return [scatter_send(sent, side.order[0]) for side, sent in zip(sides, slabs)]

    def scatter_in(sides, arrived):
        after = []
        for side, come in zip(sides, arrived):
            left = [dim for dim in side.terms[-1][1] if dim != side.order[0]]
            new = [(array, left, slice(0, side.cols())) for array in come]
            after.append(Side(side.terms + new, side.order[1:]))
        return after

    def go_pooled(value):
        return lax.all_to_all(value, "dp", 0, 0, tiled=True)

    come = [swap_core(down_other), swap_core(in_other), swap_core(rest_other)]
    grad_send = scatter_start(
        ((slice(0, down_shape.shape[1]), down_own, come[0]), (slice(0, in_shape.shape[1]), in_own, come[1]))
    )
    (rest_send,) = scatter_start(((slice(0, rest_shape.shape[1]), rest_own, come[2]),))
    rest_send.order = dims[:1] + others[::-1]
    *slabs, rest_slabs = scatter_out(grad_send, VMEM_LIMIT, rest_send)
    pooled = go_pooled(emb.reshape(count, share // 2, width)) if share % 2 == 0 else emb
    tiles, slabs, rest_slabs, pooled = lax.optimization_barrier((tiles, slabs, rest_slabs, pooled))
    qkv_shape = shape_of((width, 3 * half), BF)
    dx_mine, dx_other, vec_local, own, other = tiled_call(
        attn_backward_kernel,
        out_shape=(
            shape_of((most, half), F32),
            shape_of((most, half), BF),
            shape_of((vectors.shape[0] // BLOCK, BLOCK), F32),
            qkv_shape,
            qkv_shape,
        ),
        in_specs=[
            SMEM_SPEC, tile_spec(width), tile_spec(width), tile_spec(3 * width), tile_spec(BLOCK),
            held_spec(8, vectors.shape[0]),
        ]
        + weight_specs,
        out_specs=(tile_spec(half), tile_spec(half), held_spec(vectors.shape[0] // BLOCK, BLOCK))
        + (HBM_SPEC,) * 2,
        scratch_shapes=[
            pltpu.VMEM((TILE, 3 * width), BF),
            pltpu.VMEM((TILE, width), F32),
            pltpu.VMEM((8, vectors.shape[0]), F32),
            pltpu.VMEM((2, width, 3 * half), F32),
            pltpu.VMEM((2, width, 3 * half), BF),
            pltpu.SemaphoreType.DMA((2, 1)),
        ],
        cost_estimate=cost(2 * row_total * 18 * width * width, 30e6),
    )(tiles, most, core_word, grad_one, rows, qkv, seg, vec_ffn, *weights)
    arrived, rest_arrived, own, other, dx_other = lax.optimization_barrier(
        (scatter_go(grad_send, slabs), scatter_go([rest_send], [rest_slabs]), own, other, dx_other)
    )
    grad_send = scatter_in(grad_send, arrived)
    (rest_send,) = scatter_in([rest_send], rest_arrived)
    *slabs, rest_slabs = scatter_out(grad_send, VMEM_LIMIT, rest_send)
    come = swap_core(other)
    own, come, slabs, rest_slabs = lax.optimization_barrier((own, come, slabs, rest_slabs))
    cut = 3 * half // (2 * BLOCK) * BLOCK
    qkv_send = scatter_start(((slice(0, cut), own, come), (slice(cut, 3 * half), own, come)))
    qkv_slabs = scatter_out(qkv_send)
    order_word, slabs = lax.optimization_barrier((send_order, slabs))

    tokens_grad = pl.pallas_call(
        unpack_kernel,
        out_shape=shape_of((sents, span, half), F32),
        in_specs=[SMEM_SPEC] * 4 + [VMEM_SPEC] * 2,
        out_specs=VMEM_SPEC,
        scratch_shapes=[pltpu.VMEM((most, BLOCK), F32)] * (2 * half // BLOCK),
        compiler_params=params(),
        cost_estimate=cost(0, 20e6),
    )(core_word, order_word, lengths, offsets, dx_mine, swap_core(dx_other))
    arrived, rest_arrived, tokens_grad, qkv_slabs = lax.optimization_barrier(
        (scatter_go(grad_send, slabs), scatter_go([rest_send], [rest_slabs]), tokens_grad, qkv_slabs)
    )
    grad_send = scatter_in(grad_send, arrived)
    (rest_send,) = scatter_in([rest_send], rest_arrived)
    (ffn_grad, *slabs), (rest_grad, *rest_slabs) = slab_sums(
        grad_send, dims, joined=True, also=rest_send, limit=VMEM_LIMIT
    )
    qkv_slabs, slabs = lax.optimization_barrier((qkv_slabs, slabs))
    last_go = scatter_send(slabs, first)
    go = scatter_go(qkv_send, qkv_slabs)
    qkv_send = scatter_in(qkv_send, go)
    while qkv_send[0].order:
        go = scatter_go(qkv_send, scatter_out(qkv_send))
        go, last_go, pooled, rest_slabs = lax.optimization_barrier((go, last_go, pooled, rest_slabs))
        qkv_send = scatter_in(qkv_send, go)
    rest_go = scatter_send(rest_slabs, rest_send.order[0])
    (qkv_grad, *slabs), _ = slab_sums(qkv_send, dims, joined=True)
    go = scatter_send(slabs, first)

    both = flip(jnp.stack([pooled, swap_core(pooled)]))
    if share % 2 == 0:
        pooled = jnp.moveaxis(both, 0, 2).reshape(sents, width)
    else:
        both = jnp.moveaxis(both, 0, 1).reshape(sents, width)
        pooled = go_pooled(both)

    go, pooled = lax.optimization_barrier((go, pooled))
    ffn_states = [
        (out_weight.T, out_moment.T, out_square.T),
        (in_weight, in_moment, in_square),
        (down_weight.T, down_moment.T, down_square.T),
    ]
    shapes = [shape_of(state[0].shape, F32) for state in ffn_states for _ in range(4)]
    *ffn_new, norms = pl.pallas_call(
        functools.partial(ffn_update_kernel, len(last_go)),
        out_shape=shapes + [shape_of((8, BLOCK), F32)],
        in_specs=[VMEM_SPEC] * (11 + len(last_go) + len(rest_go)),
        out_specs=[VMEM_SPEC] * 13,
        compiler_params=params(SMALL_LIMIT),
        cost_estimate=cost(0, 4e6),
    )(ffn_grad, rest_grad, *[value for state in ffn_states for value in state], *last_go, *rest_go)
    out_grad, out_m, out_s, out_u, in_grad, in_m, in_s, in_u, down_grad, down_m, down_s, down_u = ffn_new
    lines = vectors.shape[0] // BLOCK
    like = [shape_of(qkv_weight.shape, F32)]
    qkv_grad, qkv_m, qkv_s, qkv_u, totals = pl.pallas_call(
        qkv_update_kernel,
        out_shape=like * 4 + [shape_of((lines + 8, BLOCK), F32)],
        in_specs=[VMEM_SPEC] * (6 + len(go)),
        out_specs=[VMEM_SPEC] * 5,
        compiler_params=params(SMALL_LIMIT),
        cost_estimate=cost(0, 4e6),
    )(qkv_grad, qkv_weight, qkv_moment, qkv_square, vec_local, norms, *go)
    totals = sum_all(totals, dims)
    states = [
        (qkv_u, qkv_weight, qkv_average),
        (out_u, out_weight.T, out_average.T),
        (in_u, in_weight, in_average),
        (down_u, down_weight.T, down_average.T),
    ]
    pieces = [value.reshape(lines, BLOCK) for value in (vectors, vec_moment, vec_square, vec_average)]
    shapes = [shape_of(update.shape, F32) for update, _, _ in states for _ in range(2)]
    shapes += [shape_of((lines, BLOCK), F32)] * 4 + [shape_of((8, BLOCK), F32)]
    (
        new_qkv, qkv_a, new_out, out_a, new_in, in_a, new_down, down_a, vec_m, vec_s, new_vec, vec_a, ratios,
    ) = pl.pallas_call(
        finish_kernel,
        out_shape=shapes,
        in_specs=[VMEM_SPEC] * 17,
        out_specs=[VMEM_SPEC] * len(shapes),
        compiler_params=params(SMALL_LIMIT),
        cost_estimate=cost(0, 4e6),
    )(totals, *[value for state in states for value in state], *pieces)
    vec_grad, vec_m, vec_s, new_vec, vec_a = [
        value.reshape(-1) for value in (totals[:lines], vec_m, vec_s, new_vec, vec_a)
    ]
    trust_ratio, weight_norm, update_norm = [ratios[index, :6] for index in range(3)]
    out_grad, out_m, out_s, new_out, out_a = [value.T for value in (out_grad, out_m, out_s, new_out, out_a)]
    down_grad, down_m, down_s, new_down, down_a = [
        value.T for value in (down_grad, down_m, down_s, new_down, down_a)
    ]
    return (
        pooled, tokens_grad, qkv_grad, out_grad, in_grad, down_grad, vec_grad,
        trust_ratio, weight_norm, update_norm,
        qkv_m, out_m, in_m, down_m, vec_m,
        qkv_s, out_s, in_s, down_s, vec_s,
        new_qkv, new_out, new_in, new_down, new_vec,
        qkv_a, out_a, in_a, down_a, vec_a,
    )


def solution(mesh):
    matrices = (P(None, "dp", "mp"), P("mp", "dp"), P("dp", "mp"), P("mp", "dp"), P())
    return jax.shard_map(
        shards,
        mesh=mesh,
        in_specs=(P("dp", None, None), P("dp"), P("dp"), P("dp", None)) + matrices * 4,
        out_specs=(P("dp", None), P("dp", None, "mp")) + matrices + (P(), P(), P()) + matrices * 4,
        check_vma=False,
    )
```

```python
import functools

import jax
import jax.numpy as jnp
from jax import lax
from jax.experimental import pallas as pl
from jax.experimental.pallas import tpu as pltpu
from jax.sharding import PartitionSpec as P

HEAD = 64
STEP = 10
TILE = 256
BLOCK = 128
GROUP = 6

beta_one = 0.9
beta_two = 0.999
adam_eps = 1e-06
weight_decay = 0.01
learn_rate = 0.3
vector_rate = 0.05
ema_keep = 0.9
norm_eps = 1e-12
masked_score = -1000000000.0
gelu_in = 0.7978845608028654
gelu_cube = 0.044715

BF = jnp.bfloat16
F32 = jnp.float32
VMEM_LIMIT = 62 * 1024 * 1024
SMALL_LIMIT = 14 * 1024 * 1024


def dp_dims(count):
    known = {16: ((4, 4), (2, 2), (2, 1)), 128: ((4, 32), (8, 4), (4, 1))}
    return known.get(count, ((count, 1),))


def dp_shift(value, dim, step):
    size, stride = dim
    count = lax.axis_size("dp")
    pairs = []
    for index in range(count):
        place = index // stride % size
        pairs.append((index, index + ((place + step) % size - place) * stride))
    return lax.ppermute(value, "dp", pairs)


def dp_place(dim):
    size, stride = dim
    return lax.rem(lax.div(lax.axis_index("dp"), stride), size)


def swap_core(value):
    return lax.ppermute(value, "mp", [(0, 1), (1, 0)])


def arrange(pieces, dim, axis):
    size, _ = dim
    place = dp_place(dim)
    if size == 2:
        return jnp.where(place == 0, jnp.stack(pieces, axis), jnp.stack(pieces[::-1], axis))
    ordered = []
    for target in range(size):
        which = lax.rem(target - place + size, size)
        chosen = pieces[0]
        for step in range(1, size):
            chosen = jnp.where(which == step, pieces[step], chosen)
        ordered.append(chosen)
    return jnp.stack(ordered, axis)


def gather_send(value, dim):
    return [value] + [dp_shift(value, dim, -step) for step in range(1, dim[0])]


def scatter_send(slabs, dim):
    return [dp_shift(slab, dim, step) for step, slab in enumerate(slabs, 1)]


def sum_all(value, dims):
    value = value + swap_core(value)
    count = lax.axis_size("dp")
    for size, stride in dims:
        bit = 1
        while bit < size:
            pairs = []
            for index in range(count):
                place = index // stride % size
                pairs.append((index, index + ((place ^ bit) - place) * stride))
            value = value + lax.ppermute(value, "dp", pairs)
            bit *= 2
    return value


def dot_nn(left, right):
    return jnp.dot(left, right, preferred_element_type=F32)


def dot_nt(left, right):
    return lax.dot_general(left, right, (((1,), (1,)), ((), ())), preferred_element_type=F32)


def dot_tn(left, right):
    return lax.dot_general(left, right, (((0,), (0,)), ((), ())), preferred_element_type=F32)


def vec_at(index, width, core=None, part=0, cols=None):
    if core is None:
        return slice(index * width, (index + 1) * width)
    which = core if part == 0 else 1 - core
    return pl.ds(pl.multiple_of(index * width + which * cols, BLOCK), cols)


def column_sums(value):
    rows, cols = value.shape
    return jnp.sum(value.reshape(rows // 8, 8, cols), axis=0)


def pack_kernel(
    core_ref, order_ref, len_ref, tok_ref, rows_ref, seg_ref, off_ref, tiles_ref, *stage
):
    core = core_ref[0]
    half = order_ref.shape[0] // 2
    total = rows_ref.shape[0]

    def clear(step, carry):
        rows = pl.ds(pl.multiple_of(step * BLOCK, BLOCK), BLOCK)
        for column in stage:
            column[rows, :] = jnp.zeros((BLOCK, BLOCK), F32)
        seg_ref[rows, :] = jnp.full((BLOCK, BLOCK), -1.0, F32)
        return carry

    lax.fori_loop(0, total // BLOCK, clear, 0)

    def choose(carry, parity):
        cursor, short, long = carry
        inside = cursor & (BLOCK - 1)
        room = BLOCK - inside
        fits = len_ref[order_ref[2 * long + parity]] <= room
        takes = jnp.logical_and(
            jnp.logical_not(fits), len_ref[order_ref[2 * short + parity]] <= room
        )
        slot = jnp.where(takes, short, long)
        start = jnp.where(jnp.logical_or(fits, takes), cursor, cursor + room)
        sentence = order_ref[2 * slot + parity]
        count = len_ref[sentence]
        left = (start + count, jnp.where(takes, short + 1, short), jnp.where(takes, long, long - 1))
        return slot, sentence, count, start, left

    def place(step, carry):
        slot, sentence, count, start, carry = choose(carry, core)
        off_ref[0, slot] = start
        span = tok_ref.shape[1]
        value = tok_ref[sentence].astype(F32)
        for index, column in enumerate(stage):
            column[pl.ds(start, span), :] = value[:, index * BLOCK : (index + 1) * BLOCK]
        row = lax.broadcasted_iota(jnp.int32, (span, BLOCK), 0)
        seg_ref[pl.ds(start, span), :] = jnp.where(row < count, slot.astype(F32), -1.0)
        return carry

    def partner(step, carry):
        slot, _, _, start, carry = choose(carry, 1 - core)
        off_ref[1, slot] = start
        return carry

    begin = (jnp.int32(0), jnp.int32(0), jnp.int32(half - 1))
    used, _, _ = lax.fori_loop(0, half, place, begin)
    tiles_ref[0] = (used + TILE - 1) // TILE
    lax.fori_loop(0, half, partner, begin)

    def low(step, carry):
        rows = pl.ds(pl.multiple_of(step * BLOCK, BLOCK), BLOCK)
        for index, column in enumerate(stage):
            rows_ref[rows, index * BLOCK : (index + 1) * BLOCK] = column[rows, :].astype(BF)
        return carry

    lax.fori_loop(0, total // BLOCK, low, 0)


def head_masks():
    lane = lax.broadcasted_iota(jnp.int32, (1, 2 * HEAD), 1)
    first = jnp.where(lane < HEAD, 1.0, 0.0)
    return first.astype(BF), (1.0 - first).astype(BF)


def two_heads(value, masks):
    return jnp.concatenate([value * masks[0], value * masks[1]], axis=0)


def same_sentence(seg):
    across = jnp.transpose(seg)
    return jnp.concatenate([seg, seg], axis=1) == jnp.concatenate([across, across], axis=1)


def softmax_rows(scores, mask):
    scores = jnp.where(mask, scores, masked_score)
    expon = jnp.exp(scores - jnp.max(scores, axis=0, keepdims=True))
    return expon * (1.0 / jnp.sum(expon, axis=0, keepdims=True))


def one_above_other(value):
    return jnp.concatenate([value[:, :BLOCK], value[:, BLOCK:]], axis=0)


def attn_forward_kernel(
    last, core_ref, rows_ref, seg_ref, vec_ref, qk0, vo0, qk1, vo1, qkv_ref, att_ref, norm_ref, inv_ref
):
    width = rows_ref.shape[1]
    half = width // 2
    core = core_ref[0]
    rows = rows_ref[...]
    weights = ((qk0, vo0), (qk1, vo1))
    for part, (qk, vo) in enumerate(weights):
        base = part * 3 * half
        value = dot_nn(rows, qk[...])
        query = value[:, :half] + vec_ref[:, vec_at(0, width, core, part, half)]
        qkv_ref[:, base : base + half] = query.astype(BF)
        qkv_ref[:, base + half : base + width] = value[:, half:].astype(BF)
        value = dot_nn(rows, vo[:, :half]) + vec_ref[:, vec_at(1, width, core, part, half)]
        qkv_ref[:, base + width : base + 3 * half] = value.astype(BF)
    masks = head_masks()
    for block in range(TILE // BLOCK):
        span = slice(block * BLOCK, (block + 1) * BLOCK)
        mask = same_sentence(seg_ref[span, :])
        for part in range(2):
            for pair in range(half // (2 * HEAD)):
                at = part * 3 * half + pair * 2 * HEAD
                query = qkv_ref[span, at : at + 2 * HEAD] * BF(HEAD**-0.5)
                key = qkv_ref[span, at + half : at + half + 2 * HEAD]
                value = qkv_ref[span, at + width : at + width + 2 * HEAD]
                probs = softmax_rows(dot_nt(key, two_heads(query, masks)), mask).astype(BF)
                mixed = dot_tn(one_above_other(probs), two_heads(value, masks))
                to = part * half + pair * 2 * HEAD
                att_ref[span, to : to + 2 * HEAD] = mixed.astype(BF)
    mixed = dot_nt(att_ref[:, :half], vo0[:, half:]) + dot_nt(att_ref[:, half:], vo1[:, half:])
    pre = rows.astype(F32) + (mixed + vec_ref[:, vec_at(2, width)])
    centre = pre - jnp.mean(pre, axis=-1, keepdims=True)
    inverse = lax.rsqrt(jnp.mean(centre * centre, axis=-1, keepdims=True) + norm_eps)
    norm_ref[...] = centre * inverse
    inv_ref[...] = jnp.broadcast_to(inverse, inv_ref.shape)


def norm_back(grad, normed, inverse, gain):
    scaled = grad * gain
    first = jnp.mean(scaled, axis=-1, keepdims=True)
    second = jnp.mean(scaled * normed, axis=-1, keepdims=True)
    return (scaled - first - normed * second) * inverse


def hidden_pieces(core, width):
    return [
        pl.ds(
            pl.multiple_of(8 * width + (2 * (core if part < 2 else 1 - core) + part % 2) * width, BLOCK),
            width,
        )
        for part in range(4)
    ]


def ffn_kernel(
    last, core_ref, norm_ref, inv_ref, seg_ref, att_ref, vec_ref, high_ref, low_ref,
    w1_own, w1_other, w2_own, w2_other,
    grad_ref, emb_ref, sums_ref, down_own, down_other, in_own, in_other, rest_own, rest_other,
    sum1, sum2, sum3, act, slope, emb, counts, stage, sems,
):
    step = pl.program_id(0)
    width = norm_ref.shape[1]
    half = width // 2
    lanes = [slice(part % 2 * width, (part % 2 + 1) * width) for part in range(4)]
    w1 = [(w1_own, w1_other)[part // 2].at[:, lanes[part]] for part in range(4)]
    w2 = [(w2_own, w2_other)[part // 2].at[:, lanes[part]] for part in range(4)]
    hidden_at = hidden_pieces(core_ref[0], width)

    @pl.when(step == 0)
    def _():
        emb[...] = jnp.zeros_like(emb)
        counts[...] = jnp.zeros_like(counts)
        sums_ref[...] = jnp.zeros_like(sums_ref)

    gain_one, shift_one = vec_ref[:, vec_at(4, width)], vec_ref[:, vec_at(5, width)]
    gain_two, shift_two = vec_ref[:, vec_at(6, width)], vec_ref[:, vec_at(7, width)]
    bias_ffn = vec_ref[:, vec_at(3, width)]
    hidden_low = (norm_ref[...] * gain_one + shift_one).astype(BF)
    for part in range(4):
        pre = dot_nn(hidden_low, w1[part][...]) + vec_ref[:, hidden_at[part]]
        square = pre * pre
        tanh = jnp.tanh(pre * (gelu_in + gelu_in * gelu_cube * square))
        gate = 0.5 + 0.5 * tanh
        out = pre * gate
        act[part] = out.astype(BF)
        slope[part] = gate + out * (1.0 - tanh) * (gelu_in + 3.0 * gelu_in * gelu_cube * square)
    total = dot_nt(act[0], w2[0][...])
    for part in range(1, 4):
        total = total + dot_nt(act[part], w2[part][...])
    pre = (norm_ref[...] * gain_one + shift_one) + (total + bias_ffn)
    centre = pre - jnp.mean(pre, axis=-1, keepdims=True)
    inverse = lax.rsqrt(jnp.mean(centre * centre, axis=-1, keepdims=True) + norm_eps)
    normed = centre * inverse
    final = normed * gain_two + shift_two
    final_high = final.astype(BF)
    final_rest = (final - final_high.astype(F32)).astype(BF)
    seg = seg_ref[...]
    lane = lax.broadcasted_iota(jnp.int32, seg.shape, 1).astype(F32)
    pick = jnp.where(seg == lane, 1.0, 0.0)
    pick_across = jnp.transpose(pick).astype(BF)
    pick = pick.astype(BF)
    emb[...] += dot_nn(pick_across, final_high) + dot_nn(pick_across, final_rest)
    counts[...] += dot_nn(pick_across, jnp.ones((TILE, BLOCK), BF))
    back = dot_nn(pick, high_ref[...]) + dot_nn(pick, low_ref[...])
    sums_ref[:, vec_at(6, width)] += column_sums(back * normed)
    sums_ref[:, vec_at(7, width)] += column_sums(back)
    grad_two = norm_back(back, normed, inverse, gain_two)
    ffn_low = grad_two.astype(BF)
    sums_ref[:, vec_at(3, width)] += column_sums(ffn_low.astype(F32))
    grad_hidden, pres = grad_two, []
    for part in range(4):
        grad_act = dot_nn(ffn_low, w2[part][...])
        grad_pre = (grad_act * slope[part]).astype(BF)
        sums_ref[:, hidden_at[part]] += column_sums(grad_pre.astype(F32))
        grad_hidden = grad_hidden + dot_nt(grad_pre, w1[part][...])
        pres.append(grad_pre)
    normed_one = norm_ref[...]
    sums_ref[:, vec_at(4, width)] += column_sums(grad_hidden * normed_one)
    sums_ref[:, vec_at(5, width)] += column_sums(grad_hidden)
    grad_one = norm_back(grad_hidden, normed_one, inv_ref[:, :1], gain_one)
    grad_ref[...] = grad_one
    grad_low = grad_one.astype(BF)
    sums_ref[:, vec_at(2, width)] += column_sums(grad_low.astype(F32))

    fresh = step == 0
    rest = (rest_own, rest_other)
    places, at = [], 0
    for outs, sums in (((down_own, down_other), sum2), ((in_own, in_other), sum1)):
        cut = outs[0].shape[1] - width
        for index in (2, 3, 0, 1):
            out = outs[index // 2]
            if index % 2 == 0:
                targets = [(0, out.at[:, pl.ds(0, width)])]
            else:
                targets = [(0, out.at[:, pl.ds(width, cut)]), (cut, rest[index // 2].at[:, pl.ds(at, width - cut)])]
            places.append((sums.at[index], targets))
        at += width - cut
    for index in (1, 0):
        places.append((sum3.at[index], [(0, rest[index].at[:, pl.ds(at, half)])]))
    for part in range(4):
        sum2[part] = jnp.where(fresh, 0.0, sum2[part]) + dot_tn(ffn_low, act[part])
    pl.when(last)(lambda: store_sums(places[:4], stage, sems))
    for part in range(4):
        sum1[part] = jnp.where(fresh, 0.0, sum1[part]) + dot_tn(hidden_low, pres[part])
    for part in range(2):
        sum3[part] = jnp.where(fresh, 0.0, sum3[part]) + dot_tn(
            grad_low, att_ref[:, part * half : (part + 1) * half]
        )

    @pl.when(last)
    def _():
        store_sums(places[4:], stage, sems, 4)
        stores_done(places, stage, sems)
        held = emb_ref.shape[0]
        number = jnp.maximum(counts[:held], 1.0)
        emb_ref[...] = emb[:held] / jnp.concatenate([number] * (width // BLOCK), axis=1)


def attn_backward_kernel(
    last, core_ref, grad_ref, rows_ref, qkv_ref, seg_ref, before_ref, qk0, vo0, qk1, vo1,
    mine_ref, dx_ref, total_ref, own, other, dqkv_ref, dx, sums, weights, stage, sems,
):
    width = grad_ref.shape[1]
    half = width // 2
    core = core_ref[0]

    @pl.when(pl.program_id(0) == 0)
    def _():
        sums[...] = before_ref[...]

    grad_low = grad_ref[...].astype(BF)
    masks = head_masks()
    mask = [same_sentence(seg_ref[b * BLOCK : (b + 1) * BLOCK, :]) for b in range(TILE // BLOCK)]
    for part, vo in enumerate((vo0, vo1)):
        base = part * 3 * half
        grad_att = dot_nn(grad_low, vo[:, half:]).astype(BF)
        units = [(block, pair) for block in range(TILE // BLOCK) for pair in range(half // (2 * HEAD))]
        for start in range(0, len(units), GROUP):
            group = units[start : start + GROUP]
            spans = [slice(block * BLOCK, (block + 1) * BLOCK) for block, _ in group]
            ats = [pair * 2 * HEAD for _, pair in group]
            query_at = [slice(base + at, base + at + 2 * HEAD) for at in ats]
            key_at = [slice(base + half + at, base + half + at + 2 * HEAD) for at in ats]
            value_at = [slice(base + width + at, base + width + at + 2 * HEAD) for at in ats]
            each = range(len(group))
            query_two = [
                two_heads(qkv_ref[spans[i], query_at[i]] * BF(HEAD**-0.5), masks) for i in each
            ]
            att_two = [two_heads(grad_att[spans[i], ats[i] : ats[i] + 2 * HEAD], masks) for i in each]
            scores = [dot_nt(qkv_ref[spans[i], key_at[i]], query_two[i]) for i in each]
            grad_probs = [dot_nt(qkv_ref[spans[i], value_at[i]], att_two[i]) for i in each]
            probs = [softmax_rows(scores[i], mask[group[i][0]]) for i in each]
            for i in each:
                dqkv_ref[spans[i], value_at[i]] = dot_nn(probs[i].astype(BF), att_two[i]).astype(BF)
            inner = [jnp.sum(grad_probs[i] * probs[i], axis=0, keepdims=True) for i in each]
            grad_scores = [(probs[i] * (grad_probs[i] - inner[i])).astype(BF) for i in each]
            for i in each:
                dqkv_ref[spans[i], key_at[i]] = dot_nn(grad_scores[i], query_two[i]).astype(BF)
            for i in each:
                key_two = two_heads(qkv_ref[spans[i], key_at[i]], masks)
                grad_query = dot_tn(one_above_other(grad_scores[i]), key_two) * HEAD**-0.5
                dqkv_ref[spans[i], query_at[i]] = grad_query.astype(BF)
        sums[:, vec_at(0, width, core, part, half)] += column_sums(
            dqkv_ref[:, base : base + half].astype(F32)
        )
        sums[:, vec_at(1, width, core, part, half)] += column_sums(
            dqkv_ref[:, base + width : base + 3 * half].astype(F32)
        )

    rows = rows_ref[...]
    total = grad_ref[...]
    for part, (qk, vo) in enumerate(((qk0, vo0), (qk1, vo1))):
        base = part * 3 * half
        total = total + dot_nt(dqkv_ref[:, base : base + width], qk[...])
        total = total + dot_nt(dqkv_ref[:, base + width : base + 3 * half], vo[:, :half])
    dx[...] = total
    mine_ref[...] = dx[:, pl.ds(pl.multiple_of(core * half, half), half)]
    dx_ref[...] = dx[:, pl.ds(pl.multiple_of((1 - core) * half, half), half)].astype(BF)
    for part in range(2):
        before = jnp.where(pl.program_id(0) == 0, 0.0, weights[part])
        weights[part] = before + dot_tn(rows, dqkv_ref[:, part * 3 * half : (part + 1) * 3 * half])

    @pl.when(last)
    def _():
        places = [(weights.at[1], [(0, other)]), (weights.at[0], [(0, own)])]
        store_sums(places, stage, sems)
        for row in range(total_ref.shape[0]):
            lanes = sums[:, row * BLOCK : (row + 1) * BLOCK]
            total_ref[row : row + 1, :] = jnp.sum(lanes, axis=0, keepdims=True)
        stores_done(places, stage, sems)


def store_sums(places, stage, sems, start=0):
    for slot, (source, targets) in enumerate(places, start):
        stage[slot, :, : source.shape[-1]] = source[...].astype(BF)
        for index, (at, target) in enumerate(targets):
            lanes = pl.ds(at, target.shape[-1])
            pltpu.make_async_copy(stage.at[slot, :, lanes], target, sems.at[slot, index]).start()


def stores_done(places, stage, sems):
    for slot, (_, targets) in enumerate(places):
        for index, (at, target) in enumerate(targets):
            lanes = pl.ds(at, target.shape[-1])
            pltpu.make_async_copy(stage.at[slot, :, lanes], target, sems.at[slot, index]).wait()


def unpack_kernel(core_ref, order_ref, len_ref, off_ref, mine_ref, recv_ref, out_ref, *columns):
    core = core_ref[0]
    half = order_ref.shape[0] // 2
    span, cols = out_ref.shape[1], out_ref.shape[2]
    each = cols // BLOCK

    def spread(step, carry):
        rows = pl.ds(pl.multiple_of(step * BLOCK, BLOCK), BLOCK)
        for index in range(each):
            lanes = slice(index * BLOCK, (index + 1) * BLOCK)
            columns[index][rows, :] = mine_ref[rows, lanes]
            columns[each + index][rows, :] = recv_ref[rows, lanes].astype(F32)
        return carry

    lax.fori_loop(0, recv_ref.shape[0] // BLOCK, spread, 0)
    row = lax.broadcasted_iota(jnp.int32, (span, BLOCK), 0)

    def place(slot, carry):
        for which in range(2):
            parity = core if which == 0 else 1 - core
            sentence = order_ref[2 * slot + parity]
            count = len_ref[sentence]
            start = off_ref[which, slot]
            for index in range(each):
                value = columns[which * each + index][pl.ds(start, span), :]
                out_ref[sentence, :, index * BLOCK : (index + 1) * BLOCK] = jnp.where(
                    row < count, value, 0.0
                )
        return carry

    lax.fori_loop(0, half, place, 0)


SMEM_SPEC = pl.BlockSpec(memory_space=pltpu.SMEM)
VMEM_SPEC = pl.BlockSpec(memory_space=pltpu.VMEM)
HBM_SPEC = pl.BlockSpec(memory_space=pl.ANY)


def params(limit=VMEM_LIMIT):
    return pltpu.CompilerParams(vmem_limit_bytes=limit)


def tile_spec(cols):
    return pl.BlockSpec((TILE, cols), lambda step, tiles: (jnp.minimum(step, tiles[0] - 1), 0))


def held_spec(*shape):
    return pl.BlockSpec(
        shape, lambda step, tiles: (0,) * len(shape), pipeline_mode=pl.Buffered(1)
    )


def column_spec(width, column):
    return pl.BlockSpec((width, width), lambda step, tiles: (0, column), pipeline_mode=pl.Buffered(1))


def tiled_call(kernel, out_shape, in_specs, out_specs, scratch_shapes, cost_estimate):
    def body(tiles_ref, *refs):
        @pl.when(pl.program_id(0) < tiles_ref[0])
        def _():
            kernel(pl.program_id(0) == tiles_ref[0] - 1, *refs)

    def call(tiles, most, *operands):
        return pl.pallas_call(
            body,
            grid_spec=pltpu.PrefetchScalarGridSpec(
                num_scalar_prefetch=1,
                grid=(most // TILE,),
                in_specs=in_specs,
                out_specs=out_specs,
                scratch_shapes=scratch_shapes,
            ),
            out_shape=out_shape,
            compiler_params=params(),
            cost_estimate=cost_estimate,
        )(tiles, *operands)

    return call


def shape_of(shape, dtype):
    return jax.ShapeDtypeStruct(shape, dtype)


def cost(flops, read):
    return pl.CostEstimate(flops=int(flops), bytes_accessed=int(read), transcendentals=0)


class Side:
    def __init__(self, terms, order):
        self.terms, self.order = terms, order

    def cols(self):
        _, _, lanes = self.terms[0]
        return lanes.stop - lanes.start


def slab_sums(sides, dims, joined=False, also=None, limit=SMALL_LIMIT):
    first = dims[0]
    places = jnp.stack([dp_place(dim) for dim in dims]).astype(jnp.int32)
    at_of = {dim: index for index, dim in enumerate(dims)}
    lead = 1 if joined else first[0]
    operands, in_specs, plan = [], [], []
    out_shape, out_specs, targets = [], [], []

    def index_map(term_dims, current, step, left):
        def of(grid, at):
            index = []
            for dim in term_dims:
                if dim == first and (dim in left or (dim == current and not joined)):
                    index.append(grid)
                elif dim == current:
                    index.append(lax.rem(at[at_of[dim]] + step, dim[0]))
                else:
                    index.append(0 if dim in left else at[at_of[dim]])
            return (*index, 0, 0)

        return of

    for number, side in enumerate([*sides, *([also] if also else [])]):
        main = number < len(sides)
        current = first if joined and main else side.order[0]
        rows = side.terms[0][0].shape[-2]
        left = [dim for dim in side.terms[-1][1] if dim != current]
        rest = [dim[0] for dim in left if dim != first]
        for step in range(current[0]) if joined else range(1, current[0]):
            ids = []
            shared = ids if current != first or joined or step == 1 else plan[-1][0]
            if shared is ids:
                for array, term_dims, lanes in side.terms:
                    block, pick = [], []
                    for dim in term_dims:
                        whole = dim in left and dim != first
                        block.append(dim[0] if whole else 1)
                        pick.append(slice(None) if whole else 0)
                    ids.append((len(operands), tuple(pick), lanes))
                    operands.append(array)
                    spec = (*block, rows, array.shape[-1])
                    in_specs.append(pl.BlockSpec(spec, index_map(term_dims, current, step, left)))
            plan.append((shared, number, step))
            if joined and main:
                continue
            over = main and not joined
            shape = (lead if over else 1, *rest, rows, side.cols())
            out_shape.append(shape_of(shape, F32 if step == 0 else BF))
            out_specs.append(
                pl.BlockSpec(
                    (1, *shape[1:]), lambda grid, at, n=len(shape), over=over: (grid if over else 0,) + (0,) * (n - 1)
                )
            )
            targets.append((number, step))
    if joined:
        width = sum(side.cols() for side in sides)
        rows = sides[0].terms[0][0].shape[-2]
        for step in range(first[0]):
            out_shape.append(shape_of((rows, width), BF if step else F32))
            out_specs.append(pl.BlockSpec((rows, width), lambda grid, at: (0, 0)))
            targets.append((None, step))
    starts = [sum(side.cols() for side in sides[:number]) for number in range(len(sides))]

    def kernel(places_ref, *refs):
        ins, outs = refs[: len(operands)], refs[len(operands) :]

        def total_of(ids):
            total = None
            for index, pick, lanes in ids:
                value = ins[index][(*pick, slice(None), lanes)].astype(F32)
                total = value if total is None else total + value
            return total

        def keep(out, ids):
            out[0] = total_of(ids).astype(out.dtype)

        for ids, number, step in plan:
            if number >= len(sides):
                out = outs[targets.index((number, step))]
                if also.order[0] == first:
                    here = lax.rem(places_ref[0] + step, first[0])
                else:
                    here = 0
                pl.when(pl.program_id(0) == here)(lambda out=out, ids=ids: keep(out, ids))
            elif joined:
                out = outs[targets.index((None, step))]
                out[:, starts[number] : starts[number] + sides[number].cols()] = total_of(ids).astype(out.dtype)
            else:
                keep(outs[targets.index((number, step))], ids)

    sums = pl.pallas_call(
        kernel,
        grid_spec=pltpu.PrefetchScalarGridSpec(
            num_scalar_prefetch=1, grid=(lead,), in_specs=in_specs, out_specs=out_specs
        ),
        out_shape=out_shape,
        compiler_params=params(limit),
        cost_estimate=cost(0, 8e6),
    )(places, *operands)
    more = [value[0] for value, (which, _) in zip(sums, targets) if which == len(sides)]
    if joined:
        return [value for value, (which, _) in zip(sums, targets) if which is None], more
    lists = [[value for value, (which, _) in zip(sums, targets) if which == number] for number in range(len(sides))]
    return [*lists, more] if also else lists


def adam_moments(grad_value, moment, square):
    moment_new = beta_one * moment + (1.0 - beta_one) * grad_value
    square_new = beta_two * square + (1.0 - beta_two) * grad_value * grad_value
    scaled = (
        moment_new
        / (1.0 - beta_one**STEP)
        / (jnp.sqrt(square_new / (1.0 - beta_two**STEP)) + adam_eps)
    )
    return (moment_new, square_new, scaled)


def square_sum(value):
    return jnp.sum(jnp.sum(value * value, axis=0, keepdims=True), axis=1, keepdims=True)


def note_norms(norms, matrix, weight, update):
    row = lax.broadcasted_iota(jnp.int32, norms.shape, 0)
    lane = lax.broadcasted_iota(jnp.int32, norms.shape, 1)
    here = jnp.where(row == 0, square_sum(weight), square_sum(update))
    return norms + jnp.where(jnp.logical_and(row < 2, lane == matrix), here, 0.0)


def ffn_update_kernel(count, own_ref, rest_ref, *refs):
    states, arrived, outs = refs[:9], refs[9:-13], refs[-13:]
    total, rest = own_ref[...], rest_ref[...]
    for ref in arrived[:count]:
        total = total + ref[...].astype(F32)
    for ref in arrived[count:]:
        rest = rest + ref[...].astype(F32)
    norms = jnp.zeros(outs[12].shape, F32)
    cut = states[6].shape[1] - BLOCK
    grads = (
        rest[:, 3 * BLOCK :],
        jnp.concatenate([total[:, cut:], rest[:, BLOCK : 3 * BLOCK]], axis=1),
        jnp.concatenate([total[:, :cut], rest[:, :BLOCK]], axis=1),
    )
    for index in range(3):
        weight, moment, square = states[3 * index : 3 * index + 3]
        grad = grads[index]
        moment_new, square_new, scaled = adam_moments(grad, moment[...], square[...])
        update = scaled + weight_decay * weight[...]
        for target, value in zip(outs[4 * index :], (grad, moment_new, square_new, update)):
            target[...] = value
        norms = note_norms(norms, 3 + index, weight[...], update)
    outs[12][...] = norms


def qkv_update_kernel(
    own_ref, weight_ref, moment_ref, square_ref, vec_ref, norms_ref, *refs
):
    arrived, (grad_out, moment_out, square_out, update_out, totals_ref) = refs[:-5], refs[-5:]
    cols = weight_ref.shape[2]
    total = own_ref[...]
    for ref in arrived:
        total = total + ref[...].astype(F32)
    rows = vec_ref.shape[0]
    norms = norms_ref[...]
    for index in range(3):
        grad = total[:, index * cols : (index + 1) * cols]
        moment, square, scaled = adam_moments(grad, moment_ref[index], square_ref[index])
        update = scaled + weight_decay * weight_ref[index]
        grad_out[index] = grad
        moment_out[index] = moment
        square_out[index] = square
        update_out[index] = update
        norms = note_norms(norms, index, weight_ref[index], update)
    totals_ref[:rows, :] = vec_ref[...]
    totals_ref[rows:, :] = norms


def finish_kernel(totals_ref, *refs):
    ins, outs = refs[:16], refs[16:]
    rows = totals_ref.shape[0] - 8
    weight_norm = jnp.sqrt(totals_ref[rows : rows + 1, :])
    update_norm = jnp.sqrt(totals_ref[rows + 1 : rows + 2, :])
    trust = weight_norm / update_norm
    lane = lax.broadcasted_iota(jnp.int32, trust.shape, 1)
    outs[12][0:1, :] = trust
    outs[12][1:2, :] = weight_norm
    outs[12][2:3, :] = update_norm

    def step(matrix):
        return learn_rate * jnp.sum(jnp.where(lane == matrix, trust, 0.0), axis=1, keepdims=True)

    for index in range(4):
        update, weight, average = ins[3 * index : 3 * index + 3]
        for piece in range(3 if index == 0 else 1):
            at = (piece,) if index == 0 else (Ellipsis,)
            new = weight[at] - step(piece if index == 0 else index + 2) * update[at]
            outs[2 * index][at] = new
            outs[2 * index + 1][at] = ema_keep * average[at] + (1.0 - ema_keep) * new
    vectors, moment, square, average = ins[12:16]
    grad = totals_ref[:rows, :]
    moment_new, square_new, scaled = adam_moments(grad, moment[...], square[...])
    new = vectors[...] - vector_rate * scaled
    outs[8][...] = moment_new
    outs[9][...] = square_new
    outs[10][...] = new
    outs[11][...] = ema_keep * average[...] + (1.0 - ema_keep) * new


def shards(
    tokens, lengths, send_order, pooled_grad,
    qkv_weight, out_weight, in_weight, down_weight, vectors,
    qkv_moment, out_moment, in_moment, down_moment, vec_moment,
    qkv_square, out_square, in_square, down_square, vec_square,
    qkv_average, out_average, in_average, down_average, vec_average,
):
    core = lax.axis_index("mp")
    count = lax.axis_size("dp")
    dims = dp_dims(count)
    sents, span, width = tokens.shape
    half = width // 2
    mine = sents // 2
    most = mine * span
    shard_rows = qkv_weight.shape[1]
    core_word = core.reshape(1).astype(jnp.int32)

    def flip(value):
        return jnp.where(core == 0, value, value[::-1])

    chunk = jnp.concatenate([qkv_weight[0], qkv_weight[1], qkv_weight[2], out_weight.T], axis=1)
    down_t = down_weight.T.astype(BF)
    first, others = dims[0], dims[1:]
    orders = (others, others[::-1])
    sides = (0, 1)

    def gather_start(pieces):
        value = arrange(pieces, first, 0)
        cols = value.shape[-1] // 2
        return [
            (value[..., side * cols : (side + 1) * cols], [first], orders[side]) for side in sides
        ]

    def gather_out(state):
        return [gather_send(value, order[0]) if order else [value] for value, _, order in state]

    def gather_in(state, pieces):
        after = []
        for (value, done, order), come in zip(state, pieces):
            if order:
                axis = sum(1 for other in done if other[1] > order[0][1])
                value = arrange(come, order[0], axis)
                done = done + [order[0]]
            after.append((value, done, order[1:]))
        return after

    def gather_end(state):
        return [value.reshape(width, -1) for value, _, _ in state]

    share = sents // count
    if share % 2 == 0:
        own = lax.dynamic_index_in_dim(
            pooled_grad.reshape(count, share // 2, 2, width), core, 2, keepdims=False
        )
        pair_grad = lax.all_to_all(own, "dp", 0, 0, tiled=True).reshape(mine, width)
    else:
        own = lax.all_to_all(pooled_grad, "dp", 0, 0, tiled=True)
        pair_grad = lax.dynamic_index_in_dim(
            own.reshape(mine, 2, width), core, 1, keepdims=False
        )

    pieces0 = gather_send(chunk.astype(BF), first)
    qkvo = gather_start(pieces0)
    pieces0 = gather_out(qkvo)
    own, held = lax.optimization_barrier((in_weight.astype(BF), [pieces[0] for pieces in pieces0]))
    pieces1 = gather_send(own, first)
    pieces0, pieces1, pair_grad = lax.optimization_barrier((pieces0, pieces1, pair_grad))
    qkvo = gather_in(qkvo, pieces0)
    pieces0 = gather_out(qkvo)
    held = [pieces[0] for pieces in pieces0]
    own, held = lax.optimization_barrier((down_t, held))
    pieces2 = gather_send(own, first)

    order_word, _ = lax.optimization_barrier((send_order, [pieces[0] for pieces in pieces0]))
    packed = pl.pallas_call(
        pack_kernel,
        out_shape=(
            shape_of((most, width), BF),
            shape_of((most, BLOCK), F32),
            shape_of((2, mine), jnp.int32),
            shape_of((1,), jnp.int32),
        ),
        in_specs=[SMEM_SPEC, SMEM_SPEC, SMEM_SPEC, VMEM_SPEC],
        out_specs=(VMEM_SPEC, VMEM_SPEC, SMEM_SPEC, SMEM_SPEC),
        scratch_shapes=[pltpu.VMEM((most, BLOCK), F32)] * (width // BLOCK),
        compiler_params=params(),
        cost_estimate=cost(0, 30e6),
    )(core_word, order_word, lengths, tokens)
    packed, pieces0, pieces2 = lax.optimization_barrier((packed, pieces0, pieces2))
    rows, seg, offsets, tiles = packed
    full = jnp.concatenate(gather_end(gather_in(qkvo, pieces0)), axis=1)
    full = (full, swap_core(full))
    weights = (full[0], full[0], full[1], full[1])
    ffn = [
        (arrange(pieces, first, 0), [first], orders[side]) for side, pieces in enumerate((pieces1, pieces2))
    ]
    ffn = gather_in(ffn, gather_out(ffn))
    ffn_pieces = gather_out(ffn)

    own_order = lax.dynamic_index_in_dim(send_order.reshape(mine, 2), core, 1, keepdims=False)
    own_count = lengths[own_order].astype(F32)[:, None]
    back = jnp.pad(pair_grad / own_count, ((0, BLOCK - mine), (0, 0)))
    back_high = back.astype(BF)
    back_rest = (back - back_high.astype(F32)).astype(BF)
    weight_specs = [column_spec(width, 0), column_spec(width, 1)] * 2
    long_spec = held_spec(width, 2 * width)
    vec_spec = held_spec(1, vectors.shape[0])
    vec_row = vectors.reshape(1, -1)
    row_total = most * 0.6
    mids = [pieces[0] for pieces in ffn_pieces]
    tiles, mids, _, _ = lax.optimization_barrier((tiles, mids, back_high, back_rest))
    qkv, att, normed, inverse = tiled_call(
        attn_forward_kernel,
        out_shape=(
            shape_of((most, 3 * width), BF),
            shape_of((most, width), BF),
            shape_of((most, width), F32),
            shape_of((most, BLOCK), F32),
        ),
        in_specs=[SMEM_SPEC, tile_spec(width), tile_spec(BLOCK), vec_spec] + weight_specs,
        out_specs=(tile_spec(3 * width), tile_spec(width), tile_spec(width), tile_spec(BLOCK)),
        scratch_shapes=[],
        cost_estimate=cost(2 * row_total * 4 * width * width * 2, 30e6),
    )(tiles, most, core_word, rows, seg, vec_row, *weights)
    normed, ffn_pieces = lax.optimization_barrier((normed, ffn_pieces))

    w1, w2 = [(value, swap_core(value)) for value in gather_end(gather_in(ffn, ffn_pieces))]
    down_shape = shape_of((width, 2 * width - BLOCK), BF)
    in_shape = shape_of((width, 2 * width - 2 * BLOCK), BF)
    rest_shape = shape_of((width, half + 3 * BLOCK), BF)
    (
        grad_one, emb, vec_ffn, down_own, down_other, in_own, in_other, rest_own, rest_other,
    ) = tiled_call(
        ffn_kernel,
        out_shape=(
            shape_of((most, width), F32),
            shape_of((mine, width), F32),
            shape_of((8, vectors.shape[0]), F32),
            down_shape,
            down_shape,
            in_shape,
            in_shape,
            rest_shape,
            rest_shape,
        ),
        in_specs=[
            SMEM_SPEC, tile_spec(width), tile_spec(BLOCK), tile_spec(BLOCK), tile_spec(width), vec_spec,
        ]
        + [held_spec(BLOCK, width)] * 2
        + [long_spec] * 4,
        out_specs=(tile_spec(width), held_spec(mine, width), held_spec(8, vectors.shape[0])) + (HBM_SPEC,) * 6,
        scratch_shapes=[
            pltpu.VMEM((4, width, width), F32),
            pltpu.VMEM((4, width, width), F32),
            pltpu.VMEM((2, width, half), F32),
            pltpu.VMEM((4, TILE, width), BF),
            pltpu.VMEM((4, TILE, width), F32),
            pltpu.VMEM((BLOCK, width), F32),
            pltpu.VMEM((BLOCK, BLOCK), F32),
            pltpu.VMEM((10, width, width), BF),
            pltpu.SemaphoreType.DMA((10, 2)),
        ],
        cost_estimate=cost(2 * row_total * 24 * width * width, 30e6),
    )(
        tiles, most, core_word, normed, inverse, seg, att, vec_row, back_high, back_rest, *w1, *w2
    )

    def scatter_start(parts):
        sides = []
        for side, (lanes, *arrays) in enumerate(parts):
            terms = [
                (array.reshape(*[size for size, _ in dims], shard_rows, -1), list(dims), lanes)
                for array in arrays
            ]
            sides.append(Side(terms, orders[side][::-1]))
        return sides

    def scatter_out(sides, limit=SMALL_LIMIT, also=None):
        if len({side.order[0][0] for side in sides}) == 1:
            return slab_sums(sides, dims, also=also, limit=limit)
        heads = [slab_sums([side], dims, limit=limit)[0] for side in sides[:-1]]
        return heads + slab_sums(sides[-1:], dims, also=also, limit=limit)

    def scatter_go(sides, slabs):
        return [scatter_send(sent, side.order[0]) for side, sent in zip(sides, slabs)]

    def scatter_in(sides, arrived):
        after = []
        for side, come in zip(sides, arrived):
            left = [dim for dim in side.terms[-1][1] if dim != side.order[0]]
            new = [(array, left, slice(0, side.cols())) for array in come]
            after.append(Side(side.terms + new, side.order[1:]))
        return after

    def go_pooled(value):
        return lax.all_to_all(value, "dp", 0, 0, tiled=True)

    come = [swap_core(down_other), swap_core(in_other), swap_core(rest_other)]
    grad_send = scatter_start(
        ((slice(0, down_shape.shape[1]), down_own, come[0]), (slice(0, in_shape.shape[1]), in_own, come[1]))
    )
    (rest_send,) = scatter_start(((slice(0, rest_shape.shape[1]), rest_own, come[2]),))
    rest_send.order = dims[:1] + others[::-1]
    *slabs, rest_slabs = scatter_out(grad_send, VMEM_LIMIT, rest_send)
    pooled = go_pooled(emb.reshape(count, share // 2, width)) if share % 2 == 0 else emb
    tiles, slabs, rest_slabs, pooled = lax.optimization_barrier((tiles, slabs, rest_slabs, pooled))
    qkv_shape = shape_of((width, 3 * half), BF)
    dx_mine, dx_other, vec_local, own, other = tiled_call(
        attn_backward_kernel,
        out_shape=(
            shape_of((most, half), F32),
            shape_of((most, half), BF),
            shape_of((vectors.shape[0] // BLOCK, BLOCK), F32),
            qkv_shape,
            qkv_shape,
        ),
        in_specs=[
            SMEM_SPEC, tile_spec(width), tile_spec(width), tile_spec(3 * width), tile_spec(BLOCK),
            held_spec(8, vectors.shape[0]),
        ]
        + weight_specs,
        out_specs=(tile_spec(half), tile_spec(half), held_spec(vectors.shape[0] // BLOCK, BLOCK))
        + (HBM_SPEC,) * 2,
        scratch_shapes=[
            pltpu.VMEM((TILE, 3 * width), BF),
            pltpu.VMEM((TILE, width), F32),
            pltpu.VMEM((8, vectors.shape[0]), F32),
            pltpu.VMEM((2, width, 3 * half), F32),
            pltpu.VMEM((2, width, 3 * half), BF),
            pltpu.SemaphoreType.DMA((2, 1)),
        ],
        cost_estimate=cost(2 * row_total * 18 * width * width, 30e6),
    )(tiles, most, core_word, grad_one, rows, qkv, seg, vec_ffn, *weights)
    arrived, rest_arrived, own, other, dx_other = lax.optimization_barrier(
        (scatter_go(grad_send, slabs), scatter_go([rest_send], [rest_slabs]), own, other, dx_other)
    )
    grad_send = scatter_in(grad_send, arrived)
    (rest_send,) = scatter_in([rest_send], rest_arrived)
    *slabs, rest_slabs = scatter_out(grad_send, VMEM_LIMIT, rest_send)
    come = swap_core(other)
    own, come, slabs, rest_slabs = lax.optimization_barrier((own, come, slabs, rest_slabs))
    cut = 3 * half // (2 * BLOCK) * BLOCK
    qkv_send = scatter_start(((slice(0, cut), own, come), (slice(cut, 3 * half), own, come)))
    qkv_slabs = scatter_out(qkv_send)
    order_word, slabs = lax.optimization_barrier((send_order, slabs))

    tokens_grad = pl.pallas_call(
        unpack_kernel,
        out_shape=shape_of((sents, span, half), F32),
        in_specs=[SMEM_SPEC] * 4 + [VMEM_SPEC] * 2,
        out_specs=VMEM_SPEC,
        scratch_shapes=[pltpu.VMEM((most, BLOCK), F32)] * (2 * half // BLOCK),
        compiler_params=params(),
        cost_estimate=cost(0, 20e6),
    )(core_word, order_word, lengths, offsets, dx_mine, swap_core(dx_other))
    arrived, rest_arrived, tokens_grad, qkv_slabs = lax.optimization_barrier(
        (scatter_go(grad_send, slabs), scatter_go([rest_send], [rest_slabs]), tokens_grad, qkv_slabs)
    )
    grad_send = scatter_in(grad_send, arrived)
    (rest_send,) = scatter_in([rest_send], rest_arrived)
    (ffn_grad, *slabs), (rest_grad, *rest_slabs) = slab_sums(
        grad_send, dims, joined=True, also=rest_send, limit=VMEM_LIMIT
    )
    qkv_slabs, slabs = lax.optimization_barrier((qkv_slabs, slabs))
    last_go = scatter_send(slabs, first)
    go = scatter_go(qkv_send, qkv_slabs)
    qkv_send = scatter_in(qkv_send, go)
    while qkv_send[0].order:
        go = scatter_go(qkv_send, scatter_out(qkv_send))
        go, last_go, pooled, rest_slabs = lax.optimization_barrier((go, last_go, pooled, rest_slabs))
        qkv_send = scatter_in(qkv_send, go)
    rest_go = scatter_send(rest_slabs, rest_send.order[0])
    (qkv_grad, *slabs), _ = slab_sums(qkv_send, dims, joined=True)
    go = scatter_send(slabs, first)

    both = flip(jnp.stack([pooled, swap_core(pooled)]))
    if share % 2 == 0:
        pooled = jnp.moveaxis(both, 0, 2).reshape(sents, width)
    else:
        both = jnp.moveaxis(both, 0, 1).reshape(sents, width)
        pooled = go_pooled(both)

    go, pooled = lax.optimization_barrier((go, pooled))
    ffn_states = [
        (out_weight.T, out_moment.T, out_square.T),
        (in_weight, in_moment, in_square),
        (down_weight.T, down_moment.T, down_square.T),
    ]
    shapes = [shape_of(state[0].shape, F32) for state in ffn_states for _ in range(4)]
    *ffn_new, norms = pl.pallas_call(
        functools.partial(ffn_update_kernel, len(last_go)),
        out_shape=shapes + [shape_of((8, BLOCK), F32)],
        in_specs=[VMEM_SPEC] * (11 + len(last_go) + len(rest_go)),
        out_specs=[VMEM_SPEC] * 13,
        compiler_params=params(SMALL_LIMIT),
        cost_estimate=cost(0, 4e6),
    )(ffn_grad, rest_grad, *[value for state in ffn_states for value in state], *last_go, *rest_go)
    out_grad, out_m, out_s, out_u, in_grad, in_m, in_s, in_u, down_grad, down_m, down_s, down_u = ffn_new
    lines = vectors.shape[0] // BLOCK
    like = [shape_of(qkv_weight.shape, F32)]
    qkv_grad, qkv_m, qkv_s, qkv_u, totals = pl.pallas_call(
        qkv_update_kernel,
        out_shape=like * 4 + [shape_of((lines + 8, BLOCK), F32)],
        in_specs=[VMEM_SPEC] * (6 + len(go)),
        out_specs=[VMEM_SPEC] * 5,
        compiler_params=params(SMALL_LIMIT),
        cost_estimate=cost(0, 4e6),
    )(qkv_grad, qkv_weight, qkv_moment, qkv_square, vec_local, norms, *go)
    totals = sum_all(totals, dims)
    states = [
        (qkv_u, qkv_weight, qkv_average),
        (out_u, out_weight.T, out_average.T),
        (in_u, in_weight, in_average),
        (down_u, down_weight.T, down_average.T),
    ]
    pieces = [value.reshape(lines, BLOCK) for value in (vectors, vec_moment, vec_square, vec_average)]
    shapes = [shape_of(update.shape, F32) for update, _, _ in states for _ in range(2)]
    shapes += [shape_of((lines, BLOCK), F32)] * 4 + [shape_of((8, BLOCK), F32)]
    (
        new_qkv, qkv_a, new_out, out_a, new_in, in_a, new_down, down_a, vec_m, vec_s, new_vec, vec_a, ratios,
    ) = pl.pallas_call(
        finish_kernel,
        out_shape=shapes,
        in_specs=[VMEM_SPEC] * 17,
        out_specs=[VMEM_SPEC] * len(shapes),
        compiler_params=params(SMALL_LIMIT),
        cost_estimate=cost(0, 4e6),
    )(totals, *[value for state in states for value in state], *pieces)
    vec_grad, vec_m, vec_s, new_vec, vec_a = [
        value.reshape(-1) for value in (totals[:lines], vec_m, vec_s, new_vec, vec_a)
    ]
    trust_ratio, weight_norm, update_norm = [ratios[index, :6] for index in range(3)]
    out_grad, out_m, out_s, new_out, out_a = [value.T for value in (out_grad, out_m, out_s, new_out, out_a)]
    down_grad, down_m, down_s, new_down, down_a = [
        value.T for value in (down_grad, down_m, down_s, new_down, down_a)
    ]
    return (
        pooled, tokens_grad, qkv_grad, out_grad, in_grad, down_grad, vec_grad,
        trust_ratio, weight_norm, update_norm,
        qkv_m, out_m, in_m, down_m, vec_m,
        qkv_s, out_s, in_s, down_s, vec_s,
        new_qkv, new_out, new_in, new_down, new_vec,
        qkv_a, out_a, in_a, down_a, vec_a,
    )


def solution(mesh):
    matrices = (P(None, "dp", "mp"), P("mp", "dp"), P("dp", "mp"), P("mp", "dp"), P())
    return jax.shard_map(
        shards,
        mesh=mesh,
        in_specs=(P("dp", None, None), P("dp"), P("dp"), P("dp", None)) + matrices * 4,
        out_specs=(P("dp", None), P("dp", None, "mp")) + matrices + (P(), P(), P()) + matrices * 4,
        check_vma=False,
    )
```

```python
import functools

import jax
import jax.numpy as jnp
from jax import lax
from jax.experimental import pallas as pl
from jax.experimental.pallas import tpu as pltpu
from jax.sharding import PartitionSpec as P

HEAD = 64
STEP = 10
TILE = 256
BLOCK = 128
GROUP = 6

beta_one = 0.9
beta_two = 0.999
adam_eps = 1e-06
weight_decay = 0.01
learn_rate = 0.3
vector_rate = 0.05
ema_keep = 0.9
norm_eps = 1e-12
masked_score = -1000000000.0
gelu_in = 0.7978845608028654
gelu_cube = 0.044715

BF = jnp.bfloat16
F32 = jnp.float32
VMEM_LIMIT = 62 * 1024 * 1024
SMALL_LIMIT = 14 * 1024 * 1024


def dp_dims(count):
    known = {16: ((4, 4), (2, 2), (2, 1)), 128: ((4, 32), (8, 4), (4, 1))}
    return known.get(count, ((count, 1),))


def dp_shift(value, dim, step):
    size, stride = dim
    count = lax.axis_size("dp")
    pairs = []
    for index in range(count):
        place = index // stride % size
        pairs.append((index, index + ((place + step) % size - place) * stride))
    return lax.ppermute(value, "dp", pairs)


def dp_place(dim):
    size, stride = dim
    return lax.rem(lax.div(lax.axis_index("dp"), stride), size)


def swap_core(value):
    return lax.ppermute(value, "mp", [(0, 1), (1, 0)])


def arrange(pieces, dim, axis):
    size, _ = dim
    place = dp_place(dim)
    if size == 2:
        return jnp.where(place == 0, jnp.stack(pieces, axis), jnp.stack(pieces[::-1], axis))
    ordered = []
    for target in range(size):
        which = lax.rem(target - place + size, size)
        chosen = pieces[0]
        for step in range(1, size):
            chosen = jnp.where(which == step, pieces[step], chosen)
        ordered.append(chosen)
    return jnp.stack(ordered, axis)


def gather_send(value, dim):
    return [value] + [dp_shift(value, dim, -step) for step in range(1, dim[0])]


def scatter_send(slabs, dim):
    return [dp_shift(slab, dim, step) for step, slab in enumerate(slabs, 1)]


def sum_all(value, dims):
    value = value + swap_core(value)
    count = lax.axis_size("dp")
    for size, stride in dims:
        bit = 1
        while bit < size:
            pairs = []
            for index in range(count):
                place = index // stride % size
                pairs.append((index, index + ((place ^ bit) - place) * stride))
            value = value + lax.ppermute(value, "dp", pairs)
            bit *= 2
    return value


def dot_nn(left, right):
    return jnp.dot(left, right, preferred_element_type=F32)


def dot_nt(left, right):
    return lax.dot_general(left, right, (((1,), (1,)), ((), ())), preferred_element_type=F32)


def dot_tn(left, right):
    return lax.dot_general(left, right, (((0,), (0,)), ((), ())), preferred_element_type=F32)


def vec_at(index, width, core=None, part=0, cols=None):
    if core is None:
        return slice(index * width, (index + 1) * width)
    which = core if part == 0 else 1 - core
    return pl.ds(pl.multiple_of(index * width + which * cols, BLOCK), cols)


def column_sums(value):
    rows, cols = value.shape
    return jnp.sum(value.reshape(rows // 8, 8, cols), axis=0)


def pack_kernel(
    core_ref, order_ref, len_ref, tok_ref, rows_ref, seg_ref, off_ref, tiles_ref, *stage
):
    core = core_ref[0]
    half = order_ref.shape[0] // 2
    total = rows_ref.shape[0]

    def clear(step, carry):
        rows = pl.ds(pl.multiple_of(step * BLOCK, BLOCK), BLOCK)
        for column in stage:
            column[rows, :] = jnp.zeros((BLOCK, BLOCK), F32)
        seg_ref[rows, :] = jnp.full((BLOCK, BLOCK), -1.0, F32)
        return carry

    lax.fori_loop(0, total // BLOCK, clear, 0)

    def choose(carry, parity):
        cursor, short, long = carry
        inside = cursor & (BLOCK - 1)
        room = BLOCK - inside
        fits = len_ref[order_ref[2 * long + parity]] <= room
        takes = jnp.logical_and(
            jnp.logical_not(fits), len_ref[order_ref[2 * short + parity]] <= room
        )
        slot = jnp.where(takes, short, long)
        start = jnp.where(jnp.logical_or(fits, takes), cursor, cursor + room)
        sentence = order_ref[2 * slot + parity]
        count = len_ref[sentence]
        left = (start + count, jnp.where(takes, short + 1, short), jnp.where(takes, long, long - 1))
        return slot, sentence, count, start, left

    def place(step, carry):
        slot, sentence, count, start, carry = choose(carry, core)
        off_ref[0, slot] = start
        span = tok_ref.shape[1]
        value = tok_ref[sentence].astype(F32)
        for index, column in enumerate(stage):
            column[pl.ds(start, span), :] = value[:, index * BLOCK : (index + 1) * BLOCK]
        row = lax.broadcasted_iota(jnp.int32, (span, BLOCK), 0)
        seg_ref[pl.ds(start, span), :] = jnp.where(row < count, slot.astype(F32), -1.0)
        return carry

    def partner(step, carry):
        slot, _, _, start, carry = choose(carry, 1 - core)
        off_ref[1, slot] = start
        return carry

    begin = (jnp.int32(0), jnp.int32(0), jnp.int32(half - 1))
    used, _, _ = lax.fori_loop(0, half, place, begin)
    tiles_ref[0] = (used + TILE - 1) // TILE
    lax.fori_loop(0, half, partner, begin)

    def low(step, carry):
        rows = pl.ds(pl.multiple_of(step * BLOCK, BLOCK), BLOCK)
        for index, column in enumerate(stage):
            rows_ref[rows, index * BLOCK : (index + 1) * BLOCK] = column[rows, :].astype(BF)
        return carry

    lax.fori_loop(0, total // BLOCK, low, 0)


def head_masks():
    lane = lax.broadcasted_iota(jnp.int32, (1, 2 * HEAD), 1)
    first = jnp.where(lane < HEAD, 1.0, 0.0)
    return first.astype(BF), (1.0 - first).astype(BF)


def two_heads(value, masks):
    return jnp.concatenate([value * masks[0], value * masks[1]], axis=0)


def same_sentence(seg):
    across = jnp.transpose(seg)
    return jnp.concatenate([seg, seg], axis=1) == jnp.concatenate([across, across], axis=1)


def softmax_rows(scores, mask):
    scores = jnp.where(mask, scores, masked_score)
    expon = jnp.exp(scores - jnp.max(scores, axis=0, keepdims=True))
    return expon * (1.0 / jnp.sum(expon, axis=0, keepdims=True))


def one_above_other(value):
    return jnp.concatenate([value[:, :BLOCK], value[:, BLOCK:]], axis=0)


def attn_forward_kernel(
    last, core_ref, rows_ref, seg_ref, vec_ref, qk0, vo0, qk1, vo1, qkv_ref, att_ref, norm_ref, inv_ref
):
    width = rows_ref.shape[1]
    half = width // 2
    core = core_ref[0]
    rows = rows_ref[...]
    weights = ((qk0, vo0), (qk1, vo1))
    for part, (qk, vo) in enumerate(weights):
        base = part * 3 * half
        value = dot_nn(rows, qk[...])
        query = value[:, :half] + vec_ref[:, vec_at(0, width, core, part, half)]
        qkv_ref[:, base : base + half] = query.astype(BF)
        qkv_ref[:, base + half : base + width] = value[:, half:].astype(BF)
        value = dot_nn(rows, vo[:, :half]) + vec_ref[:, vec_at(1, width, core, part, half)]
        qkv_ref[:, base + width : base + 3 * half] = value.astype(BF)
    masks = head_masks()
    for block in range(TILE // BLOCK):
        span = slice(block * BLOCK, (block + 1) * BLOCK)
        mask = same_sentence(seg_ref[span, :])
        for part in range(2):
            for pair in range(half // (2 * HEAD)):
                at = part * 3 * half + pair * 2 * HEAD
                query = qkv_ref[span, at : at + 2 * HEAD] * BF(HEAD**-0.5)
                key = qkv_ref[span, at + half : at + half + 2 * HEAD]
                value = qkv_ref[span, at + width : at + width + 2 * HEAD]
                probs = softmax_rows(dot_nt(key, two_heads(query, masks)), mask).astype(BF)
                mixed = dot_tn(one_above_other(probs), two_heads(value, masks))
                to = part * half + pair * 2 * HEAD
                att_ref[span, to : to + 2 * HEAD] = mixed.astype(BF)
    mixed = dot_nt(att_ref[:, :half], vo0[:, half:]) + dot_nt(att_ref[:, half:], vo1[:, half:])
    pre = rows.astype(F32) + (mixed + vec_ref[:, vec_at(2, width)])
    centre = pre - jnp.mean(pre, axis=-1, keepdims=True)
    inverse = lax.rsqrt(jnp.mean(centre * centre, axis=-1, keepdims=True) + norm_eps)
    norm_ref[...] = centre * inverse
    inv_ref[...] = jnp.broadcast_to(inverse, inv_ref.shape)


def norm_back(grad, normed, inverse, gain):
    scaled = grad * gain
    first = jnp.mean(scaled, axis=-1, keepdims=True)
    second = jnp.mean(scaled * normed, axis=-1, keepdims=True)
    return (scaled - first - normed * second) * inverse


def hidden_pieces(core, width):
    return [
        pl.ds(
            pl.multiple_of(8 * width + (2 * (core if part < 2 else 1 - core) + part % 2) * width, BLOCK),
            width,
        )
        for part in range(4)
    ]


def ffn_kernel(
    last, core_ref, norm_ref, inv_ref, seg_ref, att_ref, vec_ref, high_ref, low_ref,
    w1_own, w1_other, w2_own, w2_other,
    grad_ref, emb_ref, sums_ref, down_own, down_other, in_own, in_other, rest_own, rest_other,
    sum1, sum2, sum3, act, slope, emb, counts, stage, sems,
):
    step = pl.program_id(0)
    width = norm_ref.shape[1]
    half = width // 2
    lanes = [slice(part % 2 * width, (part % 2 + 1) * width) for part in range(4)]
    w1 = [(w1_own, w1_other)[part // 2].at[:, lanes[part]] for part in range(4)]
    w2 = [(w2_own, w2_other)[part // 2].at[:, lanes[part]] for part in range(4)]
    hidden_at = hidden_pieces(core_ref[0], width)

    @pl.when(step == 0)
    def _():
        emb[...] = jnp.zeros_like(emb)
        counts[...] = jnp.zeros_like(counts)
        sums_ref[...] = jnp.zeros_like(sums_ref)

    gain_one, shift_one = vec_ref[:, vec_at(4, width)], vec_ref[:, vec_at(5, width)]
    gain_two, shift_two = vec_ref[:, vec_at(6, width)], vec_ref[:, vec_at(7, width)]
    bias_ffn = vec_ref[:, vec_at(3, width)]
    hidden_low = (norm_ref[...] * gain_one + shift_one).astype(BF)
    for part in range(4):
        pre = dot_nn(hidden_low, w1[part][...]) + vec_ref[:, hidden_at[part]]
        square = pre * pre
        tanh = jnp.tanh(pre * (gelu_in + gelu_in * gelu_cube * square))
        gate = 0.5 + 0.5 * tanh
        out = pre * gate
        act[part] = out.astype(BF)
        slope[part] = gate + out * (1.0 - tanh) * (gelu_in + 3.0 * gelu_in * gelu_cube * square)
    total = dot_nt(act[0], w2[0][...])
    for part in range(1, 4):
        total = total + dot_nt(act[part], w2[part][...])
    pre = (norm_ref[...] * gain_one + shift_one) + (total + bias_ffn)
    centre = pre - jnp.mean(pre, axis=-1, keepdims=True)
    inverse = lax.rsqrt(jnp.mean(centre * centre, axis=-1, keepdims=True) + norm_eps)
    normed = centre * inverse
    final = normed * gain_two + shift_two
    final_high = final.astype(BF)
    final_rest = (final - final_high.astype(F32)).astype(BF)
    seg = seg_ref[...]
    lane = lax.broadcasted_iota(jnp.int32, seg.shape, 1).astype(F32)
    pick = jnp.where(seg == lane, 1.0, 0.0)
    pick_across = jnp.transpose(pick).astype(BF)
    pick = pick.astype(BF)
    emb[...] += dot_nn(pick_across, final_high) + dot_nn(pick_across, final_rest)
    counts[...] += dot_nn(pick_across, jnp.ones((TILE, BLOCK), BF))
    back = dot_nn(pick, high_ref[...]) + dot_nn(pick, low_ref[...])
    sums_ref[:, vec_at(6, width)] += column_sums(back * normed)
    sums_ref[:, vec_at(7, width)] += column_sums(back)
    grad_two = norm_back(back, normed, inverse, gain_two)
    ffn_low = grad_two.astype(BF)
    sums_ref[:, vec_at(3, width)] += column_sums(ffn_low.astype(F32))
    grad_hidden, pres = grad_two, []
    for part in range(4):
        grad_act = dot_nn(ffn_low, w2[part][...])
        grad_pre = (grad_act * slope[part]).astype(BF)
        sums_ref[:, hidden_at[part]] += column_sums(grad_pre.astype(F32))
        grad_hidden = grad_hidden + dot_nt(grad_pre, w1[part][...])
        pres.append(grad_pre)
    normed_one = norm_ref[...]
    sums_ref[:, vec_at(4, width)] += column_sums(grad_hidden * normed_one)
    sums_ref[:, vec_at(5, width)] += column_sums(grad_hidden)
    grad_one = norm_back(grad_hidden, normed_one, inv_ref[:, :1], gain_one)
    grad_ref[...] = grad_one
    grad_low = grad_one.astype(BF)
    sums_ref[:, vec_at(2, width)] += column_sums(grad_low.astype(F32))

    fresh = step == 0
    rest = (rest_own, rest_other)
    places, at = [], 0
    for outs, sums in (((down_own, down_other), sum2), ((in_own, in_other), sum1)):
        cut = outs[0].shape[1] - width
        for index in (2, 3, 0, 1):
            out = outs[index // 2]
            if index % 2 == 0:
                targets = [(0, out.at[:, pl.ds(0, width)])]
            else:
                targets = [(0, out.at[:, pl.ds(width, cut)]), (cut, rest[index // 2].at[:, pl.ds(at, width - cut)])]
            places.append((sums.at[index], targets))
        at += width - cut
    for index in (1, 0):
        places.append((sum3.at[index], [(0, rest[index].at[:, pl.ds(at, half)])]))
    for part in range(4):
        sum2[part] = jnp.where(fresh, 0.0, sum2[part]) + dot_tn(ffn_low, act[part])
    pl.when(last)(lambda: store_sums(places[:4], stage, sems))
    for part in range(4):
        sum1[part] = jnp.where(fresh, 0.0, sum1[part]) + dot_tn(hidden_low, pres[part])
    for part in range(2):
        sum3[part] = jnp.where(fresh, 0.0, sum3[part]) + dot_tn(
            grad_low, att_ref[:, part * half : (part + 1) * half]
        )

    @pl.when(last)
    def _():
        store_sums(places[4:], stage, sems, 4)
        stores_done(places, stage, sems)
        held = emb_ref.shape[0]
        number = jnp.maximum(counts[:held], 1.0)
        emb_ref[...] = emb[:held] / jnp.concatenate([number] * (width // BLOCK), axis=1)


def attn_backward_kernel(
    last, core_ref, grad_ref, rows_ref, qkv_ref, seg_ref, before_ref, qk0, vo0, qk1, vo1,
    mine_ref, dx_ref, total_ref, own, other, dqkv_ref, dx, sums, weights, stage, sems,
):
    width = grad_ref.shape[1]
    half = width // 2
    core = core_ref[0]

    @pl.when(pl.program_id(0) == 0)
    def _():
        sums[...] = before_ref[...]

    grad_low = grad_ref[...].astype(BF)
    masks = head_masks()
    mask = [same_sentence(seg_ref[b * BLOCK : (b + 1) * BLOCK, :]) for b in range(TILE // BLOCK)]
    for part, vo in enumerate((vo0, vo1)):
        base = part * 3 * half
        grad_att = dot_nn(grad_low, vo[:, half:]).astype(BF)
        units = [(block, pair) for block in range(TILE // BLOCK) for pair in range(half // (2 * HEAD))]
        for start in range(0, len(units), GROUP):
            group = units[start : start + GROUP]
            spans = [slice(block * BLOCK, (block + 1) * BLOCK) for block, _ in group]
            ats = [pair * 2 * HEAD for _, pair in group]
            query_at = [slice(base + at, base + at + 2 * HEAD) for at in ats]
            key_at = [slice(base + half + at, base + half + at + 2 * HEAD) for at in ats]
            value_at = [slice(base + width + at, base + width + at + 2 * HEAD) for at in ats]
            each = range(len(group))
            query_two = [
                two_heads(qkv_ref[spans[i], query_at[i]] * BF(HEAD**-0.5), masks) for i in each
            ]
            att_two = [two_heads(grad_att[spans[i], ats[i] : ats[i] + 2 * HEAD], masks) for i in each]
            scores = [dot_nt(qkv_ref[spans[i], key_at[i]], query_two[i]) for i in each]
            grad_probs = [dot_nt(qkv_ref[spans[i], value_at[i]], att_two[i]) for i in each]
            probs = [softmax_rows(scores[i], mask[group[i][0]]) for i in each]
            for i in each:
                dqkv_ref[spans[i], value_at[i]] = dot_nn(probs[i].astype(BF), att_two[i]).astype(BF)
            inner = [jnp.sum(grad_probs[i] * probs[i], axis=0, keepdims=True) for i in each]
            grad_scores = [(probs[i] * (grad_probs[i] - inner[i])).astype(BF) for i in each]
            for i in each:
                dqkv_ref[spans[i], key_at[i]] = dot_nn(grad_scores[i], query_two[i]).astype(BF)
            for i in each:
                key_two = two_heads(qkv_ref[spans[i], key_at[i]], masks)
                grad_query = dot_tn(one_above_other(grad_scores[i]), key_two) * HEAD**-0.5
                dqkv_ref[spans[i], query_at[i]] = grad_query.astype(BF)
        sums[:, vec_at(0, width, core, part, half)] += column_sums(
            dqkv_ref[:, base : base + half].astype(F32)
        )
        sums[:, vec_at(1, width, core, part, half)] += column_sums(
            dqkv_ref[:, base + width : base + 3 * half].astype(F32)
        )

    rows = rows_ref[...]
    total = grad_ref[...]
    for part, (qk, vo) in enumerate(((qk0, vo0), (qk1, vo1))):
        base = part * 3 * half
        total = total + dot_nt(dqkv_ref[:, base : base + width], qk[...])
        total = total + dot_nt(dqkv_ref[:, base + width : base + 3 * half], vo[:, :half])
    dx[...] = total
    mine_ref[...] = dx[:, pl.ds(pl.multiple_of(core * half, half), half)]
    dx_ref[...] = dx[:, pl.ds(pl.multiple_of((1 - core) * half, half), half)].astype(BF)
    for part in range(2):
        before = jnp.where(pl.program_id(0) == 0, 0.0, weights[part])
        weights[part] = before + dot_tn(rows, dqkv_ref[:, part * 3 * half : (part + 1) * 3 * half])

    @pl.when(last)
    def _():
        places = [(weights.at[1], [(0, other)]), (weights.at[0], [(0, own)])]
        store_sums(places, stage, sems)
        for row in range(total_ref.shape[0]):
            lanes = sums[:, row * BLOCK : (row + 1) * BLOCK]
            total_ref[row : row + 1, :] = jnp.sum(lanes, axis=0, keepdims=True)
        stores_done(places, stage, sems)


def store_sums(places, stage, sems, start=0):
    for slot, (source, targets) in enumerate(places, start):
        stage[slot, :, : source.shape[-1]] = source[...].astype(BF)
        for index, (at, target) in enumerate(targets):
            lanes = pl.ds(at, target.shape[-1])
            pltpu.make_async_copy(stage.at[slot, :, lanes], target, sems.at[slot, index]).start()


def stores_done(places, stage, sems):
    for slot, (_, targets) in enumerate(places):
        for index, (at, target) in enumerate(targets):
            lanes = pl.ds(at, target.shape[-1])
            pltpu.make_async_copy(stage.at[slot, :, lanes], target, sems.at[slot, index]).wait()


def unpack_kernel(core_ref, order_ref, len_ref, off_ref, mine_ref, recv_ref, out_ref, *columns):
    core = core_ref[0]
    half = order_ref.shape[0] // 2
    span, cols = out_ref.shape[1], out_ref.shape[2]
    each = cols // BLOCK

    def spread(step, carry):
        rows = pl.ds(pl.multiple_of(step * BLOCK, BLOCK), BLOCK)
        for index in range(each):
            lanes = slice(index * BLOCK, (index + 1) * BLOCK)
            columns[index][rows, :] = mine_ref[rows, lanes]
            columns[each + index][rows, :] = recv_ref[rows, lanes].astype(F32)
        return carry

    lax.fori_loop(0, recv_ref.shape[0] // BLOCK, spread, 0)
    row = lax.broadcasted_iota(jnp.int32, (span, BLOCK), 0)

    def place(slot, carry):
        for which in range(2):
            parity = core if which == 0 else 1 - core
            sentence = order_ref[2 * slot + parity]
            count = len_ref[sentence]
            start = off_ref[which, slot]
            for index in range(each):
                value = columns[which * each + index][pl.ds(start, span), :]
                out_ref[sentence, :, index * BLOCK : (index + 1) * BLOCK] = jnp.where(
                    row < count, value, 0.0
                )
        return carry

    lax.fori_loop(0, half, place, 0)


SMEM_SPEC = pl.BlockSpec(memory_space=pltpu.SMEM)
VMEM_SPEC = pl.BlockSpec(memory_space=pltpu.VMEM)
HBM_SPEC = pl.BlockSpec(memory_space=pl.ANY)


def params(limit=VMEM_LIMIT):
    return pltpu.CompilerParams(vmem_limit_bytes=limit)


def tile_spec(cols):
    return pl.BlockSpec((TILE, cols), lambda step, tiles: (jnp.minimum(step, tiles[0] - 1), 0))


def held_spec(*shape):
    return pl.BlockSpec(
        shape, lambda step, tiles: (0,) * len(shape), pipeline_mode=pl.Buffered(1)
    )


def column_spec(width, column):
    return pl.BlockSpec((width, width), lambda step, tiles: (0, column), pipeline_mode=pl.Buffered(1))


def tiled_call(kernel, out_shape, in_specs, out_specs, scratch_shapes, cost_estimate):
    def body(tiles_ref, *refs):
        @pl.when(pl.program_id(0) < tiles_ref[0])
        def _():
            kernel(pl.program_id(0) == tiles_ref[0] - 1, *refs)

    def call(tiles, most, *operands):
        return pl.pallas_call(
            body,
            grid_spec=pltpu.PrefetchScalarGridSpec(
                num_scalar_prefetch=1,
                grid=(most // TILE,),
                in_specs=in_specs,
                out_specs=out_specs,
                scratch_shapes=scratch_shapes,
            ),
            out_shape=out_shape,
            compiler_params=params(),
            cost_estimate=cost_estimate,
        )(tiles, *operands)

    return call


def shape_of(shape, dtype):
    return jax.ShapeDtypeStruct(shape, dtype)


def cost(flops, read):
    return pl.CostEstimate(flops=int(flops), bytes_accessed=int(read), transcendentals=0)


class Side:
    def __init__(self, terms, order):
        self.terms, self.order = terms, order

    def cols(self):
        _, _, lanes = self.terms[0]
        return lanes.stop - lanes.start


def slab_sums(sides, dims, joined=False, also=None, limit=SMALL_LIMIT):
    first = dims[0]
    places = jnp.stack([dp_place(dim) for dim in dims]).astype(jnp.int32)
    at_of = {dim: index for index, dim in enumerate(dims)}
    lead = 1 if joined else first[0]
    operands, in_specs, plan = [], [], []
    out_shape, out_specs, targets = [], [], []

    def index_map(term_dims, current, step, left):
        def of(grid, at):
            index = []
            for dim in term_dims:
                if dim == first and (dim in left or (dim == current and not joined)):
                    index.append(grid)
                elif dim == current:
                    index.append(lax.rem(at[at_of[dim]] + step, dim[0]))
                else:
                    index.append(0 if dim in left else at[at_of[dim]])
            return (*index, 0, 0)

        return of

    for number, side in enumerate([*sides, *([also] if also else [])]):
        main = number < len(sides)
        current = first if joined and main else side.order[0]
        rows = side.terms[0][0].shape[-2]
        left = [dim for dim in side.terms[-1][1] if dim != current]
        rest = [dim[0] for dim in left if dim != first]
        for step in range(current[0]) if joined else range(1, current[0]):
            ids = []
            shared = ids if current != first or joined or step == 1 else plan[-1][0]
            if shared is ids:
                for array, term_dims, lanes in side.terms:
                    block, pick = [], []
                    for dim in term_dims:
                        whole = dim in left and dim != first
                        block.append(dim[0] if whole else 1)
                        pick.append(slice(None) if whole else 0)
                    ids.append((len(operands), tuple(pick), lanes))
                    operands.append(array)
                    spec = (*block, rows, array.shape[-1])
                    in_specs.append(pl.BlockSpec(spec, index_map(term_dims, current, step, left)))
            plan.append((shared, number, step))
            if joined and main:
                continue
            over = main and not joined
            shape = (lead if over else 1, *rest, rows, side.cols())
            out_shape.append(shape_of(shape, F32 if step == 0 else BF))
            out_specs.append(
                pl.BlockSpec(
                    (1, *shape[1:]), lambda grid, at, n=len(shape), over=over: (grid if over else 0,) + (0,) * (n - 1)
                )
            )
            targets.append((number, step))
    if joined:
        width = sum(side.cols() for side in sides)
        rows = sides[0].terms[0][0].shape[-2]
        for step in range(first[0]):
            out_shape.append(shape_of((rows, width), BF if step else F32))
            out_specs.append(pl.BlockSpec((rows, width), lambda grid, at: (0, 0)))
            targets.append((None, step))
    starts = [sum(side.cols() for side in sides[:number]) for number in range(len(sides))]

    def kernel(places_ref, *refs):
        ins, outs = refs[: len(operands)], refs[len(operands) :]

        def total_of(ids):
            total = None
            for index, pick, lanes in ids:
                value = ins[index][(*pick, slice(None), lanes)].astype(F32)
                total = value if total is None else total + value
            return total

        def keep(out, ids):
            out[0] = total_of(ids).astype(out.dtype)

        for ids, number, step in plan:
            if number >= len(sides):
                out = outs[targets.index((number, step))]
                if also.order[0] == first:
                    here = lax.rem(places_ref[0] + step, first[0])
                else:
                    here = 0
                pl.when(pl.program_id(0) == here)(lambda out=out, ids=ids: keep(out, ids))
            elif joined:
                out = outs[targets.index((None, step))]
                out[:, starts[number] : starts[number] + sides[number].cols()] = total_of(ids).astype(out.dtype)
            else:
                keep(outs[targets.index((number, step))], ids)

    sums = pl.pallas_call(
        kernel,
        grid_spec=pltpu.PrefetchScalarGridSpec(
            num_scalar_prefetch=1, grid=(lead,), in_specs=in_specs, out_specs=out_specs
        ),
        out_shape=out_shape,
        compiler_params=params(limit),
        cost_estimate=cost(0, 8e6),
    )(places, *operands)
    more = [value[0] for value, (which, _) in zip(sums, targets) if which == len(sides)]
    if joined:
        return [value for value, (which, _) in zip(sums, targets) if which is None], more
    lists = [[value for value, (which, _) in zip(sums, targets) if which == number] for number in range(len(sides))]
    return [*lists, more] if also else lists


def adam_moments(grad_value, moment, square):
    moment_new = beta_one * moment + (1.0 - beta_one) * grad_value
    square_new = beta_two * square + (1.0 - beta_two) * grad_value * grad_value
    scaled = (
        moment_new
        / (1.0 - beta_one**STEP)
        / (jnp.sqrt(square_new / (1.0 - beta_two**STEP)) + adam_eps)
    )
    return (moment_new, square_new, scaled)


def square_sum(value):
    return jnp.sum(jnp.sum(value * value, axis=0, keepdims=True), axis=1, keepdims=True)


def note_norms(norms, matrix, weight, update):
    row = lax.broadcasted_iota(jnp.int32, norms.shape, 0)
    lane = lax.broadcasted_iota(jnp.int32, norms.shape, 1)
    here = jnp.where(row == 0, square_sum(weight), square_sum(update))
    return norms + jnp.where(jnp.logical_and(row < 2, lane == matrix), here, 0.0)


def ffn_update_kernel(count, own_ref, rest_ref, *refs):
    states, arrived, outs = refs[:9], refs[9:-13], refs[-13:]
    total, rest = own_ref[...], rest_ref[...]
    for ref in arrived[:count]:
        total = total + ref[...].astype(F32)
    for ref in arrived[count:]:
        rest = rest + ref[...].astype(F32)
    norms = jnp.zeros(outs[12].shape, F32)
    cut = states[6].shape[1] - BLOCK
    grads = (
        rest[:, 3 * BLOCK :],
        jnp.concatenate([total[:, cut:], rest[:, BLOCK : 3 * BLOCK]], axis=1),
        jnp.concatenate([total[:, :cut], rest[:, :BLOCK]], axis=1),
    )
    for index in range(3):
        weight, moment, square = states[3 * index : 3 * index + 3]
        grad = grads[index]
        moment_new, square_new, scaled = adam_moments(grad, moment[...], square[...])
        update = scaled + weight_decay * weight[...]
        for target, value in zip(outs[4 * index :], (grad, moment_new, square_new, update)):
            target[...] = value
        norms = note_norms(norms, 3 + index, weight[...], update)
    outs[12][...] = norms


def qkv_update_kernel(
    own_ref, weight_ref, moment_ref, square_ref, vec_ref, norms_ref, *refs
):
    arrived, (grad_out, moment_out, square_out, update_out, totals_ref) = refs[:-5], refs[-5:]
    cols = weight_ref.shape[2]
    total = own_ref[...]
    for ref in arrived:
        total = total + ref[...].astype(F32)
    rows = vec_ref.shape[0]
    norms = norms_ref[...]
    for index in range(3):
        grad = total[:, index * cols : (index + 1) * cols]
        moment, square, scaled = adam_moments(grad, moment_ref[index], square_ref[index])
        update = scaled + weight_decay * weight_ref[index]
        grad_out[index] = grad
        moment_out[index] = moment
        square_out[index] = square
        update_out[index] = update
        norms = note_norms(norms, index, weight_ref[index], update)
    totals_ref[:rows, :] = vec_ref[...]
    totals_ref[rows:, :] = norms


def finish_kernel(totals_ref, *refs):
    ins, outs = refs[:16], refs[16:]
    rows = totals_ref.shape[0] - 8
    weight_norm = jnp.sqrt(totals_ref[rows : rows + 1, :])
    update_norm = jnp.sqrt(totals_ref[rows + 1 : rows + 2, :])
    trust = weight_norm / update_norm
    lane = lax.broadcasted_iota(jnp.int32, trust.shape, 1)
    outs[12][0:1, :] = trust
    outs[12][1:2, :] = weight_norm
    outs[12][2:3, :] = update_norm

    def step(matrix):
        return learn_rate * jnp.sum(jnp.where(lane == matrix, trust, 0.0), axis=1, keepdims=True)

    for index in range(4):
        update, weight, average = ins[3 * index : 3 * index + 3]
        for piece in range(3 if index == 0 else 1):
            at = (piece,) if index == 0 else (Ellipsis,)
            new = weight[at] - step(piece if index == 0 else index + 2) * update[at]
            outs[2 * index][at] = new
            outs[2 * index + 1][at] = ema_keep * average[at] + (1.0 - ema_keep) * new
    vectors, moment, square, average = ins[12:16]
    grad = totals_ref[:rows, :]
    moment_new, square_new, scaled = adam_moments(grad, moment[...], square[...])
    new = vectors[...] - vector_rate * scaled
    outs[8][...] = moment_new
    outs[9][...] = square_new
    outs[10][...] = new
    outs[11][...] = ema_keep * average[...] + (1.0 - ema_keep) * new


def shards(
    tokens, lengths, send_order, pooled_grad,
    qkv_weight, out_weight, in_weight, down_weight, vectors,
    qkv_moment, out_moment, in_moment, down_moment, vec_moment,
    qkv_square, out_square, in_square, down_square, vec_square,
    qkv_average, out_average, in_average, down_average, vec_average,
):
    core = lax.axis_index("mp")
    count = lax.axis_size("dp")
    dims = dp_dims(count)
    sents, span, width = tokens.shape
    half = width // 2
    mine = sents // 2
    most = mine * span
    shard_rows = qkv_weight.shape[1]
    core_word = core.reshape(1).astype(jnp.int32)

    def flip(value):
        return jnp.where(core == 0, value, value[::-1])

    chunk = jnp.concatenate([qkv_weight[0], qkv_weight[1], qkv_weight[2], out_weight.T], axis=1)
    first, others = dims[0], dims[1:]
    orders = (others, others[::-1])
    sides = (0, 1)

    def gather_start(pieces):
        value = arrange(pieces, first, 0)
        cols = value.shape[-1] // 2
        return [
            (value[..., side * cols : (side + 1) * cols], [first], orders[side]) for side in sides
        ]

    def gather_out(state):
        return [gather_send(value, order[0]) if order else [value] for value, _, order in state]

    def gather_in(state, pieces):
        after = []
        for (value, done, order), come in zip(state, pieces):
            if order:
                axis = sum(1 for other in done if other[1] > order[0][1])
                value = arrange(come, order[0], axis)
                done = done + [order[0]]
            after.append((value, done, order[1:]))
        return after

    def gather_end(state):
        return [value.reshape(width, -1) for value, _, _ in state]

    share = sents // count
    if share % 2 == 0:
        own = lax.dynamic_index_in_dim(
            pooled_grad.reshape(count, share // 2, 2, width), core, 2, keepdims=False
        )
        pair_grad = lax.all_to_all(own, "dp", 0, 0, tiled=True).reshape(mine, width)
    else:
        own = lax.all_to_all(pooled_grad, "dp", 0, 0, tiled=True)
        pair_grad = lax.dynamic_index_in_dim(
            own.reshape(mine, 2, width), core, 1, keepdims=False
        )

    pieces0 = gather_send(chunk.astype(BF), first)
    qkvo = gather_start(pieces0)
    pieces0 = gather_out(qkvo)
    own, held = lax.optimization_barrier((in_weight, [pieces[0] for pieces in pieces0]))
    pieces1 = gather_send(own.astype(BF), first)
    pieces0, pieces1, pair_grad = lax.optimization_barrier((pieces0, pieces1, pair_grad))
    qkvo = gather_in(qkvo, pieces0)
    pieces0 = gather_out(qkvo)
    held = [pieces[0] for pieces in pieces0]
    own, held = lax.optimization_barrier((down_weight, held))
    pieces2 = gather_send(own.T.astype(BF), first)

    order_word, _ = lax.optimization_barrier((send_order, [pieces[0] for pieces in pieces0]))
    packed = pl.pallas_call(
        pack_kernel,
        out_shape=(
            shape_of((most, width), BF),
            shape_of((most, BLOCK), F32),
            shape_of((2, mine), jnp.int32),
            shape_of((1,), jnp.int32),
        ),
        in_specs=[SMEM_SPEC, SMEM_SPEC, SMEM_SPEC, VMEM_SPEC],
        out_specs=(VMEM_SPEC, VMEM_SPEC, SMEM_SPEC, SMEM_SPEC),
        scratch_shapes=[pltpu.VMEM((most, BLOCK), F32)] * (width // BLOCK),
        compiler_params=params(),
        cost_estimate=cost(0, 30e6),
    )(core_word, order_word, lengths, tokens)
    packed, pieces0, pieces2 = lax.optimization_barrier((packed, pieces0, pieces2))
    rows, seg, offsets, tiles = packed
    full = jnp.concatenate(gather_end(gather_in(qkvo, pieces0)), axis=1)
    full = (full, swap_core(full))
    weights = (full[0], full[0], full[1], full[1])
    ffn = [
        (arrange(pieces, first, 0), [first], orders[side]) for side, pieces in enumerate((pieces1, pieces2))
    ]
    ffn = gather_in(ffn, gather_out(ffn))
    ffn_pieces = gather_out(ffn)

    own_order = lax.dynamic_index_in_dim(send_order.reshape(mine, 2), core, 1, keepdims=False)
    own_count = lengths[own_order].astype(F32)[:, None]
    back = jnp.pad(pair_grad / own_count, ((0, BLOCK - mine), (0, 0)))
    back_high = back.astype(BF)
    back_rest = (back - back_high.astype(F32)).astype(BF)
    weight_specs = [column_spec(width, 0), column_spec(width, 1)] * 2
    long_spec = held_spec(width, 2 * width)
    vec_spec = held_spec(1, vectors.shape[0])
    vec_row = vectors.reshape(1, -1)
    row_total = most * 0.6
    mids = [pieces[0] for pieces in ffn_pieces]
    tiles, mids, _, _ = lax.optimization_barrier((tiles, mids, back_high, back_rest))
    qkv, att, normed, inverse = tiled_call(
        attn_forward_kernel,
        out_shape=(
            shape_of((most, 3 * width), BF),
            shape_of((most, width), BF),
            shape_of((most, width), F32),
            shape_of((most, BLOCK), F32),
        ),
        in_specs=[SMEM_SPEC, tile_spec(width), tile_spec(BLOCK), vec_spec] + weight_specs,
        out_specs=(tile_spec(3 * width), tile_spec(width), tile_spec(width), tile_spec(BLOCK)),
        scratch_shapes=[],
        cost_estimate=cost(2 * row_total * 4 * width * width * 2, 30e6),
    )(tiles, most, core_word, rows, seg, vec_row, *weights)
    normed, ffn_pieces = lax.optimization_barrier((normed, ffn_pieces))

    w1, w2 = [(value, swap_core(value)) for value in gather_end(gather_in(ffn, ffn_pieces))]
    down_shape = shape_of((width, 2 * width - BLOCK), BF)
    in_shape = shape_of((width, 2 * width - 2 * BLOCK), BF)
    rest_shape = shape_of((width, half + 3 * BLOCK), BF)
    (
        grad_one, emb, vec_ffn, down_own, down_other, in_own, in_other, rest_own, rest_other,
    ) = tiled_call(
        ffn_kernel,
        out_shape=(
            shape_of((most, width), F32),
            shape_of((mine, width), F32),
            shape_of((8, vectors.shape[0]), F32),
            down_shape,
            down_shape,
            in_shape,
            in_shape,
            rest_shape,
            rest_shape,
        ),
        in_specs=[
            SMEM_SPEC, tile_spec(width), tile_spec(BLOCK), tile_spec(BLOCK), tile_spec(width), vec_spec,
        ]
        + [held_spec(BLOCK, width)] * 2
        + [long_spec] * 4,
        out_specs=(tile_spec(width), held_spec(mine, width), held_spec(8, vectors.shape[0])) + (HBM_SPEC,) * 6,
        scratch_shapes=[
            pltpu.VMEM((4, width, width), F32),
            pltpu.VMEM((4, width, width), F32),
            pltpu.VMEM((2, width, half), F32),
            pltpu.VMEM((4, TILE, width), BF),
            pltpu.VMEM((4, TILE, width), F32),
            pltpu.VMEM((BLOCK, width), F32),
            pltpu.VMEM((BLOCK, BLOCK), F32),
            pltpu.VMEM((10, width, width), BF),
            pltpu.SemaphoreType.DMA((10, 2)),
        ],
        cost_estimate=cost(2 * row_total * 24 * width * width, 30e6),
    )(
        tiles, most, core_word, normed, inverse, seg, att, vec_row, back_high, back_rest, *w1, *w2
    )

    def scatter_start(parts):
        sides = []
        for side, (lanes, *arrays) in enumerate(parts):
            terms = [
                (array.reshape(*[size for size, _ in dims], shard_rows, -1), list(dims), lanes)
                for array in arrays
            ]
            sides.append(Side(terms, orders[side][::-1]))
        return sides

    def scatter_out(sides, limit=SMALL_LIMIT, also=None):
        if len({side.order[0][0] for side in sides}) == 1:
            return slab_sums(sides, dims, also=also, limit=limit)
        heads = [slab_sums([side], dims, limit=limit)[0] for side in sides[:-1]]
        return heads + slab_sums(sides[-1:], dims, also=also, limit=limit)

    def scatter_go(sides, slabs):
        return [scatter_send(sent, side.order[0]) for side, sent in zip(sides, slabs)]

    def scatter_in(sides, arrived):
        after = []
        for side, come in zip(sides, arrived):
            left = [dim for dim in side.terms[-1][1] if dim != side.order[0]]
            new = [(array, left, slice(0, side.cols())) for array in come]
            after.append(Side(side.terms + new, side.order[1:]))
        return after

    def go_pooled(value):
        return lax.all_to_all(value, "dp", 0, 0, tiled=True)

    come = [swap_core(down_other), swap_core(in_other), swap_core(rest_other)]
    grad_send = scatter_start(
        ((slice(0, down_shape.shape[1]), down_own, come[0]), (slice(0, in_shape.shape[1]), in_own, come[1]))
    )
    (rest_send,) = scatter_start(((slice(0, rest_shape.shape[1]), rest_own, come[2]),))
    rest_send.order = dims[:1] + others[::-1]
    *slabs, rest_slabs = scatter_out(grad_send, VMEM_LIMIT, rest_send)
    pooled = go_pooled(emb.reshape(count, share // 2, width)) if share % 2 == 0 else emb
    tiles, slabs, rest_slabs, pooled = lax.optimization_barrier((tiles, slabs, rest_slabs, pooled))
    qkv_shape = shape_of((width, 3 * half), BF)
    dx_mine, dx_other, vec_local, own, other = tiled_call(
        attn_backward_kernel,
        out_shape=(
            shape_of((most, half), F32),
            shape_of((most, half), BF),
            shape_of((vectors.shape[0] // BLOCK, BLOCK), F32),
            qkv_shape,
            qkv_shape,
        ),
        in_specs=[
            SMEM_SPEC, tile_spec(width), tile_spec(width), tile_spec(3 * width), tile_spec(BLOCK),
            held_spec(8, vectors.shape[0]),
        ]
        + weight_specs,
        out_specs=(tile_spec(half), tile_spec(half), held_spec(vectors.shape[0] // BLOCK, BLOCK))
        + (HBM_SPEC,) * 2,
        scratch_shapes=[
            pltpu.VMEM((TILE, 3 * width), BF),
            pltpu.VMEM((TILE, width), F32),
            pltpu.VMEM((8, vectors.shape[0]), F32),
            pltpu.VMEM((2, width, 3 * half), F32),
            pltpu.VMEM((2, width, 3 * half), BF),
            pltpu.SemaphoreType.DMA((2, 1)),
        ],
        cost_estimate=cost(2 * row_total * 18 * width * width, 30e6),
    )(tiles, most, core_word, grad_one, rows, qkv, seg, vec_ffn, *weights)
    arrived, rest_arrived, own, other, dx_other = lax.optimization_barrier(
        (scatter_go(grad_send, slabs), scatter_go([rest_send], [rest_slabs]), own, other, dx_other)
    )
    grad_send = scatter_in(grad_send, arrived)
    (rest_send,) = scatter_in([rest_send], rest_arrived)
    *slabs, rest_slabs = scatter_out(grad_send, VMEM_LIMIT, rest_send)
    come = swap_core(other)
    own, come, slabs, rest_slabs = lax.optimization_barrier((own, come, slabs, rest_slabs))
    cut = 3 * half // (2 * BLOCK) * BLOCK
    qkv_send = scatter_start(((slice(0, cut), own, come), (slice(cut, 3 * half), own, come)))
    qkv_slabs = scatter_out(qkv_send)
    order_word, slabs = lax.optimization_barrier((send_order, slabs))

    tokens_grad = pl.pallas_call(
        unpack_kernel,
        out_shape=shape_of((sents, span, half), F32),
        in_specs=[SMEM_SPEC] * 4 + [VMEM_SPEC] * 2,
        out_specs=VMEM_SPEC,
        scratch_shapes=[pltpu.VMEM((most, BLOCK), F32)] * (2 * half // BLOCK),
        compiler_params=params(),
        cost_estimate=cost(0, 20e6),
    )(core_word, order_word, lengths, offsets, dx_mine, swap_core(dx_other))
    arrived, rest_arrived, tokens_grad, qkv_slabs = lax.optimization_barrier(
        (scatter_go(grad_send, slabs), scatter_go([rest_send], [rest_slabs]), tokens_grad, qkv_slabs)
    )
    grad_send = scatter_in(grad_send, arrived)
    (rest_send,) = scatter_in([rest_send], rest_arrived)
    (ffn_grad, *slabs), (rest_grad, *rest_slabs) = slab_sums(
        grad_send, dims, joined=True, also=rest_send, limit=VMEM_LIMIT
    )
    qkv_slabs, slabs = lax.optimization_barrier((qkv_slabs, slabs))
    last_go = scatter_send(slabs, first)
    go = scatter_go(qkv_send, qkv_slabs)
    qkv_send = scatter_in(qkv_send, go)
    while qkv_send[0].order:
        go = scatter_go(qkv_send, scatter_out(qkv_send))
        go, last_go, pooled, rest_slabs = lax.optimization_barrier((go, last_go, pooled, rest_slabs))
        qkv_send = scatter_in(qkv_send, go)
    rest_go = scatter_send(rest_slabs, rest_send.order[0])
    (qkv_grad, *slabs), _ = slab_sums(qkv_send, dims, joined=True)
    go = scatter_send(slabs, first)

    both = [pooled, swap_core(pooled)]
    go, both = lax.optimization_barrier((go, both))
    ffn_states = [
        (out_weight.T, out_moment.T, out_square.T),
        (in_weight, in_moment, in_square),
        (down_weight.T, down_moment.T, down_square.T),
    ]
    shapes = [shape_of(state[0].shape, F32) for state in ffn_states for _ in range(4)]
    *ffn_new, norms = pl.pallas_call(
        functools.partial(ffn_update_kernel, len(last_go)),
        out_shape=shapes + [shape_of((8, BLOCK), F32)],
        in_specs=[VMEM_SPEC] * (11 + len(last_go) + len(rest_go)),
        out_specs=[VMEM_SPEC] * 13,
        compiler_params=params(SMALL_LIMIT),
        cost_estimate=cost(0, 4e6),
    )(ffn_grad, rest_grad, *[value for state in ffn_states for value in state], *last_go, *rest_go)
    out_grad, out_m, out_s, out_u, in_grad, in_m, in_s, in_u, down_grad, down_m, down_s, down_u = ffn_new
    lines = vectors.shape[0] // BLOCK
    like = [shape_of(qkv_weight.shape, F32)]
    qkv_grad, qkv_m, qkv_s, qkv_u, totals = pl.pallas_call(
        qkv_update_kernel,
        out_shape=like * 4 + [shape_of((lines + 8, BLOCK), F32)],
        in_specs=[VMEM_SPEC] * (6 + len(go)),
        out_specs=[VMEM_SPEC] * 5,
        compiler_params=params(SMALL_LIMIT),
        cost_estimate=cost(0, 4e6),
    )(qkv_grad, qkv_weight, qkv_moment, qkv_square, vec_local, norms, *go)
    totals, both = lax.optimization_barrier((totals, both))
    both = flip(jnp.stack(both))
    if share % 2 == 0:
        pooled = jnp.moveaxis(both, 0, 2).reshape(sents, width)
    else:
        both = jnp.moveaxis(both, 0, 1).reshape(sents, width)
        pooled = go_pooled(both)

    totals = sum_all(totals, dims)
    states = [
        (qkv_u, qkv_weight, qkv_average),
        (out_u, out_weight.T, out_average.T),
        (in_u, in_weight, in_average),
        (down_u, down_weight.T, down_average.T),
    ]
    pieces = [value.reshape(lines, BLOCK) for value in (vectors, vec_moment, vec_square, vec_average)]
    shapes = [shape_of(update.shape, F32) for update, _, _ in states for _ in range(2)]
    shapes += [shape_of((lines, BLOCK), F32)] * 4 + [shape_of((8, BLOCK), F32)]
    (
        new_qkv, qkv_a, new_out, out_a, new_in, in_a, new_down, down_a, vec_m, vec_s, new_vec, vec_a, ratios,
    ) = pl.pallas_call(
        finish_kernel,
        out_shape=shapes,
        in_specs=[VMEM_SPEC] * 17,
        out_specs=[VMEM_SPEC] * len(shapes),
        compiler_params=params(SMALL_LIMIT),
        cost_estimate=cost(0, 4e6),
    )(totals, *[value for state in states for value in state], *pieces)
    vec_grad, vec_m, vec_s, new_vec, vec_a = [
        value.reshape(-1) for value in (totals[:lines], vec_m, vec_s, new_vec, vec_a)
    ]
    trust_ratio, weight_norm, update_norm = [ratios[index, :6] for index in range(3)]
    out_grad, out_m, out_s, new_out, out_a = [value.T for value in (out_grad, out_m, out_s, new_out, out_a)]
    down_grad, down_m, down_s, new_down, down_a = [
        value.T for value in (down_grad, down_m, down_s, new_down, down_a)
    ]
    return (
        pooled, tokens_grad, qkv_grad, out_grad, in_grad, down_grad, vec_grad,
        trust_ratio, weight_norm, update_norm,
        qkv_m, out_m, in_m, down_m, vec_m,
        qkv_s, out_s, in_s, down_s, vec_s,
        new_qkv, new_out, new_in, new_down, new_vec,
        qkv_a, out_a, in_a, down_a, vec_a,
    )


def solution(mesh):
    matrices = (P(None, "dp", "mp"), P("mp", "dp"), P("dp", "mp"), P("mp", "dp"), P())
    return jax.shard_map(
        shards,
        mesh=mesh,
        in_specs=(P("dp", None, None), P("dp"), P("dp"), P("dp", None)) + matrices * 4,
        out_specs=(P("dp", None), P("dp", None, "mp")) + matrices + (P(), P(), P()) + matrices * 4,
        check_vma=False,
    )
```

```python
import functools

import jax
import jax.numpy as jnp
from jax import lax
from jax.experimental import pallas as pl
from jax.experimental.pallas import tpu as pltpu
from jax.sharding import PartitionSpec as P

HEAD = 64
STEP = 10
TILE = 256
BLOCK = 128
GROUP = 6

beta_one = 0.9
beta_two = 0.999
adam_eps = 1e-06
weight_decay = 0.01
learn_rate = 0.3
vector_rate = 0.05
ema_keep = 0.9
norm_eps = 1e-12
masked_score = -1000000000.0
gelu_in = 0.7978845608028654
gelu_cube = 0.044715

BF = jnp.bfloat16
F32 = jnp.float32
VMEM_LIMIT = 62 * 1024 * 1024
SMALL_LIMIT = 14 * 1024 * 1024


def dp_dims(count):
    known = {16: ((4, 4), (2, 2), (2, 1)), 128: ((4, 32), (8, 4), (4, 1))}
    return known.get(count, ((count, 1),))


def dp_shift(value, dim, step):
    size, stride = dim
    count = lax.axis_size("dp")
    pairs = []
    for index in range(count):
        place = index // stride % size
        pairs.append((index, index + ((place + step) % size - place) * stride))
    return lax.ppermute(value, "dp", pairs)


def dp_place(dim):
    size, stride = dim
    return lax.rem(lax.div(lax.axis_index("dp"), stride), size)


def swap_core(value):
    return lax.ppermute(value, "mp", [(0, 1), (1, 0)])


def arrange(pieces, dim, axis):
    size, _ = dim
    place = dp_place(dim)
    if size == 2:
        return jnp.where(place == 0, jnp.stack(pieces, axis), jnp.stack(pieces[::-1], axis))
    ordered = []
    for target in range(size):
        which = lax.rem(target - place + size, size)
        chosen = pieces[0]
        for step in range(1, size):
            chosen = jnp.where(which == step, pieces[step], chosen)
        ordered.append(chosen)
    return jnp.stack(ordered, axis)


def gather_send(value, dim):
    return [value] + [dp_shift(value, dim, -step) for step in range(1, dim[0])]


def scatter_send(slabs, dim):
    return [dp_shift(slab, dim, step) for step, slab in enumerate(slabs, 1)]


def sum_all(value, dims):
    value = value + swap_core(value)
    count = lax.axis_size("dp")
    for size, stride in dims:
        bit = 1
        while bit < size:
            pairs = []
            for index in range(count):
                place = index // stride % size
                pairs.append((index, index + ((place ^ bit) - place) * stride))
            value = value + lax.ppermute(value, "dp", pairs)
            bit *= 2
    return value


def dot_nn(left, right):
    return jnp.dot(left, right, preferred_element_type=F32)


def dot_nt(left, right):
    return lax.dot_general(left, right, (((1,), (1,)), ((), ())), preferred_element_type=F32)


def dot_tn(left, right):
    return lax.dot_general(left, right, (((0,), (0,)), ((), ())), preferred_element_type=F32)


def vec_at(index, width, core=None, part=0, cols=None):
    if core is None:
        return slice(index * width, (index + 1) * width)
    which = core if part == 0 else 1 - core
    return pl.ds(pl.multiple_of(index * width + which * cols, BLOCK), cols)


def column_sums(value):
    rows, cols = value.shape
    return jnp.sum(value.reshape(rows // 8, 8, cols), axis=0)


def pack_kernel(
    core_ref, order_ref, len_ref, tok_ref, rows_ref, seg_ref, off_ref, tiles_ref, *stage
):
    core = core_ref[0]
    half = order_ref.shape[0] // 2
    total = rows_ref.shape[0]

    def clear(step, carry):
        rows = pl.ds(pl.multiple_of(step * BLOCK, BLOCK), BLOCK)
        for column in stage:
            column[rows, :] = jnp.zeros((BLOCK, BLOCK), F32)
        seg_ref[rows, :] = jnp.full((BLOCK, BLOCK), -1.0, F32)
        return carry

    lax.fori_loop(0, total // BLOCK, clear, 0)

    def choose(carry, parity):
        cursor, short, long = carry
        inside = cursor & (BLOCK - 1)
        room = BLOCK - inside
        fits = len_ref[order_ref[2 * long + parity]] <= room
        takes = jnp.logical_and(
            jnp.logical_not(fits), len_ref[order_ref[2 * short + parity]] <= room
        )
        slot = jnp.where(takes, short, long)
        start = jnp.where(jnp.logical_or(fits, takes), cursor, cursor + room)
        sentence = order_ref[2 * slot + parity]
        count = len_ref[sentence]
        left = (start + count, jnp.where(takes, short + 1, short), jnp.where(takes, long, long - 1))
        return slot, sentence, count, start, left

    def place(step, carry):
        slot, sentence, count, start, carry = choose(carry, core)
        off_ref[0, slot] = start
        span = tok_ref.shape[1]
        value = tok_ref[sentence].astype(F32)
        for index, column in enumerate(stage):
            column[pl.ds(start, span), :] = value[:, index * BLOCK : (index + 1) * BLOCK]
        row = lax.broadcasted_iota(jnp.int32, (span, BLOCK), 0)
        seg_ref[pl.ds(start, span), :] = jnp.where(row < count, slot.astype(F32), -1.0)
        return carry

    def partner(step, carry):
        slot, _, _, start, carry = choose(carry, 1 - core)
        off_ref[1, slot] = start
        return carry

    begin = (jnp.int32(0), jnp.int32(0), jnp.int32(half - 1))
    used, _, _ = lax.fori_loop(0, half, place, begin)
    tiles_ref[0] = (used + TILE - 1) // TILE
    lax.fori_loop(0, half, partner, begin)

    def low(step, carry):
        rows = pl.ds(pl.multiple_of(step * BLOCK, BLOCK), BLOCK)
        for index, column in enumerate(stage):
            rows_ref[rows, index * BLOCK : (index + 1) * BLOCK] = column[rows, :].astype(BF)
        return carry

    lax.fori_loop(0, total // BLOCK, low, 0)


def head_masks():
    lane = lax.broadcasted_iota(jnp.int32, (1, 2 * HEAD), 1)
    first = jnp.where(lane < HEAD, 1.0, 0.0)
    return first.astype(BF), (1.0 - first).astype(BF)


def two_heads(value, masks):
    return jnp.concatenate([value * masks[0], value * masks[1]], axis=0)


def same_sentence(seg):
    across = jnp.transpose(seg)
    return jnp.concatenate([seg, seg], axis=1) == jnp.concatenate([across, across], axis=1)


def softmax_rows(scores, mask):
    scores = jnp.where(mask, scores, masked_score)
    expon = jnp.exp(scores - jnp.max(scores, axis=0, keepdims=True))
    return expon * (1.0 / jnp.sum(expon, axis=0, keepdims=True))


def one_above_other(value):
    return jnp.concatenate([value[:, :BLOCK], value[:, BLOCK:]], axis=0)


def attn_forward_kernel(
    last, core_ref, rows_ref, seg_ref, vec_ref, qk0, vo0, qk1, vo1, qkv_ref, att_ref, norm_ref, inv_ref
):
    width = rows_ref.shape[1]
    half = width // 2
    core = core_ref[0]
    rows = rows_ref[...]
    weights = ((qk0, vo0), (qk1, vo1))
    for part, (qk, vo) in enumerate(weights):
        base = part * 3 * half
        value = dot_nn(rows, qk[...])
        query = value[:, :half] + vec_ref[:, vec_at(0, width, core, part, half)]
        qkv_ref[:, base : base + half] = query.astype(BF)
        qkv_ref[:, base + half : base + width] = value[:, half:].astype(BF)
        value = dot_nn(rows, vo[:, :half]) + vec_ref[:, vec_at(1, width, core, part, half)]
        qkv_ref[:, base + width : base + 3 * half] = value.astype(BF)
    masks = head_masks()
    for block in range(TILE // BLOCK):
        span = slice(block * BLOCK, (block + 1) * BLOCK)
        mask = same_sentence(seg_ref[span, :])
        for part in range(2):
            for pair in range(half // (2 * HEAD)):
                at = part * 3 * half + pair * 2 * HEAD
                query = qkv_ref[span, at : at + 2 * HEAD] * BF(HEAD**-0.5)
                key = qkv_ref[span, at + half : at + half + 2 * HEAD]
                value = qkv_ref[span, at + width : at + width + 2 * HEAD]
                probs = softmax_rows(dot_nt(key, two_heads(query, masks)), mask).astype(BF)
                mixed = dot_tn(one_above_other(probs), two_heads(value, masks))
                to = part * half + pair * 2 * HEAD
                att_ref[span, to : to + 2 * HEAD] = mixed.astype(BF)
    mixed = dot_nt(att_ref[:, :half], vo0[:, half:]) + dot_nt(att_ref[:, half:], vo1[:, half:])
    pre = rows.astype(F32) + (mixed + vec_ref[:, vec_at(2, width)])
    centre = pre - jnp.mean(pre, axis=-1, keepdims=True)
    inverse = lax.rsqrt(jnp.mean(centre * centre, axis=-1, keepdims=True) + norm_eps)
    norm_ref[...] = centre * inverse
    inv_ref[...] = jnp.broadcast_to(inverse, inv_ref.shape)


def norm_back(grad, normed, inverse, gain):
    scaled = grad * gain
    first = jnp.mean(scaled, axis=-1, keepdims=True)
    second = jnp.mean(scaled * normed, axis=-1, keepdims=True)
    return (scaled - first - normed * second) * inverse


def hidden_pieces(core, width):
    return [
        pl.ds(
            pl.multiple_of(8 * width + (2 * (core if part < 2 else 1 - core) + part % 2) * width, BLOCK),
            width,
        )
        for part in range(4)
    ]


def ffn_kernel(
    last, core_ref, norm_ref, inv_ref, seg_ref, att_ref, vec_ref, high_ref, low_ref,
    w1_own, w1_other, w2_own, w2_other,
    grad_ref, emb_ref, sums_ref, down_own, down_other, in_own, in_other, rest_own, rest_other,
    sum1, sum2, sum3, act, slope, emb, counts, stage, sems,
):
    step = pl.program_id(0)
    width = norm_ref.shape[1]
    half = width // 2
    lanes = [slice(part % 2 * width, (part % 2 + 1) * width) for part in range(4)]
    w1 = [(w1_own, w1_other)[part // 2].at[:, lanes[part]] for part in range(4)]
    w2 = [(w2_own, w2_other)[part // 2].at[:, lanes[part]] for part in range(4)]
    hidden_at = hidden_pieces(core_ref[0], width)

    @pl.when(step == 0)
    def _():
        emb[...] = jnp.zeros_like(emb)
        counts[...] = jnp.zeros_like(counts)
        sums_ref[...] = jnp.zeros_like(sums_ref)

    gain_one, shift_one = vec_ref[:, vec_at(4, width)], vec_ref[:, vec_at(5, width)]
    gain_two, shift_two = vec_ref[:, vec_at(6, width)], vec_ref[:, vec_at(7, width)]
    bias_ffn = vec_ref[:, vec_at(3, width)]
    hidden_low = (norm_ref[...] * gain_one + shift_one).astype(BF)
    for part in range(4):
        pre = dot_nn(hidden_low, w1[part][...]) + vec_ref[:, hidden_at[part]]
        square = pre * pre
        tanh = jnp.tanh(pre * (gelu_in + gelu_in * gelu_cube * square))
        gate = 0.5 + 0.5 * tanh
        out = pre * gate
        act[part] = out.astype(BF)
        slope[part] = gate + out * (1.0 - tanh) * (gelu_in + 3.0 * gelu_in * gelu_cube * square)
    total = dot_nt(act[0], w2[0][...])
    for part in range(1, 4):
        total = total + dot_nt(act[part], w2[part][...])
    pre = (norm_ref[...] * gain_one + shift_one) + (total + bias_ffn)
    centre = pre - jnp.mean(pre, axis=-1, keepdims=True)
    inverse = lax.rsqrt(jnp.mean(centre * centre, axis=-1, keepdims=True) + norm_eps)
    normed = centre * inverse
    final = normed * gain_two + shift_two
    final_high = final.astype(BF)
    final_rest = (final - final_high.astype(F32)).astype(BF)
    seg = seg_ref[...]
    lane = lax.broadcasted_iota(jnp.int32, seg.shape, 1).astype(F32)
    pick = jnp.where(seg == lane, 1.0, 0.0)
    pick_across = jnp.transpose(pick).astype(BF)
    pick = pick.astype(BF)
    emb[...] += dot_nn(pick_across, final_high) + dot_nn(pick_across, final_rest)
    counts[...] += dot_nn(pick_across, jnp.ones((TILE, BLOCK), BF))
    back = dot_nn(pick, high_ref[...]) + dot_nn(pick, low_ref[...])
    sums_ref[:, vec_at(6, width)] += column_sums(back * normed)
    sums_ref[:, vec_at(7, width)] += column_sums(back)
    grad_two = norm_back(back, normed, inverse, gain_two)
    ffn_low = grad_two.astype(BF)
    sums_ref[:, vec_at(3, width)] += column_sums(ffn_low.astype(F32))
    grad_hidden, pres = grad_two, []
    for part in range(4):
        grad_act = dot_nn(ffn_low, w2[part][...])
        grad_pre = (grad_act * slope[part]).astype(BF)
        sums_ref[:, hidden_at[part]] += column_sums(grad_pre.astype(F32))
        grad_hidden = grad_hidden + dot_nt(grad_pre, w1[part][...])
        pres.append(grad_pre)
    normed_one = norm_ref[...]
    sums_ref[:, vec_at(4, width)] += column_sums(grad_hidden * normed_one)
    sums_ref[:, vec_at(5, width)] += column_sums(grad_hidden)
    grad_one = norm_back(grad_hidden, normed_one, inv_ref[:, :1], gain_one)
    grad_ref[...] = grad_one
    grad_low = grad_one.astype(BF)
    sums_ref[:, vec_at(2, width)] += column_sums(grad_low.astype(F32))

    fresh = step == 0
    rest = (rest_own, rest_other)
    places, at = [], 0
    for outs, sums in (((down_own, down_other), sum2), ((in_own, in_other), sum1)):
        cut = outs[0].shape[1] - width
        for index in (2, 3, 0, 1):
            out = outs[index // 2]
            if index % 2 == 0:
                targets = [(0, out.at[:, pl.ds(0, width)])]
            else:
                targets = [(0, out.at[:, pl.ds(width, cut)]), (cut, rest[index // 2].at[:, pl.ds(at, width - cut)])]
            places.append((sums.at[index], targets))
        at += width - cut
    for index in (1, 0):
        places.append((sum3.at[index], [(0, rest[index].at[:, pl.ds(at, half)])]))
    for part in range(4):
        sum2[part] = jnp.where(fresh, 0.0, sum2[part]) + dot_tn(ffn_low, act[part])
    pl.when(last)(lambda: store_sums(places[:4], stage, sems))
    for part in range(4):
        sum1[part] = jnp.where(fresh, 0.0, sum1[part]) + dot_tn(hidden_low, pres[part])
    for part in range(2):
        sum3[part] = jnp.where(fresh, 0.0, sum3[part]) + dot_tn(
            grad_low, att_ref[:, part * half : (part + 1) * half]
        )

    @pl.when(last)
    def _():
        store_sums(places[4:], stage, sems, 4)
        stores_done(places, stage, sems)
        held = emb_ref.shape[0]
        number = jnp.maximum(counts[:held], 1.0)
        emb_ref[...] = emb[:held] / jnp.concatenate([number] * (width // BLOCK), axis=1)


def attn_backward_kernel(
    last, core_ref, grad_ref, rows_ref, qkv_ref, seg_ref, before_ref, qk0, vo0, qk1, vo1,
    mine_ref, dx_ref, total_ref, own, other, dqkv_ref, dx, sums, weights, stage, sems,
):
    width = grad_ref.shape[1]
    half = width // 2
    core = core_ref[0]

    @pl.when(pl.program_id(0) == 0)
    def _():
        sums[...] = before_ref[...]

    grad_low = grad_ref[...].astype(BF)
    masks = head_masks()
    mask = [same_sentence(seg_ref[b * BLOCK : (b + 1) * BLOCK, :]) for b in range(TILE // BLOCK)]
    for part, vo in enumerate((vo0, vo1)):
        base = part * 3 * half
        grad_att = dot_nn(grad_low, vo[:, half:]).astype(BF)
        units = [(block, pair) for block in range(TILE // BLOCK) for pair in range(half // (2 * HEAD))]
        for start in range(0, len(units), GROUP):
            group = units[start : start + GROUP]
            spans = [slice(block * BLOCK, (block + 1) * BLOCK) for block, _ in group]
            ats = [pair * 2 * HEAD for _, pair in group]
            query_at = [slice(base + at, base + at + 2 * HEAD) for at in ats]
            key_at = [slice(base + half + at, base + half + at + 2 * HEAD) for at in ats]
            value_at = [slice(base + width + at, base + width + at + 2 * HEAD) for at in ats]
            each = range(len(group))
            query_two = [
                two_heads(qkv_ref[spans[i], query_at[i]] * BF(HEAD**-0.5), masks) for i in each
            ]
            att_two = [two_heads(grad_att[spans[i], ats[i] : ats[i] + 2 * HEAD], masks) for i in each]
            scores = [dot_nt(qkv_ref[spans[i], key_at[i]], query_two[i]) for i in each]
            grad_probs = [dot_nt(qkv_ref[spans[i], value_at[i]], att_two[i]) for i in each]
            probs = [softmax_rows(scores[i], mask[group[i][0]]) for i in each]
            for i in each:
                dqkv_ref[spans[i], value_at[i]] = dot_nn(probs[i].astype(BF), att_two[i]).astype(BF)
            inner = [jnp.sum(grad_probs[i] * probs[i], axis=0, keepdims=True) for i in each]
            grad_scores = [(probs[i] * (grad_probs[i] - inner[i])).astype(BF) for i in each]
            for i in each:
                dqkv_ref[spans[i], key_at[i]] = dot_nn(grad_scores[i], query_two[i]).astype(BF)
            for i in each:
                key_two = two_heads(qkv_ref[spans[i], key_at[i]], masks)
                grad_query = dot_tn(one_above_other(grad_scores[i]), key_two) * HEAD**-0.5
                dqkv_ref[spans[i], query_at[i]] = grad_query.astype(BF)
        sums[:, vec_at(0, width, core, part, half)] += column_sums(
            dqkv_ref[:, base : base + half].astype(F32)
        )
        sums[:, vec_at(1, width, core, part, half)] += column_sums(
            dqkv_ref[:, base + width : base + 3 * half].astype(F32)
        )

    rows = rows_ref[...]
    total = grad_ref[...]
    for part, (qk, vo) in enumerate(((qk0, vo0), (qk1, vo1))):
        base = part * 3 * half
        total = total + dot_nt(dqkv_ref[:, base : base + width], qk[...])
        total = total + dot_nt(dqkv_ref[:, base + width : base + 3 * half], vo[:, :half])
    dx[...] = total
    mine_ref[...] = dx[:, pl.ds(pl.multiple_of(core * half, half), half)]
    dx_ref[...] = dx[:, pl.ds(pl.multiple_of((1 - core) * half, half), half)].astype(BF)
    for part in range(2):
        before = jnp.where(pl.program_id(0) == 0, 0.0, weights[part])
        weights[part] = before + dot_tn(rows, dqkv_ref[:, part * 3 * half : (part + 1) * 3 * half])

    @pl.when(last)
    def _():
        places = [(weights.at[1], [(0, other)]), (weights.at[0], [(0, own)])]
        store_sums(places, stage, sems)
        for row in range(total_ref.shape[0]):
            lanes = sums[:, row * BLOCK : (row + 1) * BLOCK]
            total_ref[row : row + 1, :] = jnp.sum(lanes, axis=0, keepdims=True)
        stores_done(places, stage, sems)


def store_sums(places, stage, sems, start=0):
    for slot, (source, targets) in enumerate(places, start):
        stage[slot, :, : source.shape[-1]] = source[...].astype(BF)
        for index, (at, target) in enumerate(targets):
            lanes = pl.ds(at, target.shape[-1])
            pltpu.make_async_copy(stage.at[slot, :, lanes], target, sems.at[slot, index]).start()


def stores_done(places, stage, sems):
    for slot, (_, targets) in enumerate(places):
        for index, (at, target) in enumerate(targets):
            lanes = pl.ds(at, target.shape[-1])
            pltpu.make_async_copy(stage.at[slot, :, lanes], target, sems.at[slot, index]).wait()


def unpack_kernel(core_ref, order_ref, len_ref, off_ref, mine_ref, recv_ref, out_ref, *columns):
    core = core_ref[0]
    half = order_ref.shape[0] // 2
    span, cols = out_ref.shape[1], out_ref.shape[2]
    each = cols // BLOCK

    def spread(step, carry):
        rows = pl.ds(pl.multiple_of(step * BLOCK, BLOCK), BLOCK)
        for index in range(each):
            lanes = slice(index * BLOCK, (index + 1) * BLOCK)
            columns[index][rows, :] = mine_ref[rows, lanes]
            columns[each + index][rows, :] = recv_ref[rows, lanes].astype(F32)
        return carry

    lax.fori_loop(0, recv_ref.shape[0] // BLOCK, spread, 0)
    row = lax.broadcasted_iota(jnp.int32, (span, BLOCK), 0)

    def place(slot, carry):
        for which in range(2):
            parity = core if which == 0 else 1 - core
            sentence = order_ref[2 * slot + parity]
            count = len_ref[sentence]
            start = off_ref[which, slot]
            for index in range(each):
                value = columns[which * each + index][pl.ds(start, span), :]
                out_ref[sentence, :, index * BLOCK : (index + 1) * BLOCK] = jnp.where(
                    row < count, value, 0.0
                )
        return carry

    lax.fori_loop(0, half, place, 0)


SMEM_SPEC = pl.BlockSpec(memory_space=pltpu.SMEM)
VMEM_SPEC = pl.BlockSpec(memory_space=pltpu.VMEM)
HBM_SPEC = pl.BlockSpec(memory_space=pl.ANY)


def params(limit=VMEM_LIMIT):
    return pltpu.CompilerParams(vmem_limit_bytes=limit)


def tile_spec(cols):
    return pl.BlockSpec((TILE, cols), lambda step, tiles: (jnp.minimum(step, tiles[0] - 1), 0))


def held_spec(*shape):
    return pl.BlockSpec(
        shape, lambda step, tiles: (0,) * len(shape), pipeline_mode=pl.Buffered(1)
    )


def column_spec(width, column):
    return pl.BlockSpec((width, width), lambda step, tiles: (0, column), pipeline_mode=pl.Buffered(1))


def tiled_call(kernel, out_shape, in_specs, out_specs, scratch_shapes, cost_estimate):
    def body(tiles_ref, *refs):
        @pl.when(pl.program_id(0) < tiles_ref[0])
        def _():
            kernel(pl.program_id(0) == tiles_ref[0] - 1, *refs)

    def call(tiles, most, *operands):
        return pl.pallas_call(
            body,
            grid_spec=pltpu.PrefetchScalarGridSpec(
                num_scalar_prefetch=1,
                grid=(most // TILE,),
                in_specs=in_specs,
                out_specs=out_specs,
                scratch_shapes=scratch_shapes,
            ),
            out_shape=out_shape,
            compiler_params=params(),
            cost_estimate=cost_estimate,
        )(tiles, *operands)

    return call


def shape_of(shape, dtype):
    return jax.ShapeDtypeStruct(shape, dtype)


def cost(flops, read):
    return pl.CostEstimate(flops=int(flops), bytes_accessed=int(read), transcendentals=0)


class Side:
    def __init__(self, terms, order):
        self.terms, self.order = terms, order

    def cols(self):
        _, _, lanes = self.terms[0]
        return lanes.stop - lanes.start


def slab_sums(sides, dims, joined=False, also=None, limit=SMALL_LIMIT):
    first = dims[0]
    places = jnp.stack([dp_place(dim) for dim in dims]).astype(jnp.int32)
    at_of = {dim: index for index, dim in enumerate(dims)}
    lead = 1 if joined else first[0]
    operands, in_specs, plan = [], [], []
    out_shape, out_specs, targets = [], [], []

    def index_map(term_dims, current, step, left):
        def of(grid, at):
            index = []
            for dim in term_dims:
                if dim == first and (dim in left or (dim == current and not joined)):
                    index.append(grid)
                elif dim == current:
                    index.append(lax.rem(at[at_of[dim]] + step, dim[0]))
                else:
                    index.append(0 if dim in left else at[at_of[dim]])
            return (*index, 0, 0)

        return of

    for number, side in enumerate([*sides, *([also] if also else [])]):
        main = number < len(sides)
        current = first if joined and main else side.order[0]
        rows = side.terms[0][0].shape[-2]
        left = [dim for dim in side.terms[-1][1] if dim != current]
        rest = [dim[0] for dim in left if dim != first]
        for step in range(current[0]) if joined else range(1, current[0]):
            ids = []
            shared = ids if current != first or joined or step == 1 else plan[-1][0]
            if shared is ids:
                for array, term_dims, lanes in side.terms:
                    block, pick = [], []
                    for dim in term_dims:
                        whole = dim in left and dim != first
                        block.append(dim[0] if whole else 1)
                        pick.append(slice(None) if whole else 0)
                    ids.append((len(operands), tuple(pick), lanes))
                    operands.append(array)
                    spec = (*block, rows, array.shape[-1])
                    in_specs.append(pl.BlockSpec(spec, index_map(term_dims, current, step, left)))
            plan.append((shared, number, step))
            if joined and main:
                continue
            over = main and not joined
            shape = (lead if over else 1, *rest, rows, side.cols())
            out_shape.append(shape_of(shape, F32 if step == 0 else BF))
            out_specs.append(
                pl.BlockSpec(
                    (1, *shape[1:]), lambda grid, at, n=len(shape), over=over: (grid if over else 0,) + (0,) * (n - 1)
                )
            )
            targets.append((number, step))
    if joined:
        width = sum(side.cols() for side in sides)
        rows = sides[0].terms[0][0].shape[-2]
        for step in range(first[0]):
            out_shape.append(shape_of((rows, width), BF if step else F32))
            out_specs.append(pl.BlockSpec((rows, width), lambda grid, at: (0, 0)))
            targets.append((None, step))
    starts = [sum(side.cols() for side in sides[:number]) for number in range(len(sides))]

    def kernel(places_ref, *refs):
        ins, outs = refs[: len(operands)], refs[len(operands) :]

        def total_of(ids):
            total = None
            for index, pick, lanes in ids:
                value = ins[index][(*pick, slice(None), lanes)].astype(F32)
                total = value if total is None else total + value
            return total

        def keep(out, ids):
            out[0] = total_of(ids).astype(out.dtype)

        for ids, number, step in plan:
            if number >= len(sides):
                out = outs[targets.index((number, step))]
                if also.order[0] == first:
                    here = lax.rem(places_ref[0] + step, first[0])
                else:
                    here = 0
                pl.when(pl.program_id(0) == here)(lambda out=out, ids=ids: keep(out, ids))
            elif joined:
                out = outs[targets.index((None, step))]
                out[:, starts[number] : starts[number] + sides[number].cols()] = total_of(ids).astype(out.dtype)
            else:
                keep(outs[targets.index((number, step))], ids)

    sums = pl.pallas_call(
        kernel,
        grid_spec=pltpu.PrefetchScalarGridSpec(
            num_scalar_prefetch=1, grid=(lead,), in_specs=in_specs, out_specs=out_specs
        ),
        out_shape=out_shape,
        compiler_params=params(limit),
        cost_estimate=cost(0, 8e6),
    )(places, *operands)
    more = [value[0] for value, (which, _) in zip(sums, targets) if which == len(sides)]
    if joined:
        return [value for value, (which, _) in zip(sums, targets) if which is None], more
    lists = [[value for value, (which, _) in zip(sums, targets) if which == number] for number in range(len(sides))]
    return [*lists, more] if also else lists


def adam_moments(grad_value, moment, square):
    moment_new = beta_one * moment + (1.0 - beta_one) * grad_value
    square_new = beta_two * square + (1.0 - beta_two) * grad_value * grad_value
    scaled = (
        moment_new
        / (1.0 - beta_one**STEP)
        / (jnp.sqrt(square_new / (1.0 - beta_two**STEP)) + adam_eps)
    )
    return (moment_new, square_new, scaled)


def square_sum(value):
    return jnp.sum(jnp.sum(value * value, axis=0, keepdims=True), axis=1, keepdims=True)


def note_norms(norms, matrix, weight, update):
    row = lax.broadcasted_iota(jnp.int32, norms.shape, 0)
    lane = lax.broadcasted_iota(jnp.int32, norms.shape, 1)
    here = jnp.where(row == 0, square_sum(weight), square_sum(update))
    return norms + jnp.where(jnp.logical_and(row < 2, lane == matrix), here, 0.0)


def ffn_update_kernel(count, own_ref, rest_ref, *refs):
    states, arrived, outs = refs[:9], refs[9:-13], refs[-13:]
    total, rest = own_ref[...], rest_ref[...]
    for ref in arrived[:count]:
        total = total + ref[...].astype(F32)
    for ref in arrived[count:]:
        rest = rest + ref[...].astype(F32)
    norms = jnp.zeros(outs[12].shape, F32)
    cut = states[6].shape[1] - BLOCK
    grads = (
        rest[:, 3 * BLOCK :],
        jnp.concatenate([total[:, cut:], rest[:, BLOCK : 3 * BLOCK]], axis=1),
        jnp.concatenate([total[:, :cut], rest[:, :BLOCK]], axis=1),
    )
    for index in range(3):
        weight, moment, square = states[3 * index : 3 * index + 3]
        grad = grads[index]
        moment_new, square_new, scaled = adam_moments(grad, moment[...], square[...])
        update = scaled + weight_decay * weight[...]
        for target, value in zip(outs[4 * index :], (grad, moment_new, square_new, update)):
            target[...] = value
        norms = note_norms(norms, 3 + index, weight[...], update)
    outs[12][...] = norms


def qkv_update_kernel(
    own_ref, weight_ref, moment_ref, square_ref, vec_ref, norms_ref, *refs
):
    arrived, (grad_out, moment_out, square_out, update_out, totals_ref) = refs[:-5], refs[-5:]
    cols = weight_ref.shape[2]
    total = own_ref[...]
    for ref in arrived:
        total = total + ref[...].astype(F32)
    rows = vec_ref.shape[0]
    norms = norms_ref[...]
    for index in range(3):
        grad = total[:, index * cols : (index + 1) * cols]
        moment, square, scaled = adam_moments(grad, moment_ref[index], square_ref[index])
        update = scaled + weight_decay * weight_ref[index]
        grad_out[index] = grad
        moment_out[index] = moment
        square_out[index] = square
        update_out[index] = update
        norms = note_norms(norms, index, weight_ref[index], update)
    totals_ref[:rows, :] = vec_ref[...]
    totals_ref[rows:, :] = norms


def finish_kernel(totals_ref, *refs):
    ins, outs = refs[:16], refs[16:]
    rows = totals_ref.shape[0] - 8
    weight_norm = jnp.sqrt(totals_ref[rows : rows + 1, :])
    update_norm = jnp.sqrt(totals_ref[rows + 1 : rows + 2, :])
    trust = weight_norm / update_norm
    lane = lax.broadcasted_iota(jnp.int32, trust.shape, 1)
    outs[12][0:1, :] = trust
    outs[12][1:2, :] = weight_norm
    outs[12][2:3, :] = update_norm

    def step(matrix):
        return learn_rate * jnp.sum(jnp.where(lane == matrix, trust, 0.0), axis=1, keepdims=True)

    for index in range(4):
        update, weight, average = ins[3 * index : 3 * index + 3]
        for piece in range(3 if index == 0 else 1):
            at = (piece,) if index == 0 else (Ellipsis,)
            new = weight[at] - step(piece if index == 0 else index + 2) * update[at]
            outs[2 * index][at] = new
            outs[2 * index + 1][at] = ema_keep * average[at] + (1.0 - ema_keep) * new
    vectors, moment, square, average = ins[12:16]
    grad = totals_ref[:rows, :]
    moment_new, square_new, scaled = adam_moments(grad, moment[...], square[...])
    new = vectors[...] - vector_rate * scaled
    outs[8][...] = moment_new
    outs[9][...] = square_new
    outs[10][...] = new
    outs[11][...] = ema_keep * average[...] + (1.0 - ema_keep) * new


def shards(
    tokens, lengths, send_order, pooled_grad,
    qkv_weight, out_weight, in_weight, down_weight, vectors,
    qkv_moment, out_moment, in_moment, down_moment, vec_moment,
    qkv_square, out_square, in_square, down_square, vec_square,
    qkv_average, out_average, in_average, down_average, vec_average,
):
    core = lax.axis_index("mp")
    count = lax.axis_size("dp")
    dims = dp_dims(count)
    sents, span, width = tokens.shape
    half = width // 2
    mine = sents // 2
    most = mine * span
    shard_rows = qkv_weight.shape[1]
    core_word = core.reshape(1).astype(jnp.int32)

    def flip(value):
        return jnp.where(core == 0, value, value[::-1])

    chunk = jnp.concatenate([part.astype(BF) for part in (*qkv_weight, out_weight.T)], axis=1)
    first, others = dims[0], dims[1:]
    orders = (others, others[::-1])
    sides = (0, 1)

    def gather_start(pieces):
        value = arrange(pieces, first, 0)
        cols = value.shape[-1] // 2
        return [
            (value[..., side * cols : (side + 1) * cols], [first], orders[side]) for side in sides
        ]

    def gather_out(state):
        return [gather_send(value, order[0]) if order else [value] for value, _, order in state]

    def gather_in(state, pieces):
        after = []
        for (value, done, order), come in zip(state, pieces):
            if order:
                axis = sum(1 for other in done if other[1] > order[0][1])
                value = arrange(come, order[0], axis)
                done = done + [order[0]]
            after.append((value, done, order[1:]))
        return after

    def gather_end(state):
        return [value.reshape(width, -1) for value, _, _ in state]

    share = sents // count
    if share % 2 == 0:
        own = lax.dynamic_index_in_dim(
            pooled_grad.reshape(count, share // 2, 2, width), core, 2, keepdims=False
        )
        pair_grad = lax.all_to_all(own, "dp", 0, 0, tiled=True).reshape(mine, width)
    else:
        own = lax.all_to_all(pooled_grad, "dp", 0, 0, tiled=True)
        pair_grad = lax.dynamic_index_in_dim(
            own.reshape(mine, 2, width), core, 1, keepdims=False
        )

    pieces0 = gather_send(chunk, first)
    qkvo = gather_start(pieces0)
    pieces0 = gather_out(qkvo)
    own, held = lax.optimization_barrier((in_weight, [pieces[0] for pieces in pieces0]))
    pieces1 = gather_send(own.astype(BF), first)
    pieces0, pieces1, pair_grad = lax.optimization_barrier((pieces0, pieces1, pair_grad))
    qkvo = gather_in(qkvo, pieces0)
    pieces0 = gather_out(qkvo)
    held = [pieces[0] for pieces in pieces0]
    own, held = lax.optimization_barrier((down_weight, held))
    pieces2 = gather_send(own.T.astype(BF), first)

    order_word, _ = lax.optimization_barrier((send_order, [pieces[0] for pieces in pieces0]))
    packed = pl.pallas_call(
        pack_kernel,
        out_shape=(
            shape_of((most, width), BF),
            shape_of((most, BLOCK), F32),
            shape_of((2, mine), jnp.int32),
            shape_of((1,), jnp.int32),
        ),
        in_specs=[SMEM_SPEC, SMEM_SPEC, SMEM_SPEC, VMEM_SPEC],
        out_specs=(VMEM_SPEC, VMEM_SPEC, SMEM_SPEC, SMEM_SPEC),
        scratch_shapes=[pltpu.VMEM((most, BLOCK), F32)] * (width // BLOCK),
        compiler_params=params(),
        cost_estimate=cost(0, 30e6),
    )(core_word, order_word, lengths, tokens)
    packed, pieces0, pieces2 = lax.optimization_barrier((packed, pieces0, pieces2))
    rows, seg, offsets, tiles = packed
    full = jnp.concatenate(gather_end(gather_in(qkvo, pieces0)), axis=1)
    full = (full, swap_core(full))
    weights = (full[0], full[0], full[1], full[1])
    ffn = [
        (arrange(pieces, first, 0), [first], orders[side]) for side, pieces in enumerate((pieces1, pieces2))
    ]
    ffn = gather_in(ffn, gather_out(ffn))
    ffn_pieces = gather_out(ffn)

    own_order = lax.dynamic_index_in_dim(send_order.reshape(mine, 2), core, 1, keepdims=False)
    own_count = lengths[own_order].astype(F32)[:, None]
    back = jnp.pad(pair_grad / own_count, ((0, BLOCK - mine), (0, 0)))
    back_high = back.astype(BF)
    back_rest = (back - back_high.astype(F32)).astype(BF)
    weight_specs = [column_spec(width, 0), column_spec(width, 1)] * 2
    long_spec = held_spec(width, 2 * width)
    vec_spec = held_spec(1, vectors.shape[0])
    vec_row = vectors.reshape(1, -1)
    row_total = most * 0.6
    mids = [pieces[0] for pieces in ffn_pieces]
    tiles, mids, _, _ = lax.optimization_barrier((tiles, mids, back_high, back_rest))
    qkv, att, normed, inverse = tiled_call(
        attn_forward_kernel,
        out_shape=(
            shape_of((most, 3 * width), BF),
            shape_of((most, width), BF),
            shape_of((most, width), F32),
            shape_of((most, BLOCK), F32),
        ),
        in_specs=[SMEM_SPEC, tile_spec(width), tile_spec(BLOCK), vec_spec] + weight_specs,
        out_specs=(tile_spec(3 * width), tile_spec(width), tile_spec(width), tile_spec(BLOCK)),
        scratch_shapes=[],
        cost_estimate=cost(2 * row_total * 4 * width * width * 2, 30e6),
    )(tiles, most, core_word, rows, seg, vec_row, *weights)
    normed, ffn_pieces = lax.optimization_barrier((normed, ffn_pieces))

    w1, w2 = [(value, swap_core(value)) for value in gather_end(gather_in(ffn, ffn_pieces))]
    down_shape = shape_of((width, 2 * width - BLOCK), BF)
    in_shape = shape_of((width, 2 * width - 2 * BLOCK), BF)
    rest_shape = shape_of((width, half + 3 * BLOCK), BF)
    (
        grad_one, emb, vec_ffn, down_own, down_other, in_own, in_other, rest_own, rest_other,
    ) = tiled_call(
        ffn_kernel,
        out_shape=(
            shape_of((most, width), F32),
            shape_of((mine, width), F32),
            shape_of((8, vectors.shape[0]), F32),
            down_shape,
            down_shape,
            in_shape,
            in_shape,
            rest_shape,
            rest_shape,
        ),
        in_specs=[
            SMEM_SPEC, tile_spec(width), tile_spec(BLOCK), tile_spec(BLOCK), tile_spec(width), vec_spec,
        ]
        + [held_spec(BLOCK, width)] * 2
        + [long_spec] * 4,
        out_specs=(tile_spec(width), held_spec(mine, width), held_spec(8, vectors.shape[0])) + (HBM_SPEC,) * 6,
        scratch_shapes=[
            pltpu.VMEM((4, width, width), F32),
            pltpu.VMEM((4, width, width), F32),
            pltpu.VMEM((2, width, half), F32),
            pltpu.VMEM((4, TILE, width), BF),
            pltpu.VMEM((4, TILE, width), F32),
            pltpu.VMEM((BLOCK, width), F32),
            pltpu.VMEM((BLOCK, BLOCK), F32),
            pltpu.VMEM((10, width, width), BF),
            pltpu.SemaphoreType.DMA((10, 2)),
        ],
        cost_estimate=cost(2 * row_total * 24 * width * width, 30e6),
    )(
        tiles, most, core_word, normed, inverse, seg, att, vec_row, back_high, back_rest, *w1, *w2
    )

    def scatter_start(parts):
        sides = []
        for side, (lanes, *arrays) in enumerate(parts):
            terms = [
                (array.reshape(*[size for size, _ in dims], shard_rows, -1), list(dims), lanes)
                for array in arrays
            ]
            sides.append(Side(terms, orders[side][::-1]))
        return sides

    def scatter_out(sides, limit=SMALL_LIMIT, also=None):
        if len({side.order[0][0] for side in sides}) == 1:
            return slab_sums(sides, dims, also=also, limit=limit)
        heads = [slab_sums([side], dims, limit=limit)[0] for side in sides[:-1]]
        return heads + slab_sums(sides[-1:], dims, also=also, limit=limit)

    def scatter_go(sides, slabs):
        return [scatter_send(sent, side.order[0]) for side, sent in zip(sides, slabs)]

    def scatter_in(sides, arrived):
        after = []
        for side, come in zip(sides, arrived):
            left = [dim for dim in side.terms[-1][1] if dim != side.order[0]]
            new = [(array, left, slice(0, side.cols())) for array in come]
            after.append(Side(side.terms + new, side.order[1:]))
        return after

    def go_pooled(value):
        return lax.all_to_all(value, "dp", 0, 0, tiled=True)

    come = [swap_core(down_other), swap_core(in_other), swap_core(rest_other)]
    grad_send = scatter_start(
        ((slice(0, down_shape.shape[1]), down_own, come[0]), (slice(0, in_shape.shape[1]), in_own, come[1]))
    )
    (rest_send,) = scatter_start(((slice(0, rest_shape.shape[1]), rest_own, come[2]),))
    rest_send.order = dims[:1] + others[::-1]
    *slabs, rest_slabs = scatter_out(grad_send, VMEM_LIMIT, rest_send)
    pooled = go_pooled(emb.reshape(count, share // 2, width)) if share % 2 == 0 else emb
    tiles, slabs, rest_slabs, pooled = lax.optimization_barrier((tiles, slabs, rest_slabs, pooled))
    qkv_shape = shape_of((width, 3 * half), BF)
    dx_mine, dx_other, vec_local, own, other = tiled_call(
        attn_backward_kernel,
        out_shape=(
            shape_of((most, half), F32),
            shape_of((most, half), BF),
            shape_of((vectors.shape[0] // BLOCK, BLOCK), F32),
            qkv_shape,
            qkv_shape,
        ),
        in_specs=[
            SMEM_SPEC, tile_spec(width), tile_spec(width), tile_spec(3 * width), tile_spec(BLOCK),
            held_spec(8, vectors.shape[0]),
        ]
        + weight_specs,
        out_specs=(tile_spec(half), tile_spec(half), held_spec(vectors.shape[0] // BLOCK, BLOCK))
        + (HBM_SPEC,) * 2,
        scratch_shapes=[
            pltpu.VMEM((TILE, 3 * width), BF),
            pltpu.VMEM((TILE, width), F32),
            pltpu.VMEM((8, vectors.shape[0]), F32),
            pltpu.VMEM((2, width, 3 * half), F32),
            pltpu.VMEM((2, width, 3 * half), BF),
            pltpu.SemaphoreType.DMA((2, 1)),
        ],
        cost_estimate=cost(2 * row_total * 18 * width * width, 30e6),
    )(tiles, most, core_word, grad_one, rows, qkv, seg, vec_ffn, *weights)
    arrived, rest_arrived, own, other, dx_other = lax.optimization_barrier(
        (scatter_go(grad_send, slabs), scatter_go([rest_send], [rest_slabs]), own, other, dx_other)
    )
    grad_send = scatter_in(grad_send, arrived)
    (rest_send,) = scatter_in([rest_send], rest_arrived)
    *slabs, rest_slabs = scatter_out(grad_send, VMEM_LIMIT, rest_send)
    come = swap_core(other)
    own, come, slabs, rest_slabs = lax.optimization_barrier((own, come, slabs, rest_slabs))
    cut = 3 * half // (2 * BLOCK) * BLOCK
    qkv_send = scatter_start(((slice(0, cut), own, come), (slice(cut, 3 * half), own, come)))
    qkv_slabs = scatter_out(qkv_send)
    order_word, slabs = lax.optimization_barrier((send_order, slabs))

    tokens_grad = pl.pallas_call(
        unpack_kernel,
        out_shape=shape_of((sents, span, half), F32),
        in_specs=[SMEM_SPEC] * 4 + [VMEM_SPEC] * 2,
        out_specs=VMEM_SPEC,
        scratch_shapes=[pltpu.VMEM((most, BLOCK), F32)] * (2 * half // BLOCK),
        compiler_params=params(),
        cost_estimate=cost(0, 20e6),
    )(core_word, order_word, lengths, offsets, dx_mine, swap_core(dx_other))
    arrived, rest_arrived, tokens_grad, qkv_slabs = lax.optimization_barrier(
        (scatter_go(grad_send, slabs), scatter_go([rest_send], [rest_slabs]), tokens_grad, qkv_slabs)
    )
    grad_send = scatter_in(grad_send, arrived)
    (rest_send,) = scatter_in([rest_send], rest_arrived)
    (ffn_grad, *slabs), (rest_grad, *rest_slabs) = slab_sums(
        grad_send, dims, joined=True, also=rest_send, limit=VMEM_LIMIT
    )
    qkv_slabs, slabs = lax.optimization_barrier((qkv_slabs, slabs))
    last_go = scatter_send(slabs, first)
    go = scatter_go(qkv_send, qkv_slabs)
    qkv_send = scatter_in(qkv_send, go)
    while qkv_send[0].order:
        go = scatter_go(qkv_send, scatter_out(qkv_send))
        go, last_go, pooled, rest_slabs = lax.optimization_barrier((go, last_go, pooled, rest_slabs))
        qkv_send = scatter_in(qkv_send, go)
    rest_go = scatter_send(rest_slabs, rest_send.order[0])
    (qkv_grad, *slabs), _ = slab_sums(qkv_send, dims, joined=True)
    go = scatter_send(slabs, first)

    both = [pooled, swap_core(pooled)]
    go, both = lax.optimization_barrier((go, both))
    ffn_states = [
        (out_weight.T, out_moment.T, out_square.T),
        (in_weight, in_moment, in_square),
        (down_weight.T, down_moment.T, down_square.T),
    ]
    shapes = [shape_of(state[0].shape, F32) for state in ffn_states for _ in range(4)]
    *ffn_new, norms = pl.pallas_call(
        functools.partial(ffn_update_kernel, len(last_go)),
        out_shape=shapes + [shape_of((8, BLOCK), F32)],
        in_specs=[VMEM_SPEC] * (11 + len(last_go) + len(rest_go)),
        out_specs=[VMEM_SPEC] * 13,
        compiler_params=params(SMALL_LIMIT),
        cost_estimate=cost(0, 4e6),
    )(ffn_grad, rest_grad, *[value for state in ffn_states for value in state], *last_go, *rest_go)
    out_grad, out_m, out_s, out_u, in_grad, in_m, in_s, in_u, down_grad, down_m, down_s, down_u = ffn_new
    lines = vectors.shape[0] // BLOCK
    like = [shape_of(qkv_weight.shape, F32)]
    qkv_grad, qkv_m, qkv_s, qkv_u, totals = pl.pallas_call(
        qkv_update_kernel,
        out_shape=like * 4 + [shape_of((lines + 8, BLOCK), F32)],
        in_specs=[VMEM_SPEC] * (6 + len(go)),
        out_specs=[VMEM_SPEC] * 5,
        compiler_params=params(SMALL_LIMIT),
        cost_estimate=cost(0, 4e6),
    )(qkv_grad, qkv_weight, qkv_moment, qkv_square, vec_local, norms, *go)
    totals, both = lax.optimization_barrier((totals, both))
    both = flip(jnp.stack(both))
    if share % 2 == 0:
        pooled = jnp.moveaxis(both, 0, 2).reshape(sents, width)
    else:
        both = jnp.moveaxis(both, 0, 1).reshape(sents, width)
        pooled = go_pooled(both)

    totals = sum_all(totals, dims)
    states = [
        (qkv_u, qkv_weight, qkv_average),
        (out_u, out_weight.T, out_average.T),
        (in_u, in_weight, in_average),
        (down_u, down_weight.T, down_average.T),
    ]
    pieces = [value.reshape(lines, BLOCK) for value in (vectors, vec_moment, vec_square, vec_average)]
    shapes = [shape_of(update.shape, F32) for update, _, _ in states for _ in range(2)]
    shapes += [shape_of((lines, BLOCK), F32)] * 4 + [shape_of((8, BLOCK), F32)]
    (
        new_qkv, qkv_a, new_out, out_a, new_in, in_a, new_down, down_a, vec_m, vec_s, new_vec, vec_a, ratios,
    ) = pl.pallas_call(
        finish_kernel,
        out_shape=shapes,
        in_specs=[VMEM_SPEC] * 17,
        out_specs=[VMEM_SPEC] * len(shapes),
        compiler_params=params(SMALL_LIMIT),
        cost_estimate=cost(0, 4e6),
    )(totals, *[value for state in states for value in state], *pieces)
    vec_grad, vec_m, vec_s, new_vec, vec_a = [
        value.reshape(-1) for value in (totals[:lines], vec_m, vec_s, new_vec, vec_a)
    ]
    trust_ratio, weight_norm, update_norm = [ratios[index, :6] for index in range(3)]
    out_grad, out_m, out_s, new_out, out_a = [value.T for value in (out_grad, out_m, out_s, new_out, out_a)]
    down_grad, down_m, down_s, new_down, down_a = [
        value.T for value in (down_grad, down_m, down_s, new_down, down_a)
    ]
    return (
        pooled, tokens_grad, qkv_grad, out_grad, in_grad, down_grad, vec_grad,
        trust_ratio, weight_norm, update_norm,
        qkv_m, out_m, in_m, down_m, vec_m,
        qkv_s, out_s, in_s, down_s, vec_s,
        new_qkv, new_out, new_in, new_down, new_vec,
        qkv_a, out_a, in_a, down_a, vec_a,
    )


def solution(mesh):
    matrices = (P(None, "dp", "mp"), P("mp", "dp"), P("dp", "mp"), P("mp", "dp"), P())
    return jax.shard_map(
        shards,
        mesh=mesh,
        in_specs=(P("dp", None, None), P("dp"), P("dp"), P("dp", None)) + matrices * 4,
        out_specs=(P("dp", None), P("dp", None, "mp")) + matrices + (P(), P(), P()) + matrices * 4,
        check_vma=False,
    )
```
